128 devices in a mesh: dp: 8 (over z, x_lo), ctx: 16 (over x_hi, y, core).
Axes of the slice: x: 4 (x_hi: 2, x_lo: 2; x = x_hi * 2 + x_lo), y: 4, z: 4, core: 2. Of those that a mesh axis runs over, the one named last changes fastest.
Arguments:
- tokens: bfloat16 [16384, 1024], P(('dp', 'ctx')), may hold values from -6 to 6
- lengths: int32 [8, 8], P('dp'), may hold values from 1 to 1943, as said below
- attn_gain: bfloat16 [1024], P(('dp', 'ctx')), may hold values from 0.099609375 to 1.8984375
- q_gain: bfloat16 [128], P(('dp', 'ctx')), may hold values from 0.099609375 to 1.8984375
- k_gain: bfloat16 [128], P(('dp', 'ctx')), may hold values from 0.099609375 to 1.8984375
- query_key_value_weight: bfloat16 [1024, 4096], P(('dp', 'ctx')), may hold values from -0.1875 to 0.1875
- w_out: bfloat16 [2048, 1024], P(('dp', 'ctx')), may hold values from -0.75 to 0.75
- mlp_gain: bfloat16 [1024], P(('dp', 'ctx')), may hold values from 0.099609375 to 1.8984375
- w_gate_up: bfloat16 [1024, 6144], P(('dp', 'ctx')), may hold values from -0.1875 to 0.1875
- w_down: bfloat16 [3072, 1024], P(('dp', 'ctx')), may hold values from -0.109375 to 0.109375
- cotangent: bfloat16 [16384, 1024], P(('dp', 'ctx')), may hold values from -6 to 6
Outputs:
- output: float32 [16384, 1024], P(('dp', 'ctx'))
- input_grad: float32 [16384, 1024], P(('dp', 'ctx'))
- grad_attn_gain: float32 [1024], P(('dp', 'ctx'))
- grad_q_gain: float32 [128], P(('dp', 'ctx'))
- grad_k_gain: float32 [128], P(('dp', 'ctx'))
- grad_w_qkv: float32 [1024, 4096], P(('dp', 'ctx'))
- grad_w_out: float32 [2048, 1024], P(('dp', 'ctx'))
- grad_mlp_gain: float32 [1024], P(('dp', 'ctx'))
- grad_gate_up: float32 [1024, 6144], P(('dp', 'ctx'))
- grad_down: float32 [3072, 1024], P(('dp', 'ctx'))
The draws below stay inside these ranges and needn't reach their ends.
Inputs may be any that keep to these rules, and one draw needn't show every extreme that they name: Row p holds the lengths of the 8 documents of pack p in order; they sum to 2048. The second document of every pack has the largest length.
All inputs are finite; a program needn't handle non-finite values.
Results may differ from the reference program's by a relative error of at most 0.024.
Values may be sent and summed in bfloat16 or wider, within the bound.
A program may use at most 320 MiB of HBM per device.

```python
import math
import jax
import jax.numpy as jnp
from jax import lax

MODEL_WIDTH = 1024
QUERY_HEADS = 16
KEY_VALUE_HEADS = 8
HEAD_SIZE = 128
FF = 3072
TOK_DEV = 128
NDOC = 8
NPACK = 8
GROUP = 2048
TOKENS = 16384


def draw_lengths(key, part):
    key = jax.random.fold_in(key, 11)
    first_key, short_key = jax.random.split(key)
    others_total = TOK_DEV // 2 + (NDOC - 3) * (TOK_DEV // 16) + 1
    leading = jax.random.randint(first_key, (NPACK, 1), 1, TOK_DEV // 2 + 1, dtype=jnp.int32)
    middle = jax.random.randint(short_key, (NPACK, NDOC - 3), 1, TOK_DEV // 16 + 1, dtype=jnp.int32)
    closing = others_total - leading - jnp.sum(middle, 1, keepdims=True)
    longest = jnp.zeros((NPACK, 1), jnp.int32) + (GROUP - others_total)
    return jnp.concatenate([leading, longest, middle, closing], 1).astype(jnp.int32)


def block_levels(stream_key, extent, shards, least, high):
    level = 1.0
    for axis_at, parts in shards:
        steps = jax.random.uniform(jax.random.fold_in(jax.random.fold_in(stream_key, 6), axis_at), (parts,), jnp.float32, least / len(shards), high / len(shards))
        level = level * jnp.repeat(jnp.exp(steps), extent[axis_at] // parts).reshape((-1,) + (1,) * (len(extent) - 1 - axis_at))
    return level


def normal_values(key, extent, deviation, limit, cuts=(), kind=jnp.bfloat16):
    entries = deviation * jax.random.normal(key, extent, jnp.float32)
    if cuts:
        entries = entries * block_levels(key, extent, cuts, -0.22, 0.18)
    return jnp.clip(entries, -limit, limit).astype(kind)


def setup_inputs(seed: int = 0) -> dict:
    keys = jax.random.split(jax.random.key(seed), 12)
    tokens = normal_values(keys[0], (TOKENS, MODEL_WIDTH), 1.0, 6.0, ((0, 128),))
    lengths = draw_lengths(jax.random.fold_in(keys[11], 71), 0)
    attn_gain = jnp.clip(1.0 + 0.18 * jax.random.normal(keys[2], (MODEL_WIDTH,), jnp.float32), 0.099609375, 1.8984375).astype(jnp.bfloat16)
    q_gain = jnp.clip(1.0 + 0.18 * jax.random.normal(keys[3], (HEAD_SIZE,), jnp.float32), 0.099609375, 1.8984375).astype(jnp.bfloat16)
    k_gain = jnp.clip(1.0 + 0.18 * jax.random.normal(keys[4], (HEAD_SIZE,), jnp.float32), 0.099609375, 1.8984375).astype(jnp.bfloat16)
    query_key_value_weight = normal_values(keys[5], (MODEL_WIDTH, (QUERY_HEADS + 2 * KEY_VALUE_HEADS) * HEAD_SIZE), MODEL_WIDTH ** -0.5, 0.1875, ((0, 128),))
    w_out = normal_values(keys[6], (QUERY_HEADS * HEAD_SIZE, MODEL_WIDTH), 64 ** -0.5, 0.75, ((0, 128),))
    mlp_gain = jnp.clip(1.0 + 0.18 * jax.random.normal(keys[7], (MODEL_WIDTH,), jnp.float32), 0.099609375, 1.8984375).astype(jnp.bfloat16)
    w_gate_up = normal_values(keys[8], (MODEL_WIDTH, 2 * FF), MODEL_WIDTH ** -0.5, 0.1875, ((0, 128),))
    w_down = normal_values(keys[9], (FF, MODEL_WIDTH), FF ** -0.5, 0.109375, ((0, 128),))
    cotangent = normal_values(keys[10], (TOKENS, MODEL_WIDTH), 1.0, 6.0, ((0, 128),))
    return {"tokens": tokens, "lengths": lengths, "attn_gain": attn_gain, "q_gain": q_gain, "k_gain": k_gain, "query_key_value_weight": query_key_value_weight, "w_out": w_out, "mlp_gain": mlp_gain, "w_gate_up": w_gate_up, "w_down": w_down, "cotangent": cotangent}


@jax.custom_vjp
def reduced_precision(v):
    return lax.optimization_barrier(v.astype(jnp.bfloat16)).astype(jnp.float32)

@jax.custom_vjp
def low_back(v):
    return v

def low_keep(v):
    return (reduced_precision(v), None)

def low_pass(kept, grad):
    return (grad,)

def back_keep(v):
    return (v, None)

def back_low(kept, grad):
    return (reduced_precision(grad),)
reduced_precision.defvjp(low_keep, low_pass)
low_back.defvjp(back_keep, back_low)
EPS = 1e-06
NEG = -1e+30
THETA = 1000000.0
HIGH = lax.Precision.HIGHEST

def matmul(left_side, right_side):
    return jnp.dot(left_side, right_side, precision=HIGH, preferred_element_type=jnp.float32)

def layout(doc_lengths, group):
    ends = jnp.cumsum(doc_lengths).astype(jnp.int32)
    place = jnp.arange(group, dtype=jnp.int32)
    segment = lax.optimization_barrier(jnp.sum((place[:, None] >= ends[None, :]).astype(jnp.int32), 1))
    starts = ends - doc_lengths
    picked = segment[:, None] == jnp.arange(doc_lengths.shape[0], dtype=jnp.int32)[None, :]
    begin = lax.optimization_barrier(jnp.sum(jnp.where(picked, starts[None, :], 0), 1)).astype(jnp.int32)
    return (segment, place - begin)

def angles(position):
    half_dim = HEAD_SIZE // 2
    freq = THETA ** (-(jnp.arange(half_dim, dtype=jnp.float32) * 2.0 / HEAD_SIZE))
    phase = position.astype(jnp.float32)[:, None] * freq[None, :]
    phase = jnp.concatenate([phase, phase], 1)
    return (jnp.cos(phase), jnp.sin(phase))

def rotate(values_in, cosine, sine):
    half_dim = values_in.shape[-1] // 2
    turned = jnp.concatenate([-values_in[..., half_dim:], values_in[..., :half_dim]], -1)
    return values_in * cosine + turned * sine

def head_norm(values_in, gain_in):
    return values_in * lax.rsqrt(lax.optimization_barrier(jnp.mean(values_in * values_in, -1, keepdims=True)) + EPS) * gain_in

def layer(inputs, segment, position, weights):
    attn_gain, q_gain, k_gain, query_key_value_weight, w_out, mlp_gain, w_gate_up, w_down = weights
    every_row_total = inputs.shape[0]
    head_groups = QUERY_HEADS // KEY_VALUE_HEADS
    inverse_one = lax.rsqrt(lax.optimization_barrier(jnp.mean(inputs * inputs, -1, keepdims=True)) + EPS)
    first_in = reduced_precision(inputs * inverse_one * attn_gain)
    projected_rows = low_back(matmul(first_in, query_key_value_weight))
    query_unnormed = projected_rows[:, :QUERY_HEADS * HEAD_SIZE].reshape(every_row_total, KEY_VALUE_HEADS, head_groups, HEAD_SIZE)
    key_unnormed = projected_rows[:, QUERY_HEADS * HEAD_SIZE:(QUERY_HEADS + KEY_VALUE_HEADS) * HEAD_SIZE].reshape(every_row_total, KEY_VALUE_HEADS, HEAD_SIZE)
    value_reduced = reduced_precision(projected_rows[:, (QUERY_HEADS + KEY_VALUE_HEADS) * HEAD_SIZE:].reshape(every_row_total, KEY_VALUE_HEADS, HEAD_SIZE))
    cosine, sine = angles(position)
    query_low = reduced_precision(rotate(head_norm(query_unnormed, q_gain), cosine[:, None, None, :], sine[:, None, None, :]))
    key_low = reduced_precision(rotate(head_norm(key_unnormed, k_gain), cosine[:, None, :], sine[:, None, :]))
    scale_factor = 1.0 / math.sqrt(HEAD_SIZE)
    raw_scores = jnp.einsum('tkgd,nkd->kgtn', query_low, key_low, precision=HIGH) * scale_factor
    scores = low_back(raw_scores)
    place = jnp.arange(every_row_total, dtype=jnp.int32)
    visible = (segment[:, None] == segment[None, :]) & (place[:, None] >= place[None, :])
    scores = jnp.where(visible, scores, NEG)
    probs = jax.nn.softmax(scores, -1)
    attended = jnp.einsum('kgtn,nkd->tkgd', reduced_precision(probs), value_reduced, precision=HIGH).reshape(every_row_total, QUERY_HEADS * HEAD_SIZE)
    attended_low = low_back(reduced_precision(attended))
    residual = inputs + low_back(matmul(attended_low, w_out))
    inverse_two = lax.rsqrt(lax.optimization_barrier(jnp.mean(residual * residual, -1, keepdims=True)) + EPS)
    second_in = reduced_precision(residual * inverse_two * mlp_gain)
    gate_up = low_back(matmul(second_in, w_gate_up))
    hidden_low = reduced_precision(jax.nn.silu(gate_up[:, :FF]) * gate_up[:, FF:])
    return residual + matmul(hidden_low, w_down)

def reference(tokens, lengths, attn_gain, q_gain, k_gain, query_key_value_weight, w_out, mlp_gain, w_gate_up, w_down, cotangent):
    weights = tuple((weight_item.astype(jnp.float32) for weight_item in (attn_gain, q_gain, k_gain, query_key_value_weight, w_out, mlp_gain, w_gate_up, w_down)))
    inputs = tokens.astype(jnp.float32)

    def forward(inputs_all, weights_all):
        packs = inputs_all.reshape(NPACK, GROUP, MODEL_WIDTH)

        def one_pack(bundle):
            pack_rows, doc_lengths = bundle
            segment, position = layout(doc_lengths, GROUP)
            return layer(pack_rows, segment, position, weights_all)
        results = lax.map(jax.checkpoint(one_pack), (packs, lengths))
        return results.reshape(TOKENS, MODEL_WIDTH)
    output, pull = jax.vjp(forward, inputs, weights)
    grad_input, grads = pull(cotangent.astype(jnp.float32))
    return (output, grad_input, grads[0], grads[1], grads[2], grads[3], grads[4], grads[5], grads[6], grads[7])
```

```python
import functools
import math

import jax
import jax.numpy as jnp
from jax import lax
from jax.experimental import pallas as pl
from jax.experimental.pallas import tpu as pltpu
from jax.sharding import Mesh
from jax.sharding import PartitionSpec as P

QUERY_HEADS = 16
KEY_VALUE_HEADS = 8
HEAD_SIZE = 128
WIDTH = 1024
FF = 3072
TOK = 128
GROUP = 2048
BLOCK = 256
SLICE = FF // 8
EPS = 1e-06
THETA = 1000000.0
SCALE = 1.0 / math.sqrt(HEAD_SIZE)
SCALE2 = SCALE / math.log(2.0)

AXES = ("z", "xl", "xh", "y", "c")
SIZES = (4, 2, 2, 4, 2)
CTX = ("xh", "y", "c")
DP = ("z", "xl")
BF = jnp.bfloat16
F32 = jnp.float32
BY_MESH = pl.DeviceIdType.MESH
ANY = pl.BlockSpec(memory_space=pl.ANY)
VMEM = pl.BlockSpec(memory_space=pltpu.VMEM)
MIB = 2**20


def offsets(*axes):
    out = [()]
    for size, name in zip(SIZES, AXES):
        out = [o + (k,) for o in out for k in (range(size) if name in axes else (0,))]
    return out[1:]


SIBLING = (0, 0, 0, 0, 1)
CTX_ALL = offsets("xh", "y", "c")
CTX_SAME = offsets("xh", "y")
DP_ALL = offsets("z", "xl")
PLANE = offsets("xl", "xh", "y")
RING = offsets("z")
RING_ALL = offsets("z", "c")


def place():
    return tuple(lax.axis_index(a) for a in AXES)


def moved(me, offset):
    return tuple(lax.rem(m + o, s) if o else m for m, o, s in zip(me, offset, SIZES))


def before(me, offset):
    return tuple(lax.rem(m + s - o, s) if o else m for m, o, s in zip(me, offset, SIZES))


def ctx_of(at):
    return at[2] * 8 + at[3] * 2 + at[4]


def dp_of(at):
    return at[0] * 2 + at[1]


def ring_of(at):
    return at[0] * 2 + at[4]


def plane_of(at):
    return at[1] * 8 + at[2] * 4 + at[3]


def greet(me, peers):
    barrier = pltpu.get_barrier_semaphore()
    for o in peers:
        pl.semaphore_signal(barrier, inc=1, device_id=moved(me, o), device_id_type=BY_MESH)
    pl.semaphore_wait(barrier, len(peers))


class Net:
    def __init__(self, send, recv):
        self.send, self.recv, self.count, self.sent = send, recv, 0, []

    def put(self, src, dst, device):
        k = self.count
        self.count += 1
        copy = pltpu.make_async_remote_copy(
            src_ref=src,
            dst_ref=dst,
            send_sem=self.send.at[k],
            recv_sem=self.recv.at[k],
            device_id=device,
            device_id_type=BY_MESH,
        )
        copy.start()
        self.sent.append(copy)
        return copy

    def local(self, src, dst):
        k = self.count
        self.count += 1
        copy = pltpu.make_async_copy(src, dst, self.send.at[k])
        copy.start()
        return copy

    def finish(self):
        for copy in self.sent:
            copy.wait_send()


def sems(count):
    return [pltpu.SemaphoreType.DMA((count,)), pltpu.SemaphoreType.DMA((count,))]


def remote(body, name, identity, outs, ins, out_specs, scratch, *operands):
    return pl.pallas_call(
        body,
        name=name,
        out_shape=outs,
        in_specs=ins,
        out_specs=out_specs,
        scratch_shapes=scratch,
        compiler_params=pltpu.CompilerParams(
            collective_id=identity, has_side_effects=True, vmem_limit_bytes=50 * MIB
        ),
    )(*operands)


def shape(dims, kind):
    return jax.ShapeDtypeStruct(dims, kind)


def first_gather_body(tok, wq, gains, x_out, w_out, g_out, w_tmp, w_low, g_tmp, g_row, send, recv):
    me = place()
    net = Net(send, recv)
    greet(me, CTX_ALL + DP_ALL)
    mine = ctx_of(me)
    small, rows = [], []
    for o in CTX_ALL:
        to = moved(me, o)
        small.append(net.put(wq.at[ctx_of(to)], w_tmp.at[mine], to))
        small.append(net.put(gains, g_tmp.at[mine], to))
    for o in CTX_SAME:
        rows.append(net.put(tok, x_out.at[mine], moved(me, o)))
    over = moved(me, SIBLING)
    passed = [net.put(tok, x_out.at[mine], over)]
    locals_ = [
        net.local(wq.at[mine], w_tmp.at[mine]),
        net.local(gains, g_tmp.at[mine]),
        net.local(tok, x_out.at[mine]),
    ]
    for copy in locals_[:2]:
        copy.wait()
    for copy in small:
        copy.wait_recv()
    w_low[...] = w_tmp[...].reshape(TOK, 3 * HEAD_SIZE).astype(BF)
    g_row[...] = g_tmp[:, 0, :]
    here = dp_of(me)
    wide = []
    for o in DP_ALL:
        to = moved(me, o)
        wide.append(net.put(w_low, w_out.at[here], to))
        wide.append(net.put(g_row, g_out.at[here], to))
    more = [net.local(w_low, w_out.at[here]), net.local(g_row, g_out.at[here])]
    for o, copy in zip(CTX_SAME, rows):
        copy.wait_recv()
        source = ctx_of(before(me, o))
        passed.append(net.put(x_out.at[source], x_out.at[source], over))
    for copy in wide + passed:
        copy.wait_recv()
    locals_[2].wait()
    for copy in more:
        copy.wait()
    net.finish()


def first_gather(tokens, wq, gains):
    return remote(
        first_gather_body,
        "first_gather",
        1,
        (shape((16, TOK, WIDTH), BF), shape((8, TOK, 3 * HEAD_SIZE), BF), shape((8, 16, 128), F32)),
        [ANY, ANY, ANY],
        (ANY, ANY, ANY),
        [
            pltpu.VMEM((16, 8, 3 * HEAD_SIZE), F32),
            pltpu.VMEM((TOK, 3 * HEAD_SIZE), BF),
            pltpu.VMEM((16, 8, 128), F32),
            pltpu.VMEM((16, 128), F32),
        ]
        + sems(72),
        tokens,
        wq,
        gains,
    )


def swapped(me, offset):
    at = moved(me, offset)
    return (at[0], at[4], at[2], at[3], at[1])


def weight_gather_body(
    wo, wgu, wd, cot, wo_out, gu_out, wd_out, cot_out, gu_tmp, gu_low, wd_tmp, wd_low, send, recv, gate
):
    me = place()
    z, xl, xh, y, c = me
    net = Net(send, recv)
    barrier = pltpu.get_barrier_semaphore()
    peers = PLANE + RING_ALL
    for o in peers:
        pl.semaphore_signal(barrier, inc=1, device_id=moved(me, o), device_id_type=BY_MESH)
    for o in CTX_SAME:
        pl.semaphore_signal(barrier, inc=1, device_id=swapped(me, o), device_id_type=BY_MESH)

    @pl.when(xl != c)
    def _():
        pl.semaphore_signal(barrier, inc=1, device_id=(z, c, xh, y, xl), device_id_type=BY_MESH)

    pl.semaphore_wait(barrier, len(peers) + len(CTX_SAME) + (xl + c - 2 * xl * c))
    over = moved(me, SIBLING)
    down = net.put(wd, wd_tmp.at[c], over)
    slices = []
    for o in RING_ALL:
        to = moved(me, o)
        slices.append(net.put(wgu.at[ring_of(to)], gu_tmp.at[ring_of(me)], to))
    own = [
        net.local(wd, wd_tmp.at[c]),
        net.local(wgu.at[ring_of(me)], gu_tmp.at[ring_of(me)]),
        net.local(wo, wo_out.at[z, xl, xh, y, c]),
        net.local(cot, cot_out.at[z, c]),
    ]
    outs = [net.put(wo, wo_out.at[z, xl, xh, y, c], moved(me, o)) for o in PLANE]
    cots = [net.put(cot, cot_out.at[z, c], moved(me, o)) for o in RING]
    passed = [net.put(cot, cot_out.at[z, c], over)]
    own[0].wait()
    down.wait_recv()
    wd_low[...] = wd_tmp[...].reshape(48, WIDTH).astype(BF)
    downs = [net.put(wd_low, wd_out.at[xh, y], swapped(me, o)) for o in CTX_SAME]

    @pl.when(xl != c)
    def _():
        copy = pltpu.make_async_remote_copy(
            src_ref=wd_low,
            dst_ref=wd_out.at[xh, y],
            send_sem=gate.at[0],
            recv_sem=gate.at[1],
            device_id=(z, c, xh, y, xl),
            device_id_type=BY_MESH,
        )
        copy.start()
        copy.wait()

    @pl.when(xl == c)
    def _():
        copy = pltpu.make_async_copy(wd_low, wd_out.at[xh, y], gate.at[0])
        copy.start()
        copy.wait()

    own[1].wait()
    for copy in slices:
        copy.wait_recv()
    gu_low[...] = gu_tmp[...].reshape(4, 16, 2 * SLICE).astype(BF)
    ups = [net.put(gu_low, gu_out.at[:, xl, xh, y], moved(me, o)) for o in PLANE]
    own.append(net.local(gu_low, gu_out.at[:, xl, xh, y]))
    own[2].wait()
    for copy in outs:
        copy.wait_recv()
    wide = [net.put(wo_out.at[z, :, :, :, c], wo_out.at[z, :, :, :, c], moved(me, o)) for o in RING]
    passed.append(net.put(wo_out.at[z, :, :, :, c], wo_out.at[z, :, :, :, c], over))
    for o, copy in zip(RING, cots):
        copy.wait_recv()
        s = before(me, o)[0]
        passed.append(net.put(cot_out.at[s, c], cot_out.at[s, c], over))
    for o, copy in zip(RING, wide):
        copy.wait_recv()
        s = before(me, o)[0]
        passed.append(net.put(wo_out.at[s, :, :, :, c], wo_out.at[s, :, :, :, c], over))
    for copy in downs + ups + passed:
        copy.wait_recv()
    for copy in own[3:]:
        copy.wait()
    net.finish()


def weight_gather(wo, wgu, wd, cot):
    return remote(
        weight_gather_body,
        "weight_gather",
        2,
        (
            shape((4, 2, 2, 4, 2, 16, WIDTH), BF),
            shape((4, 2, 2, 4, 16, 2 * SLICE), BF),
            shape((2, 4, 48, WIDTH), BF),
            shape((4, 2, TOK, WIDTH), BF),
        ),
        [ANY] * 4,
        (ANY,) * 4,
        [
            pltpu.VMEM((8, 8, 2 * SLICE), F32),
            pltpu.VMEM((4, 16, 2 * SLICE), BF),
            pltpu.VMEM((2, 24, WIDTH), F32),
            pltpu.VMEM((48, WIDTH), BF),
        ]
        + sems(72)
        + [pltpu.SemaphoreType.DMA((2,))],
        wo,
        wgu,
        wd,
        cot,
    )


def heads_to_tokens_body(src, dst, send, recv):
    me = place()
    net = Net(send, recv)
    greet(me, CTX_ALL)
    mine = ctx_of(me)
    columns = pl.ds(pl.multiple_of(mine * HEAD_SIZE, HEAD_SIZE), HEAD_SIZE)
    copies = []
    for o in CTX_ALL:
        to = moved(me, o)
        copies.append(net.put(src.at[ctx_of(to)], dst.at[:, columns], to))
    own = net.local(src.at[mine], dst.at[:, columns])
    for copy in copies:
        copy.wait_recv()
    own.wait()
    net.finish()


def heads_to_tokens(attended):
    return remote(
        heads_to_tokens_body,
        "heads_to_tokens",
        3,
        shape((TOK, QUERY_HEADS * HEAD_SIZE), BF),
        [ANY],
        ANY,
        sems(16),
        attended.reshape(16, TOK, HEAD_SIZE),
    )


def tokens_to_heads_body(src, dst, send, recv):
    me = place()
    net = Net(send, recv)
    greet(me, CTX_ALL)
    mine = ctx_of(me)

    def columns(at):
        return pl.ds(pl.multiple_of(ctx_of(at) * HEAD_SIZE, HEAD_SIZE), HEAD_SIZE)

    copies = []
    for o in CTX_ALL:
        to = moved(me, o)
        copies.append(net.put(src.at[:, columns(to)], dst.at[mine], to))
    own = net.local(src.at[:, columns(me)], dst.at[mine])
    for copy in copies:
        copy.wait_recv()
    own.wait()
    net.finish()


def tokens_to_heads(grad_att):
    return remote(
        tokens_to_heads_body,
        "tokens_to_heads",
        4,
        shape((16, TOK, HEAD_SIZE), BF),
        [ANY],
        ANY,
        sems(16),
        grad_att,
    )


def ring_gather_body(src, dst, send, recv):
    me = place()
    z, c = me[0], me[4]
    net = Net(send, recv)
    greet(me, RING + [SIBLING])
    over = moved(me, SIBLING)
    copies = [net.put(src, dst.at[z, c], moved(me, o)) for o in RING]
    passed = [net.put(src, dst.at[z, c], over)]
    own = net.local(src, dst.at[z, c])
    for o, copy in zip(RING, copies):
        copy.wait_recv()
        s = before(me, o)[0]
        passed.append(net.put(dst.at[s, c], dst.at[s, c], over))
    for copy in passed:
        copy.wait_recv()
    own.wait()
    net.finish()


def ring_gather(second_in):
    return remote(
        ring_gather_body,
        "ring_gather",
        5,
        shape((4, 2, TOK, WIDTH), BF),
        [ANY],
        ANY,
        sems(16),
        second_in,
    )


def add_blocks(count, rows, first, second, out):
    @pl.loop(0, count)
    def _(k):
        @pl.loop(0, TOK // rows)
        def _(r):
            at = pl.ds(pl.multiple_of(r * rows, rows), rows)
            out[k, at] = (first[k, at].astype(F32) + second[k, at].astype(F32)).astype(BF)


def sum_blocks(count, rows, own, received, out):
    @pl.loop(0, TOK // rows)
    def _(r):
        at = pl.ds(pl.multiple_of(r * rows, rows), rows)
        total = own[at].astype(F32)
        for k in range(count):
            total = total + received[k, at].astype(F32)
        out[at] = total


def ring_scatter_body(parts, out, got, held, mixed, arrived, send, recv):
    me = place()
    z, c = me[0], me[4]
    net = Net(send, recv)
    greet(me, RING + [SIBLING])
    over = moved(me, SIBLING)
    first = net.put(parts.at[:, 1 - c], got, over)
    own = net.local(parts.at[:, c], held)
    own.wait()
    first.wait_recv()
    add_blocks(4, 32, held, got, mixed)
    copies = []
    for k, o in enumerate(RING):
        to = moved(me, o)
        copies.append(net.put(mixed.at[to[0]], arrived.at[k], to))
    for copy in copies:
        copy.wait_recv()
    sum_blocks(3, 32, mixed.at[z], arrived, out)
    net.finish()


def ring_scatter(parts):
    return remote(
        ring_scatter_body,
        "ring_scatter",
        6,
        shape((TOK, WIDTH), F32),
        [ANY],
        VMEM,
        [pltpu.VMEM((4, TOK, WIDTH), BF)] * 3 + [pltpu.VMEM((3, TOK, WIDTH), BF)] + sems(8),
        parts,
    )


def last_scatter_body(
    parts, dwq, gains, out, dwq_out, gain_out,
    got, held, mixed, arrived, dw_got, dw_sum, g_ctx, g_mine, g_dp, send, recv,
):
    me = place()
    xh, y, c = me[2], me[3], me[4]
    net = Net(send, recv)
    greet(me, CTX_ALL + DP_ALL)
    over = moved(me, SIBLING)
    mine, here = ctx_of(me), dp_of(me)
    first = net.put(parts.at[:, 1 - c], got, over)
    own = net.local(parts.at[:, c], held)
    columns = []
    for k, o in enumerate(DP_ALL):
        to = moved(me, o)
        columns.append(net.put(dwq.at[dp_of(to)], dw_got.at[k], to))
    small = [net.put(gains, g_ctx.at[k], moved(me, o)) for k, o in enumerate(CTX_ALL)]
    own.wait()
    first.wait_recv()
    add_blocks(8, 32, held, got, mixed)
    copies = []
    for k, o in enumerate(CTX_SAME):
        to = moved(me, o)
        copies.append(net.put(mixed.at[to[2] * 4 + to[3]], arrived.at[k], to))
    for copy in small:
        copy.wait_recv()
    total = gains[...]
    for k in range(15):
        total = total + g_ctx[k]
    g_mine[...] = total
    small = [net.put(g_mine, g_dp.at[k], moved(me, o)) for k, o in enumerate(DP_ALL)]
    for copy in columns:
        copy.wait_recv()
    dw = dwq[here].astype(F32)
    for k in range(7):
        dw = dw + dw_got[k].astype(F32)
    dw_sum[...] = dw.reshape(16, 8, 2 * HEAD_SIZE)
    rows = []
    for o in CTX_ALL:
        to = moved(me, o)
        rows.append(net.put(dw_sum.at[ctx_of(to)], dwq_out.at[mine], to))
    keep = net.local(dw_sum.at[mine], dwq_out.at[mine])
    for copy in small:
        copy.wait_recv()
    total = g_mine[...]
    for k in range(7):
        total = total + g_dp[k]
    gain_out[...] = total
    for copy in copies:
        copy.wait_recv()
    sum_blocks(7, 32, mixed.at[xh * 4 + y], arrived, out)
    for copy in rows:
        copy.wait_recv()
    keep.wait()
    net.finish()


def last_scatter(parts, dwq, gains):
    return remote(
        last_scatter_body,
        "last_scatter",
        7,
        (shape((TOK, WIDTH), F32), shape((16, 8, 2 * HEAD_SIZE), F32), shape((24, 128), F32)),
        [ANY, VMEM, VMEM],
        (VMEM, ANY, VMEM),
        [pltpu.VMEM((8, TOK, WIDTH), BF)] * 3
        + [
            pltpu.VMEM((7, TOK, WIDTH), BF),
            pltpu.VMEM((7, TOK, 2 * HEAD_SIZE), BF),
            pltpu.VMEM((16, 8, 2 * HEAD_SIZE), F32),
            pltpu.VMEM((15, 24, 128), F32),
            pltpu.VMEM((24, 128), F32),
            pltpu.VMEM((7, 24, 128), F32),
        ]
        + sems(72),
        parts,
        dwq,
        gains,
    )


def weight_scatter_body(
    dwo, dgu, dwd, parts, wo_out, gu_out, wd_out, out,
    wo_got, wo_one, wo_ring, wo_two, wo_plane, gu_got, gu_sum, wd_got, wd_sum, wd_half,
    p_got, p_one, p_ring, send, recv, gate,
):
    me = place()
    z, xl, xh, y, c = me
    net = Net(send, recv)
    barrier = pltpu.get_barrier_semaphore()
    peers = PLANE + RING_ALL
    for o in peers:
        pl.semaphore_signal(barrier, inc=1, device_id=moved(me, o), device_id_type=BY_MESH)
    for o in CTX_SAME:
        pl.semaphore_signal(barrier, inc=1, device_id=swapped(me, o), device_id_type=BY_MESH)

    @pl.when(xl != c)
    def _():
        pl.semaphore_signal(barrier, inc=1, device_id=(z, c, xh, y, xl), device_id_type=BY_MESH)

    pl.semaphore_wait(barrier, len(peers) + len(CTX_SAME) + (xl + c - 2 * xl * c))
    over = moved(me, SIBLING)
    near_wo = net.put(dwo.at[:, :, 1 - c], wo_got, over)
    near_p = net.put(parts.at[:, 1 - c], p_got, over)
    ups = []
    for k, o in enumerate(PLANE):
        to = moved(me, o)
        ups.append(net.put(dgu.at[:, plane_of(to)], gu_got.at[k], to))
    downs = []
    for k, o in enumerate(CTX_SAME):
        to = swapped(me, o)
        downs.append(net.put(dwd.at[to[2] * 4 + to[3]], wd_got.at[k + 1], to))

    @pl.when(xl != c)
    def _():
        copy = pltpu.make_async_remote_copy(
            src_ref=dwd.at[xh * 4 + y],
            dst_ref=wd_got.at[0],
            send_sem=gate.at[0],
            recv_sem=gate.at[1],
            device_id=(z, c, xh, y, xl),
            device_id_type=BY_MESH,
        )
        copy.start()
        copy.wait()

    @pl.when(xl == c)
    def _():
        copy = pltpu.make_async_copy(dwd.at[xh * 4 + y], wd_got.at[0], gate.at[0])
        copy.start()
        copy.wait()

    near_wo.wait_recv()

    @pl.loop(0, 4)
    def _(a):
        @pl.loop(0, 16)
        def _(b):
            wo_one[a, b] = (dwo[a, b, c].astype(F32) + wo_got[a, b].astype(F32)).astype(BF)

    ring = []
    for k, o in enumerate(RING):
        to = moved(me, o)
        ring.append(net.put(wo_one.at[to[0]], wo_ring.at[k], to))
    near_p.wait_recv()
    add_blocks(4, 32, parts.at[:, c], p_got, p_one)
    p_copies = []
    for k, o in enumerate(RING):
        to = moved(me, o)
        p_copies.append(net.put(p_one.at[to[0]], p_ring.at[k], to))
    for copy in ring:
        copy.wait_recv()

    @pl.loop(0, 16)
    def _(b):
        total = wo_one[z, b].astype(F32)
        for k in range(3):
            total = total + wo_ring[k, b].astype(F32)
        wo_two[b] = total.astype(BF)

    flat = []
    for k, o in enumerate(PLANE):
        to = moved(me, o)
        flat.append(net.put(wo_two.at[plane_of(to)], wo_plane.at[k], to))
    for copy in ups:
        copy.wait_recv()

    @pl.loop(0, 4)
    def _(a):
        total = dgu[a, plane_of(me)].astype(F32)
        for k in range(15):
            total = total + gu_got[k, a].astype(F32)
        gu_sum[2 * a] = total[:8]
        gu_sum[2 * a + 1] = total[8:]

    slices = []
    for o in RING_ALL:
        to = moved(me, o)
        slices.append(net.put(gu_sum.at[ring_of(to)], gu_out.at[ring_of(me)], to))
    keep = net.local(gu_sum.at[ring_of(me)], gu_out.at[ring_of(me)])
    for copy in downs:
        copy.wait_recv()
    total = wd_got[0].astype(F32)
    for k in range(1, 8):
        total = total + wd_got[k].astype(F32)
    wd_sum[0] = total[:24]
    wd_sum[1] = total[24:]
    half = net.put(wd_sum.at[1 - c], wd_half, over)
    for copy in p_copies:
        copy.wait_recv()
    sum_blocks(3, 32, p_one.at[z], p_ring, out)
    half.wait_recv()
    wd_out[...] = wd_sum[c] + wd_half[...]
    for copy in flat:
        copy.wait_recv()
    total = wo_two[plane_of(me)].astype(F32)
    for k in range(15):
        total = total + wo_plane[k].astype(F32)
    wo_out[...] = total
    for copy in slices:
        copy.wait_recv()
    keep.wait()
    net.finish()


def weight_scatter(dwo, dgu, dwd, parts):
    return remote(
        weight_scatter_body,
        "weight_scatter",
        8,
        (
            shape((16, WIDTH), F32),
            shape((8, 8, 2 * SLICE), F32),
            shape((24, WIDTH), F32),
            shape((TOK, WIDTH), F32),
        ),
        [VMEM] * 4,
        (VMEM, ANY, VMEM, VMEM),
        [
            pltpu.VMEM((4, 16, 16, WIDTH), BF),
            pltpu.VMEM((4, 16, 16, WIDTH), BF),
            pltpu.VMEM((3, 16, 16, WIDTH), BF),
            pltpu.VMEM((16, 16, WIDTH), BF),
            pltpu.VMEM((15, 16, WIDTH), BF),
            pltpu.VMEM((15, 4, 16, 2 * SLICE), BF),
            pltpu.VMEM((8, 8, 2 * SLICE), F32),
            pltpu.VMEM((8, 48, WIDTH), BF),
            pltpu.VMEM((2, 24, WIDTH), F32),
            pltpu.VMEM((24, WIDTH), F32),
            pltpu.VMEM((4, TOK, WIDTH), BF),
            pltpu.VMEM((4, TOK, WIDTH), BF),
            pltpu.VMEM((3, TOK, WIDTH), BF),
        ]
        + sems(72)
        + [pltpu.SemaphoreType.DMA((2,))],
        dwo,
        dgu,
        dwd,
        parts,
    )


def dot(a, b):
    return jnp.dot(a, b, preferred_element_type=F32)


def dot_t(a, b):
    return lax.dot_general(a, b, (((1,), (1,)), ((), ())), preferred_element_type=F32)


def t_dot(a, b):
    return lax.dot_general(a, b, (((0,), (0,)), ((), ())), preferred_element_type=F32)


def turned(v):
    half = HEAD_SIZE // 2
    return jnp.concatenate([-v[:, half:], v[:, :half]], 1)


def turned_back(v):
    half = HEAD_SIZE // 2
    return jnp.concatenate([v[:, half:], -v[:, :half]], 1)


def inverse_root(v):
    return lax.rsqrt(jnp.mean(v * v, -1, keepdims=True) + EPS)


def visible_at(begin, i, b):
    row = i * BLOCK + lax.broadcasted_iota(jnp.int32, (BLOCK, BLOCK), 0)
    col = b * BLOCK + lax.broadcasted_iota(jnp.int32, (BLOCK, BLOCK), 1)
    return (col >= begin) & (col <= row)


def attend_body(
    x, w, gain, q_gain, k_gain, cos, sin, begin,
    q_out, k_out, v_out, qu_out, ku_out, att_out, full_out, norm_out,
):
    i = pl.program_id(0)
    at = pl.ds(pl.multiple_of(i * BLOCK, BLOCK), BLOCK)
    inputs = x[...].astype(F32)
    first_in = (inputs * inverse_root(inputs) * gain[...]).astype(BF)
    projected = dot(first_in, w[...])
    q_un = projected[:, :HEAD_SIZE]
    k_un = projected[:, HEAD_SIZE : 2 * HEAD_SIZE]
    v_out[at] = projected[:, 2 * HEAD_SIZE :].astype(BF)
    qu_out[...] = q_un
    ku_out[...] = k_un
    cosine, sine = cos[...], sin[...]
    q_scaled = q_un * inverse_root(q_un) * q_gain[...]
    k_scaled = k_un * inverse_root(k_un) * k_gain[...]
    q = (q_scaled * cosine + turned(q_scaled) * sine).astype(BF)
    q_out[...] = q
    k_out[at] = (k_scaled * cosine + turned(k_scaled) * sine).astype(BF)
    start = begin[...]

    def step(b, carry):
        total, acc = carry
        cols = pl.ds(pl.multiple_of(b * BLOCK, BLOCK), BLOCK)
        s = dot_t(q, k_out[cols])
        e = jnp.where(visible_at(start, i, b), jnp.exp2(s * SCALE2), 0.0)
        total = total + jnp.sum(e, 1, keepdims=True)
        acc = acc + dot(e.astype(BF), v_out[cols])
        return total, acc

    total, acc = lax.fori_loop(
        0, i + 1, step, (jnp.zeros((BLOCK, 1), F32), jnp.zeros((BLOCK, HEAD_SIZE), F32))
    )
    norm = 1.0 / total
    full = acc * norm
    full_out[...] = full
    att_out[...] = full.astype(BF)
    norm_out[...] = jnp.broadcast_to(norm, (BLOCK, HEAD_SIZE))


def attend(x, w, gain, q_gain, k_gain, cos, sin, begin):
    rows = lambda cols: pl.BlockSpec((BLOCK, cols), lambda i: (i, 0))
    whole = lambda r, cols: pl.BlockSpec((r, cols), lambda i: (0, 0))
    head = (GROUP, HEAD_SIZE)
    return pl.pallas_call(
        attend_body,
        name="attend",
        grid=(GROUP // BLOCK,),
        in_specs=[
            rows(WIDTH),
            whole(WIDTH, 3 * HEAD_SIZE),
            whole(1, WIDTH),
            whole(1, HEAD_SIZE),
            whole(1, HEAD_SIZE),
            rows(HEAD_SIZE),
            rows(HEAD_SIZE),
            rows(1),
        ],
        out_specs=(
            rows(HEAD_SIZE),
            whole(*head),
            whole(*head),
            rows(HEAD_SIZE),
            rows(HEAD_SIZE),
            rows(HEAD_SIZE),
            rows(HEAD_SIZE),
            rows(HEAD_SIZE),
        ),
        out_shape=(
            shape(head, BF),
            shape(head, BF),
            shape(head, BF),
            shape(head, F32),
            shape(head, F32),
            shape(head, BF),
            shape(head, F32),
            shape(head, F32),
        ),
        compiler_params=pltpu.CompilerParams(vmem_limit_bytes=50 * MIB),
    )(x, w, gain, q_gain, k_gain, cos, sin, begin)


def attend_back_body(q, k, v, grad, full, norm, begin, dq_out, dk_out, dv_out):
    i = pl.program_id(0)

    @pl.when(i == 0)
    def _():
        dk_out[...] = jnp.zeros_like(dk_out)
        dv_out[...] = jnp.zeros_like(dv_out)

    qb, gb = q[...], grad[...]
    inverse = norm[...][:, :1]
    inner = jnp.sum(gb.astype(F32) * full[...], 1, keepdims=True)
    start = begin[...]

    def step(b, acc):
        cols = pl.ds(pl.multiple_of(b * BLOCK, BLOCK), BLOCK)
        kb, vb = k[cols], v[cols]
        s = dot_t(qb, kb)
        p = jnp.where(visible_at(start, i, b), jnp.exp2(s * SCALE2) * inverse, 0.0)
        dp = dot_t(gb, vb)
        ds = (p * (dp - inner)).astype(BF)
        dv_out[cols] += t_dot(p.astype(BF), gb)
        dk_out[cols] += t_dot(ds, qb)
        return acc + dot(ds, kb)

    dq_out[...] = lax.fori_loop(0, i + 1, step, jnp.zeros((BLOCK, HEAD_SIZE), F32)) * SCALE

    @pl.when(i == GROUP // BLOCK - 1)
    def _():
        dk_out[...] = dk_out[...] * SCALE


def attend_back(q, k, v, grad, full, norm, begin):
    rows = lambda cols: pl.BlockSpec((BLOCK, cols), lambda i: (i, 0))
    whole = lambda r, cols: pl.BlockSpec((r, cols), lambda i: (0, 0))
    head = (GROUP, HEAD_SIZE)
    return pl.pallas_call(
        attend_back_body,
        name="attend_back",
        grid=(GROUP // BLOCK,),
        in_specs=[rows(HEAD_SIZE), whole(*head), whole(*head)] + [rows(HEAD_SIZE)] * 3 + [rows(1)],
        out_specs=(rows(HEAD_SIZE), whole(*head), whole(*head)),
        out_shape=(shape(head, F32),) * 3,
        compiler_params=pltpu.CompilerParams(vmem_limit_bytes=50 * MIB),
    )(q, k, v, grad, full, norm, begin)


def feed_forward_body(s_in, cot, w_gu, w_d, p_out, p_grad, dgu_out, dwd_out, dgu_acc, dwd_acc):
    i = pl.program_id(0)

    @pl.when(i == 0)
    def _():
        dgu_acc[...] = jnp.zeros_like(dgu_acc)
        dwd_acc[...] = jnp.zeros_like(dwd_acc)

    s, ct = s_in[...], cot[...]
    gu = dot(s, w_gu[...])
    gate, up = gu[:, :SLICE], gu[:, SLICE:]
    sigma = 1.0 / (1.0 + jnp.exp(-gate))
    swish = gate * sigma
    hidden = (swish * up).astype(BF)
    p_out[...] = dot(hidden, w_d[...]).astype(BF)
    grad_hidden = dot_t(ct, w_d[...])
    grad_gate = grad_hidden * up * sigma * (1.0 + gate * (1.0 - sigma))
    grad_gu = jnp.concatenate([grad_gate, grad_hidden * swish], 1).astype(BF)
    p_grad[...] = dot_t(grad_gu, w_gu[...]).astype(BF)
    dgu_acc[...] += t_dot(s, grad_gu)
    dwd_acc[...] += t_dot(hidden, ct)

    @pl.when(i == pl.num_programs(0) - 1)
    def _():
        dgu_out[...] = dgu_acc[...].astype(BF)
        dwd_out[...] = dwd_acc[...].astype(BF)


def feed_forward(s_in, cot, w_gu, w_d):
    rows = pl.BlockSpec((BLOCK, WIDTH), lambda i: (i, 0))
    whole = lambda r, cols: pl.BlockSpec((r, cols), lambda i: (0, 0))
    return pl.pallas_call(
        feed_forward_body,
        name="feed_forward",
        grid=(8 * TOK // BLOCK,),
        in_specs=[rows, rows, whole(WIDTH, 2 * SLICE), whole(SLICE, WIDTH)],
        out_specs=(rows, rows, whole(WIDTH, 2 * SLICE), whole(SLICE, WIDTH)),
        out_shape=(
            shape((8 * TOK, WIDTH), BF),
            shape((8 * TOK, WIDTH), BF),
            shape((WIDTH, 2 * SLICE), BF),
            shape((SLICE, WIDTH), BF),
        ),
        scratch_shapes=[pltpu.VMEM((WIDTH, 2 * SLICE), F32), pltpu.VMEM((SLICE, WIDTH), F32)],
        compiler_params=pltpu.CompilerParams(vmem_limit_bytes=50 * MIB),
    )(s_in, cot, w_gu, w_d)


def head_back(unnormed, grad, cosine, sine, gain):
    inverse = inverse_root(unnormed)
    hat = unnormed * inverse
    back = grad * cosine + turned_back(grad * sine)
    g = back * gain
    raw = inverse * (g - hat * jnp.mean(g * hat, -1, keepdims=True))
    return raw, jnp.sum(back * hat, 0, keepdims=True)


def project_back_body(
    x, w, gain, q_gain, k_gain, cos, sin, q_un, k_un, dq, dkv, got, flag,
    parts, dw_out, gains_out, q_gain_out, k_gain_out, dw_acc,
):
    i = pl.program_id(0)

    @pl.when(i == 0)
    def _():
        dw_acc[...] = jnp.zeros_like(dw_acc)
        gains_out[...] = jnp.zeros_like(gains_out)
        q_gain_out[...] = jnp.zeros_like(q_gain_out)
        k_gain_out[...] = jnp.zeros_like(k_gain_out)

    is_key = flag[...]
    inputs = x[...].astype(F32)
    normed = inputs * inverse_root(inputs)
    first_in = (normed * gain[...]).astype(BF)
    cosine, sine = cos[...], sin[...]
    dq_raw, q_part = head_back(q_un[...], dq[...], cosine, sine, q_gain[...])
    both = dkv[...] + got[...].astype(F32)
    dk_raw, k_part = head_back(k_un[...], both, cosine, sine, k_gain[...])
    second = jnp.where(is_key > 0.5, dk_raw, both)
    grad = jnp.concatenate([dq_raw, second], 1).astype(BF)
    dw_acc[...] += t_dot(first_in, grad)
    grad_first = dot_t(grad, w[...])
    parts[...] = grad_first.astype(BF)
    gains_out[...] += jnp.sum(grad_first * normed, 0, keepdims=True)
    q_gain_out[...] += q_part
    k_gain_out[...] += k_part * is_key

    @pl.when(i == pl.num_programs(0) - 1)
    def _():
        dw_out[...] = dw_acc[...].astype(BF)


def project_back(x, w, gain, q_gain, k_gain, cos, sin, q_un, k_un, dq, dkv, got, flag):
    rows = lambda cols: pl.BlockSpec((BLOCK, cols), lambda i: (i, 0))
    whole = lambda r, cols: pl.BlockSpec((r, cols), lambda i: (0, 0))
    return pl.pallas_call(
        project_back_body,
        name="project_back",
        grid=(GROUP // BLOCK,),
        in_specs=[
            rows(WIDTH),
            whole(WIDTH, 2 * HEAD_SIZE),
            whole(1, WIDTH),
            whole(1, HEAD_SIZE),
            whole(1, HEAD_SIZE),
        ]
        + [rows(HEAD_SIZE)] * 7
        + [whole(1, HEAD_SIZE)],
        out_specs=(
            rows(WIDTH),
            whole(WIDTH, 2 * HEAD_SIZE),
            whole(1, WIDTH),
            whole(1, HEAD_SIZE),
            whole(1, HEAD_SIZE),
        ),
        out_shape=(
            shape((GROUP, WIDTH), BF),
            shape((WIDTH, 2 * HEAD_SIZE), BF),
            shape((1, WIDTH), F32),
            shape((1, HEAD_SIZE), F32),
            shape((1, HEAD_SIZE), F32),
        ),
        scratch_shapes=[pltpu.VMEM((WIDTH, 2 * HEAD_SIZE), F32)],
        compiler_params=pltpu.CompilerParams(vmem_limit_bytes=50 * MIB),
    )(x, w, gain, q_gain, k_gain, cos, sin, q_un, k_un, dq, dkv, got, flag)


def swap_body(src, dst, send, recv):
    me = place()
    net = Net(send, recv)
    greet(me, [SIBLING])
    net.put(src, dst, moved(me, SIBLING)).wait_recv()
    net.finish()


def swap(values):
    return remote(
        swap_body, "swap", 9, shape(values.shape, values.dtype), [ANY], ANY, sems(1), values
    )


def layout(doc_lengths):
    ends = jnp.cumsum(doc_lengths)
    index = jnp.arange(GROUP, dtype=jnp.int32)
    starts = ends - doc_lengths
    begin = jnp.max(jnp.where(index[:, None] >= starts[None, :], starts[None, :], 0), 1)
    return begin, index - begin


def angles(position):
    half = HEAD_SIZE // 2
    freq = THETA ** (-(jnp.arange(half, dtype=F32) * 2.0 / HEAD_SIZE))
    phase = position.astype(F32)[:, None] * freq[None, :]
    cosine, sine = jnp.cos(phase), jnp.sin(phase)
    return jnp.concatenate([cosine, cosine], 1), jnp.concatenate([sine, sine], 1)


def norm_back(values, inverse, grad):
    cubed = inverse * inverse * inverse
    return inverse * grad - values * cubed * jnp.mean(grad * values, -1, keepdims=True)


def on_device(
    tokens, lengths, attn_gain, q_gain, k_gain, qkv, w_out, mlp_gain, w_gate_up, w_down, cotangent
):
    core = lax.axis_index("c")
    device = lax.axis_index(AXES)
    key_at, value_at = QUERY_HEADS * HEAD_SIZE, (QUERY_HEADS + KEY_VALUE_HEADS) * HEAD_SIZE

    rows = qkv.astype(F32)
    wq = rows[:, :key_at].reshape(8, 16, 1, HEAD_SIZE)
    wk = jnp.repeat(rows[:, key_at:value_at].reshape(8, 8, 1, HEAD_SIZE), 2, axis=1)
    wv = jnp.repeat(rows[:, value_at:].reshape(8, 8, 1, HEAD_SIZE), 2, axis=1)
    wq = jnp.concatenate([wq, wk, wv], 2).reshape(8, 16, 3 * HEAD_SIZE).swapaxes(0, 1)
    gains = jnp.concatenate([attn_gain, mlp_gain, q_gain, k_gain]).astype(F32)
    gains = jnp.broadcast_to(jnp.pad(gains, (0, 128 - 18))[None], (8, 128))
    begin, position = layout(lengths[0])
    begin = begin[:, None]
    cosine, sine = angles(position)

    x_all, w_qkv, gains = first_gather(tokens, wq, gains)
    x_all = x_all.reshape(GROUP, WIDTH)
    w_qkv = w_qkv.reshape(WIDTH, 3 * HEAD_SIZE)
    gains = gains.reshape(128, 128)
    gain_one = gains[:, :8].reshape(1, WIDTH)
    gain_two = gains[:, 8:16].reshape(1, WIDTH)
    gain_q = gains[:, 16].reshape(1, HEAD_SIZE)
    gain_k = gains[:, 17].reshape(1, HEAD_SIZE)

    q, k, v, q_un, k_un, att, full, norm = attend(
        x_all, w_qkv, gain_one, gain_q, gain_k, cosine, sine, begin
    )
    attended = heads_to_tokens(att)

    wgu = w_gate_up.astype(F32)
    wgu = jnp.concatenate(
        [wgu[:, :FF].reshape(8, 8, SLICE), wgu[:, FF:].reshape(8, 8, SLICE)], 2
    ).swapaxes(0, 1)
    wo_all, gu_all, wd_all, cot_all = weight_gather(w_out, wgu, w_down.astype(F32), cotangent)
    wo_all = wo_all.reshape(QUERY_HEADS * HEAD_SIZE, WIDTH)
    gu_all = gu_all.reshape(WIDTH, 2 * SLICE)
    wd_all = wd_all.reshape(SLICE, WIDTH)
    cot_all = cot_all.reshape(8 * TOK, WIDTH)

    inputs = tokens.astype(F32)
    residual = inputs + dot(attended, wo_all)
    inverse_two = inverse_root(residual)
    second_in = (residual * inverse_two * gain_two).astype(BF)
    s_all = ring_gather(second_in).reshape(8 * TOK, WIDTH)
    p_out, p_grad, dgu, dwd = feed_forward(s_all, cot_all, gu_all, wd_all)
    grad_second = ring_scatter(p_grad.reshape(4, 2, TOK, WIDTH))

    grad_gain_two = jnp.sum(grad_second * (residual * inverse_two), 0)
    grad_resid = cotangent.astype(F32) + norm_back(residual, inverse_two, grad_second * gain_two)
    resid_low = grad_resid.astype(BF)
    grad_att = dot_t(resid_low, wo_all).astype(BF)
    dwo = t_dot(attended, resid_low).astype(BF)
    grad_heads = tokens_to_heads(grad_att).reshape(GROUP, HEAD_SIZE)

    dq, dk, dv = attend_back(q, k, v, grad_heads, full, norm, begin)
    is_key = core == 0
    dkv = jnp.where(is_key, dk, dv)
    got = swap(jnp.where(is_key, dv, dk).astype(BF))
    flag = jnp.broadcast_to(is_key.astype(F32), (1, HEAD_SIZE))
    w_two = jnp.concatenate(
        [
            w_qkv[:, :HEAD_SIZE],
            jnp.where(is_key, w_qkv[:, HEAD_SIZE : 2 * HEAD_SIZE], w_qkv[:, 2 * HEAD_SIZE :]),
        ],
        1,
    )
    parts, dwq, grad_gain_one, grad_gain_q, grad_gain_k = project_back(
        x_all, w_two, gain_one, gain_q, gain_k, cosine, sine, q_un, k_un, dq, dkv, got, flag
    )
    packed = jnp.concatenate(
        [
            grad_gain_one.reshape(8, 128),
            grad_gain_two.reshape(8, 128),
            grad_gain_q,
            grad_gain_k,
            jnp.zeros((6, 128), F32),
        ]
    )
    grad_first, dwq, packed = last_scatter(
        parts.reshape(8, 2, TOK, WIDTH), dwq.reshape(8, TOK, 2 * HEAD_SIZE), packed
    )
    inverse_one = inverse_root(inputs)
    input_grad = grad_resid + norm_back(inputs, inverse_one, grad_first * gain_one)

    grad_w_out, dgu, grad_down, mlp_out = weight_scatter(
        dwo.reshape(4, 16, 2, 16, WIDTH),
        dgu.reshape(4, 16, 16, 2 * SLICE),
        dwd.reshape(8, 48, WIDTH),
        p_out.reshape(4, 2, TOK, WIDTH),
    )
    output = residual + mlp_out

    dwq = dwq.swapaxes(0, 1)
    dkv_cols = dwq[:, :, HEAD_SIZE:].reshape(8, 8, 2, HEAD_SIZE)
    grad_w_qkv = jnp.concatenate(
        [
            dwq[:, :, :HEAD_SIZE].reshape(8, -1),
            dkv_cols[:, :, 0].reshape(8, -1),
            dkv_cols[:, :, 1].reshape(8, -1),
        ],
        1,
    )
    dgu = dgu.swapaxes(0, 1)
    grad_gate_up = jnp.concatenate(
        [dgu[:, :, :SLICE].reshape(8, FF), dgu[:, :, SLICE:].reshape(8, FF)], 1
    )

    def own(first, rows, each):
        return lax.dynamic_slice_in_dim(packed[first : first + rows].reshape(-1), device * each, each)

    return (
        output,
        input_grad,
        own(0, 8, 8),
        own(16, 1, 1),
        own(17, 1, 1),
        grad_w_qkv,
        grad_w_out,
        own(8, 8, 8),
        grad_gate_up,
        grad_down,
    )


def solution(mesh):
    torus = Mesh(mesh.devices.reshape(SIZES), AXES)
    rows, line = P(AXES, None), P(AXES)
    return jax.shard_map(
        on_device,
        mesh=torus,
        in_specs=(rows, P(DP, None), line, line, line, rows, rows, line, rows, rows, rows),
        out_specs=(rows, rows, line, line, line, rows, rows, line, rows, rows),
        check_vma=False,
    )
```

```python
import math
import types

import jax
import jax.numpy as jnp
import numpy as np
from jax import lax
from jax.experimental import pallas as pl
from jax.experimental.pallas import tpu as pltpu
from jax.sharding import Mesh
from jax.sharding import PartitionSpec as P

QUERY_HEADS = 16
KEY_VALUE_HEADS = 8
HEAD = 128
WIDTH = 1024
FF = 3072
TOK = 128
GROUP = 2048
BLOCK = 256
WIDE = 512
SLICE = FF // 8
EPS = 1e-06
THETA = 1000000.0
SCALE = 1.0 / math.sqrt(HEAD)
SCALE2 = SCALE / math.log(2.0)
KEY_AT = QUERY_HEADS * HEAD
VALUE_AT = KEY_AT + KEY_VALUE_HEADS * HEAD

AXES = ("z", "xl", "xh", "y", "c")
SIZES = (4, 2, 2, 4, 2)
DP = ("z", "xl")
BF = jnp.bfloat16
F32 = jnp.float32
BY_MESH = pl.DeviceIdType.MESH
MIB = 2**20


def offsets(*axes):
    out = [()]
    for size, name in zip(SIZES, AXES):
        out = [o + (k,) for o in out for k in (range(size) if name in axes else (0,))]
    return out[1:]


SIBLING = (0, 0, 0, 0, 1)
CTX_ALL = offsets("xh", "y", "c")
DP_ALL = offsets("z", "xl")
X_PEERS = offsets("xl", "xh")
X_HALF = (0, 0, 1, 0, 0)
Y_PEERS = [(0, 0, 0, k, 0) for k in (1, 3, 2)]
Z_PEERS = [(k, 0, 0, 0, 0) for k in (1, 3, 2)]
RING_ALL = offsets("z", "c")
PEERS = sorted(set(CTX_ALL + DP_ALL + X_PEERS + RING_ALL))


def moved(me, offset):
    return tuple(lax.rem(m + o, s) if o else m for m, o, s in zip(me, offset, SIZES))


def before(me, offset):
    return tuple(lax.rem(m + s - o, s) if o else m for m, o, s in zip(me, offset, SIZES))


def ctx_of(at):
    return at[2] * 8 + at[3] * 2 + at[4]


def dp_of(at):
    return at[0] * 2 + at[1]


def ring_of(at):
    return at[0] * 2 + at[4]


def columns(k, width=HEAD):
    return pl.ds(pl.multiple_of(k * width, width), width)


class Net:
    def __init__(self, send, recv):
        self.send, self.recv, self.count, self.sent = send, recv, 0, []

    def take(self, n=1):
        k = self.count
        self.count += n
        return k

    def copy(self, src, dst, device, send, recv):
        return pltpu.make_async_remote_copy(
            src_ref=src,
            dst_ref=dst,
            send_sem=self.send.at[send],
            recv_sem=self.recv.at[recv],
            device_id=device,
            device_id_type=BY_MESH,
        )

    def put(self, src, dst, device):
        k = self.take()
        copy = self.copy(src, dst, device, k, k)
        copy.start()
        self.sent.append(copy)
        return copy

    def local(self, src, dst):
        copy = pltpu.make_async_copy(src, dst, self.send.at[self.take()])
        copy.start()
        return copy

    def drain(self):
        for copy in self.sent:
            copy.wait_send()
        self.sent = []


def arrived(copies):
    for copy in copies:
        copy.wait_recv()


def dot(a, b):
    return jnp.dot(a, b, preferred_element_type=F32)


def dot_t(a, b):
    return lax.dot_general(a, b, (((1,), (1,)), ((), ())), preferred_element_type=F32)


def t_dot(a, b):
    return lax.dot_general(a, b, (((0,), (0,)), ((), ())), preferred_element_type=F32)


def turned(v):
    return pltpu.roll(v, HEAD // 2, 1)


def inverse_root(v):
    return lax.rsqrt(jnp.mean(v * v, -1, keepdims=True) + EPS)


def head_back(unnormed, grad, cosine, sine, gain):
    inverse = inverse_root(unnormed)
    hat = unnormed * inverse
    back = grad * cosine - turned(grad) * sine
    g = back * gain
    raw = inverse * (g - hat * jnp.mean(g * hat, -1, keepdims=True))
    return raw, jnp.sum(back * hat, 0, keepdims=True)


def norm_back(values, inverse, grad):
    cubed = inverse * inverse * inverse
    return inverse * grad - values * cubed * jnp.mean(grad * values, -1, keepdims=True)


BUFFERS = dict(
    wq_src=((16, 8, 3 * HEAD), F32),
    wq_tmp=((16, 8, 3 * HEAD), F32),
    w_low=((TOK, 3 * HEAD), BF),
    w_all=((8, TOK, 3 * HEAD), BF),
    w_two=((WIDTH, 2 * HEAD), BF),
    g_tmp=((16, 8, 128), F32),
    g_row=((16, 128), F32),
    g_all=((8, 16, 128), F32),
    gain_one=((1, WIDTH), F32),
    gain_two=((1, WIDTH), F32),
    gain_q=((1, HEAD), F32),
    gain_k=((1, HEAD), F32),
    gu_src=((8, 8, 2 * SLICE), F32),
    gu_tmp=((8, 8, 2 * SLICE), F32),
    gu_low=((4, 16, 2 * SLICE), BF),
    gu_all=((4, 2, 2, 4, 16, 2 * SLICE), BF),
    wd_src=((24, WIDTH), F32),
    wd_tmp=((2, 24, WIDTH), F32),
    wd_all=((2, 4, 48, WIDTH), BF),
    wo_all=((4, 2, 2, 4, 2, 16, WIDTH), BF),
    cot_all=((4, 2, TOK, WIDTH), BF),
    x_all=((16, TOK, WIDTH), BF),
    angle=((8, BLOCK, HEAD), F32),
    q=((8, BLOCK, HEAD), BF),
    k=((8, BLOCK, HEAD), BF),
    v=((8, BLOCK, HEAD), BF),
    k_turned=((8, HEAD, BLOCK), BF),
    v_turned=((8, HEAD, BLOCK), BF),
    q_un=((8, BLOCK, HEAD), F32),
    k_un=((8, BLOCK, HEAD), F32),
    full=((8, HEAD, BLOCK), F32),
    norm=((8, 1, BLOCK), F32),
    att=((16, TOK, HEAD), BF),
    att_all=((TOK, QUERY_HEADS * HEAD), BF),
    resid=((TOK, WIDTH), F32),
    s_all=((4, 2, TOK, WIDTH), BF),
    hidden=((4, BLOCK, SLICE), BF),
    grad_gu=((4, BLOCK, 2 * SLICE), BF),
    pg=((4, 2, TOK, WIDTH), BF),
    pg_got=((4, TOK, WIDTH), BF),
    pg_ring=((3, TOK, WIDTH), BF),
    po_got=((4, TOK, WIDTH), BF),
    po_ring=((3, TOK, WIDTH), BF),
    dgu=((4, 16, 16, 2 * SLICE), BF),
    dgu_x=((3, 4, 4, 16, 2 * SLICE), BF),
    dgu_y=((3, 4, 16, 2 * SLICE), BF),
    dgu_sum=((8, 8, 2 * SLICE), F32),
    dwd=((8, 48, WIDTH), BF),
    dwd_x=((3, 4, 48, WIDTH), BF),
    dwd_y=((3, 48, WIDTH), BF),
    dwd_sum=((2, 24, WIDTH), F32),
    dwd_half=((24, WIDTH), F32),
    dwo_got=((4, 2, 2, 4, 16, WIDTH), BF),
    dwo_z=((3, 2, 2, 4, 16, WIDTH), BF),
    dwo_x=((3, 4, 16, WIDTH), BF),
    dwo_y=((3, 16, WIDTH), BF),
    grad_resid=((TOK, WIDTH), F32),
    ga=((TOK, QUERY_HEADS * HEAD), BF),
    gh_all=((16, TOK, HEAD), BF),
    dk=((4, WIDE, HEAD), F32),
    dv=((4, WIDE, HEAD), F32),
    swap_src=((4, WIDE, HEAD), BF),
    swap_got=((4, WIDE, HEAD), BF),
    dq=((2, WIDE, HEAD), F32),
    p_y=((2, 4, TOK, WIDTH), BF),
    p_x=((TOK, WIDTH), BF),
    dw=((2 * HEAD, WIDTH), F32),
    dw_low=((2 * HEAD, WIDTH), BF),
    dw_got=((7, 2 * HEAD, TOK), BF),
    dw_sum=((16, 8, 2 * HEAD), F32),
    hg=((8, 128), F32),
    hg_got=((15, 8, 128), F32),
    hg_mid=((8, 128), F32),
    hg_dp=((7, 8, 128), F32),
)
INPUTS = ("tok", "wqkv", "wo", "wgu", "wd", "cot", "gains", "freq", "lengths")
OUTPUTS = dict(
    output=((TOK, WIDTH), F32),
    input_grad=((TOK, WIDTH), F32),
    head_gains=((8, 128), F32),
    one_gains=((8, 128), F32),
    two_gains=((8, 128), F32),
    dwq_out=((8, 4096), F32),
    dwo_out=((16, WIDTH), F32),
    dgu_out=((8, 2 * FF), F32),
    dwd_out=((24, WIDTH), F32),
)
SEMS = 320
VMEM_LIMIT = 60 * MIB


def body(*refs):
    names = list(INPUTS) + list(OUTPUTS) + list(BUFFERS) + ["send", "recv"]
    r = types.SimpleNamespace(**dict(zip(names, refs, strict=True)))
    me = tuple(lax.axis_index(a) for a in AXES)
    z, xl, xh, y, c = me
    chip = xh * 4 + y
    mine, here, ring = ctx_of(me), dp_of(me), ring_of(me)
    over = moved(me, SIBLING)
    net = Net(r.send, r.recv)

    barrier = pltpu.get_barrier_semaphore()
    for o in PEERS:
        pl.semaphore_signal(barrier, inc=1, device_id=moved(me, o), device_id_type=BY_MESH)

    w = r.wqkv[...].astype(F32)
    for j in range(16):
        kv = (j // 2) * HEAD
        r.wq_src[j, :, :HEAD] = w[:, j * HEAD : (j + 1) * HEAD]
        r.wq_src[j, :, HEAD : 2 * HEAD] = w[:, KEY_AT + kv : KEY_AT + kv + HEAD]
        r.wq_src[j, :, 2 * HEAD :] = w[:, VALUE_AT + kv : VALUE_AT + kv + HEAD]
    w = r.wgu[...].astype(F32)
    for j in range(8):
        r.gu_src[j, :, :SLICE] = w[:, j * SLICE : (j + 1) * SLICE]
        r.gu_src[j, :, SLICE:] = w[:, FF + j * SLICE : FF + (j + 1) * SLICE]
    r.wd_src[...] = r.wd[...].astype(F32)
    r.wq_tmp[mine] = r.wq_src[mine]
    r.g_tmp[mine] = r.gains[...]
    r.gu_tmp[ring] = r.gu_src[ring]
    r.wd_tmp[c] = r.wd_src[...]
    r.x_all[mine] = r.tok[...]
    r.cot_all[z, c] = r.cot[...]
    r.wo_all[z, xl, xh, y, c] = r.wo[...]
    pl.semaphore_wait(barrier, len(PEERS))

    small = []
    for o in CTX_ALL:
        to = moved(me, o)
        small.append(net.put(r.wq_src.at[ctx_of(to)], r.wq_tmp.at[mine], to))
        small.append(net.put(r.gains, r.g_tmp.at[mine], to))
    tok_x = net.put(r.tok, r.x_all.at[mine], moved(me, X_HALF))
    tok_y = [net.put(r.tok, r.x_all.at[mine], moved(me, o)) for o in Y_PEERS]
    tok_own = net.put(r.tok, r.x_all.at[mine], over)
    wd_near = net.put(r.wd_src, r.wd_tmp.at[c], over)
    gu_ring = []
    for o in RING_ALL:
        to = moved(me, o)
        gu_ring.append(net.put(r.gu_src.at[ring_of(to)], r.gu_tmp.at[ring], to))
    wo_y = [net.put(r.wo, r.wo_all.at[z, xl, xh, y, c], moved(me, o)) for o in Y_PEERS]
    cot_z = [net.put(r.cot, r.cot_all.at[z, c], moved(me, o)) for o in Z_PEERS]
    cot_near = [net.put(r.cot, r.cot_all.at[z, c], over)]

    ends, starts = [], []
    total = 0
    for d in range(8):
        starts.append(total)
        total = total + r.lengths[0, d]

    def begin_of(index):
        out = jnp.zeros_like(index)
        for s in starts[1:]:
            out = jnp.where(index >= s, s, out)
        return out

    low = lax.broadcasted_iota(jnp.int32, (BLOCK, HEAD), 1) < HEAD // 2
    shift = jnp.where(low, 0.0, 0.5 * math.pi)

    @pl.loop(0, 8)
    def _(n):
        index = n * BLOCK + lax.broadcasted_iota(jnp.int32, (BLOCK, HEAD), 0)
        phase = (index - begin_of(index)).astype(F32) * r.freq[...]
        r.angle[n] = jnp.cos(phase - shift)

    def angles(n):
        both = r.angle[n]
        other = turned(both)
        return jnp.where(low, both, other), jnp.where(low, -other, both)

    arrived(small)
    r.w_low[...] = r.wq_tmp[...].reshape(TOK, 3 * HEAD).astype(BF)
    r.g_row[...] = r.g_tmp[:, 0, :]
    w_dp = []
    for o in DP_ALL:
        to = moved(me, o)
        w_dp.append(net.put(r.w_low, r.w_all.at[here], to))
        w_dp.append(net.put(r.g_row, r.g_all.at[here], to))
    r.w_all[here] = r.w_low[...]
    r.g_all[here] = r.g_row[...]

    def pass_on(ref, at):
        return net.put(ref.at[at], ref.at[at], over)

    tok_x.wait_recv()
    from_x = before(me, X_HALF)
    at_x = ctx_of(from_x)
    near = {(1, 0): pass_on(r.x_all, at_x)}
    tok_xy = [net.put(r.x_all.at[at_x], r.x_all.at[at_x], moved(me, o)) for o in Y_PEERS]
    arrived(gu_ring)
    r.gu_low[...] = r.gu_tmp[...].reshape(4, 16, 2 * SLICE).astype(BF)
    r.gu_all[:, xl, xh, y] = r.gu_low[...]
    gu_y = [net.put(r.gu_low, r.gu_all.at[:, xl, xh, y], moved(me, o)) for o in Y_PEERS]
    wd_near.wait_recv()
    wd_sems = net.take(3)

    @pl.when(xl == c)
    def _():
        r.wd_all[xh, y] = r.wd_tmp[...].reshape(48, WIDTH).astype(BF)
        for k, o in enumerate(Y_PEERS):
            at = r.wd_all.at[xh, y]
            net.copy(at, at, moved(me, o), wd_sems + k, wd_sems + k).start()

    arrived(wo_y)
    wo_x = []
    for o in X_PEERS:
        at = r.wo_all.at[z, xl, xh, :, c]
        wo_x.append(net.put(at, at, moved(me, o)))

    arrived(w_dp)
    gains = r.g_all[...].reshape(128, 128).astype(BF)
    dev = lax.broadcasted_iota(jnp.int32, (128, WIDTH), 0)
    lane = lax.broadcasted_iota(jnp.int32, (128, WIDTH), 1)
    spread = t_dot(gains, (lane // 8 == dev).astype(F32).astype(BF))
    pick = lax.broadcasted_iota(jnp.int32, (8, WIDTH), 1) % 8 == lax.broadcasted_iota(
        jnp.int32, (8, WIDTH), 0
    )
    r.gain_one[...] = jnp.sum(jnp.where(pick, spread[:8], 0.0), 0, keepdims=True)
    r.gain_two[...] = jnp.sum(jnp.where(pick, spread[8:16], 0.0), 0, keepdims=True)
    eye = lax.broadcasted_iota(jnp.int32, (128, 128), 0) == lax.broadcasted_iota(
        jnp.int32, (128, 128), 1
    )
    spread = t_dot(gains, eye.astype(F32).astype(BF))
    r.gain_q[...] = spread[16:17]
    r.gain_k[...] = spread[17:18]
    w_all = r.w_all[...].reshape(WIDTH, 3 * HEAD)
    r.w_two[:, :HEAD] = w_all[:, :HEAD]
    r.w_two[:, HEAD:] = jnp.where(c == 0, w_all[:, HEAD : 2 * HEAD], w_all[:, 2 * HEAD :])

    def project(n):
        inputs = r.x_all[pl.ds(2 * n, 2)].reshape(BLOCK, WIDTH).astype(F32)
        first_in = (inputs * inverse_root(inputs) * r.gain_one[...]).astype(BF)
        projected = dot(first_in, r.w_all[...].reshape(WIDTH, 3 * HEAD))
        q_un, k_un = projected[:, :HEAD], projected[:, HEAD : 2 * HEAD]
        value = projected[:, 2 * HEAD :]
        r.v[n] = value.astype(BF)
        r.v_turned[n] = value.T.astype(BF)
        r.q_un[n] = q_un
        r.k_un[n] = k_un
        cosine, sine = angles(n)
        q = q_un * inverse_root(q_un) * r.gain_q[...]
        r.q[n] = (q * cosine + turned(q) * sine).astype(BF)
        key = k_un * inverse_root(k_un) * r.gain_k[...]
        key = key * cosine + turned(key) * sine
        r.k[n] = key.astype(BF)
        r.k_turned[n] = key.T.astype(BF)

    def chip_of(at):
        return at[2] * 4 + at[3]

    tok_own.wait_recv()
    project(chip)
    waiting = [(1, 0)]

    def next_project():
        a, b = waiting.pop(0)
        near[(a, b)].wait_recv()
        project(chip_of(before(me, (0, 0, a, b, 0))))

    for o, copy in zip(Y_PEERS, tok_y):
        copy.wait_recv()
        near[(0, o[3])] = pass_on(r.x_all, ctx_of(before(me, o)))
        next_project()
        waiting.append((0, o[3]))
    arrived(gu_y)
    gu_x = []
    for o in X_PEERS:
        at = r.gu_all.at[:, xl, xh]
        gu_x.append(net.put(at, at, moved(me, o)))
    wdx_sems = net.take(3)

    @pl.when(xl == c)
    def _():
        at = r.wd_all.at[xh, y]
        for k, o in enumerate(Y_PEERS):
            net.copy(at, at, moved(me, o), wd_sems + k, wd_sems + k).wait_recv()
        at = r.wd_all.at[xh]
        for k, o in enumerate(X_PEERS):
            net.copy(at, at, moved(me, o), wdx_sems + k, wdx_sems + k).start()

    arrived(wo_x)
    wo_z = []
    for o in Z_PEERS:
        at = r.wo_all.at[z, :, :, :, c]
        wo_z.append(net.put(at, at, moved(me, o)))
    wo_near = [net.put(r.wo_all.at[z, :, :, :, c], r.wo_all.at[z, :, :, :, c], over)]
    for o, copy in zip(Y_PEERS, tok_xy):
        copy.wait_recv()
        key = (1, o[3])
        near[key] = pass_on(r.x_all, ctx_of(before(me, (0, 0, 1, o[3], 0))))
        next_project()
        waiting.append(key)
    next_project()
    for o, copy in zip(Z_PEERS, cot_z):
        copy.wait_recv()
        at = r.cot_all.at[before(me, o)[0], c]
        cot_near.append(net.put(at, at, over))

    def visible(q_at, k_at, q_size, k_size):
        query = q_at + lax.broadcasted_iota(jnp.int32, (1, q_size), 1)
        start = begin_of(query)
        keys = k_at + lax.broadcasted_iota(jnp.int32, (k_size, q_size), 0)
        seen = keys >= start
        if k_at + k_size > q_at:
            seen = seen & (keys <= query)
        return seen

    att_send = net.take(16)
    for i in range(8):
        q = r.q[i]
        rows = jnp.zeros((1, BLOCK), F32)
        acc = jnp.zeros((HEAD, BLOCK), F32)
        for b in range(i + 1):
            e = jnp.exp2(dot_t(r.k[b], q) * SCALE2)
            e = jnp.where(visible(i * BLOCK, b * BLOCK, BLOCK, BLOCK), e, 0.0)
            rows = rows + jnp.sum(e, 0, keepdims=True)
            acc = acc + dot(r.v_turned[b], e.astype(BF))
        norm = 1.0 / rows
        acc = acc * norm
        r.full[i] = acc
        r.norm[i] = norm
        r.att[2 * i : 2 * i + 2] = acc.T.astype(BF).reshape(2, TOK, HEAD)
        for s in range(2):
            t = 2 * i + s

            @pl.when(mine != t)
            def _():
                net.copy(
                    r.att.at[t],
                    r.att_all.at[:, columns(mine)],
                    (z, xl, i // 4, i % 4, s),
                    att_send + t,
                    att_send + mine,
                ).start()

    keep = net.local(r.att.at[mine], r.att_all.at[:, columns(mine)])
    for o, copy in zip(Z_PEERS, wo_z):
        copy.wait_recv()
        at = r.wo_all.at[before(me, o)[0], :, :, :, c]
        wo_near.append(net.put(at, at, over))
    for o in CTX_ALL:
        k = att_send + ctx_of(before(me, o))
        net.copy(r.att.at[0], r.att_all.at[:, columns(mine)], over, k, k).wait_recv()
    keep.wait()
    arrived(wo_near)

    inputs = r.tok[...].astype(F32)
    residual = inputs + dot(r.att_all[...], r.wo_all[...].reshape(QUERY_HEADS * HEAD, WIDTH))
    r.resid[...] = residual
    inverse_two = inverse_root(residual)
    r.s_all[z, c] = (residual * inverse_two * r.gain_two[...]).astype(BF)
    s_mine = r.s_all.at[z, c]
    s_near = {0: net.put(s_mine, s_mine, over)}
    s_z = [net.put(s_mine, s_mine, moved(me, o)) for o in Z_PEERS]

    arrived(gu_x + cot_near)
    at = r.wd_all.at[0]

    @pl.when(xl == c)
    def _():
        net.copy(at, at, over, wdx_sems, wdx_sems + X_PEERS.index(X_HALF)).wait_recv()

    @pl.when(xl != c)
    def _():
        for k, o in enumerate(X_PEERS):
            if o != X_HALF:
                net.copy(at, at, over, wdx_sems, wdx_sems + k).wait_recv()

    def feed_forward(n):
        w_gu = r.gu_all[...].reshape(WIDTH, 2 * SLICE)
        gu = dot(r.s_all[n].reshape(BLOCK, WIDTH), w_gu)
        grad_hidden = dot_t(r.cot_all[n].reshape(BLOCK, WIDTH), r.wd_all[...].reshape(SLICE, WIDTH))
        gate, up = gu[:, :SLICE], gu[:, SLICE:]
        sigma = 1.0 / (1.0 + jnp.exp(-gate))
        swish = gate * sigma
        r.hidden[n] = (swish * up).astype(BF)
        grad_gate = grad_hidden * up * sigma * (1.0 + gate * (1.0 - sigma))
        grad_gu = jnp.concatenate([grad_gate, grad_hidden * swish], 1).astype(BF)
        r.grad_gu[n] = grad_gu
        r.pg[n] = dot_t(grad_gu, w_gu).astype(BF).reshape(2, TOK, WIDTH)
        return net.put(r.pg.at[n, 1 - c], r.pg_got.at[n], over)

    pg_near, pg_ring, order = {}, [], []

    def mix(n, got):
        r.pg_got[n] = (r.pg[n, c].astype(F32) + r.pg_got[n].astype(F32)).astype(BF)

    def send_mixed(k):
        o = Z_PEERS[k]
        to = moved(me, o)
        pg_near[k].wait_recv()
        mix(to[0], None)
        pg_ring.append(net.put(r.pg_got.at[to[0]], r.pg_ring.at[k], to))

    s_near[0].wait_recv()
    pg_own = feed_forward(z)
    waits = dict(zip([o[0] for o in Z_PEERS], s_z))
    done = []
    for step in (1, 3, 2):
        waits[step].wait_recv()
        source = lax.rem(z + 4 - step, 4)
        at = r.s_all.at[source, c]
        net.put(at, at, over).wait_recv()
        k = [o[0] for o in Z_PEERS].index((4 - step) % 4)
        pg_near[k] = feed_forward(source)
        if done:
            send_mixed(done[-1])
        done.append(k)
    send_mixed(done[-1])
    pg_own.wait_recv()
    mix(z, None)

    s_rows = r.s_all[...].reshape(4 * BLOCK, WIDTH)
    grad_gu = r.grad_gu[...].reshape(4 * BLOCK, 2 * SLICE)
    for a in range(4):
        part = t_dot(s_rows[:, a * BLOCK : (a + 1) * BLOCK], grad_gu)
        r.dgu[a] = part.astype(BF).reshape(16, 16, 2 * SLICE)
    dgu_x = []
    for k, o in enumerate(X_PEERS):
        to = moved(me, o)
        at = r.dgu.at[:, pl.ds((to[1] * 2 + to[2]) * 4, 4)]
        dgu_x.append(net.put(at, r.dgu_x.at[k], to))
    hidden = r.hidden[...].reshape(4 * BLOCK, SLICE)
    for a in range(4):
        cols = slice(a * BLOCK, (a + 1) * BLOCK)
        part = t_dot(hidden, r.cot_all[:, :, :, cols].reshape(4 * BLOCK, BLOCK))
        r.dwd[:, :, cols] = part.astype(BF).reshape(8, 48, BLOCK)
    dwd_sems = net.take(3)
    half_at = X_PEERS.index(X_HALF)

    def dwd_copy(k):
        to = moved(me, X_PEERS[k])
        return net.copy(
            r.dwd.at[pl.ds(to[2] * 4, 4)], r.dwd_x.at[k], to, dwd_sems + k, dwd_sems + k
        )

    @pl.when(xl == c)
    def _():
        dwd_copy(half_at).start()

    @pl.when(xl != c)
    def _():
        for k in range(3):
            if k != half_at:
                dwd_copy(k).start()

    arrived(pg_ring)
    grad_second = r.pg_got[z].astype(F32)
    for k in range(3):
        grad_second = grad_second + r.pg_ring[k].astype(F32)
    residual = r.resid[...]
    inverse_two = inverse_root(residual)
    grad_resid = r.cot[...].astype(F32) + norm_back(
        residual, inverse_two, grad_second * r.gain_two[...]
    )
    r.grad_resid[...] = grad_resid
    resid_low = grad_resid.astype(BF)
    for j in range(8):
        part = dot_t(resid_low, r.wo_all[j // 2, j % 2].reshape(BLOCK, WIDTH))
        r.ga[:, j * BLOCK : (j + 1) * BLOCK] = part.astype(BF)
    gh = []
    for o in CTX_ALL:
        to = moved(me, o)
        gh.append(net.put(r.ga.at[:, columns(ctx_of(to))], r.gh_all.at[mine], to))
    keep = net.local(r.ga.at[:, columns(mine)], r.gh_all.at[mine])

    for copy in net.sent[: -len(gh)]:
        copy.wait_send()
    net.sent = net.sent[-len(gh) :]
    for j in range(8):
        part = t_dot(r.att_all[:, j * BLOCK : (j + 1) * BLOCK], resid_low)
        r.wo_all[j // 2, j % 2] = part.astype(BF).reshape(2, 4, 2, 16, WIDTH)
    dwo_near = net.put(r.wo_all.at[:, :, :, :, 1 - c], r.dwo_got, over)
    for n in range(4):
        part = dot(r.hidden[n], r.wd_all[...].reshape(SLICE, WIDTH))
        r.pg[n] = part.astype(BF).reshape(2, TOK, WIDTH)
    po_near = net.put(r.pg.at[:, 1 - c], r.po_got, over)

    arrived(gh)
    keep.wait()

    def pair(ref, n):
        return ref[2 * n : 2 * n + 2].reshape(WIDE, HEAD)

    def beside(ref, n):
        return jnp.concatenate([ref[2 * n], ref[2 * n + 1]], 1)

    swaps = {}

    def attend_back(n):
        q = pair(r.q, n)
        g = r.gh_all[4 * n : 4 * n + 4].reshape(WIDE, HEAD)
        norm = beside(r.norm, n)
        inner = jnp.sum(g.T.astype(F32) * beside(r.full, n), 0, keepdims=True)
        acc = jnp.zeros((HEAD, WIDE), F32)
        for b in range(n + 1):
            key = pair(r.k, b)
            p = jnp.exp2(dot_t(key, q) * SCALE2) * norm
            p = jnp.where(visible(n * WIDE, b * WIDE, WIDE, WIDE), p, 0.0)
            dp = dot_t(pair(r.v, b), g)
            ds = (p * (dp - inner)).astype(BF)
            dv, dk = dot(p.astype(BF), g), dot(ds, q)
            r.dv[b] = dv if n == 3 else r.dv[b] + dv
            r.dk[b] = dk if n == 3 else r.dk[b] + dk
            acc = acc + dot(beside(r.k_turned, b), ds)
        r.dq[n % 2] = (acc * SCALE).T
        r.dk[n] = r.dk[n] * SCALE
        r.swap_src[n] = jnp.where(c == 0, r.dv[n], r.dk[n]).astype(BF)
        swaps[n] = net.put(r.swap_src.at[n], r.swap_got.at[n], over)

    p_near = {}
    r.dw[...] = jnp.zeros_like(r.dw)
    r.hg[...] = jnp.zeros_like(r.hg)

    def project_back(n):
        swaps[n].wait_recv()
        for half in range(2):
            m = 2 * n + half
            rows = slice(half * BLOCK, (half + 1) * BLOCK)
            inputs = r.x_all[2 * m : 2 * m + 2].reshape(BLOCK, WIDTH).astype(F32)
            first_in = (inputs * inverse_root(inputs) * r.gain_one[...]).astype(BF)
            cosine, sine = angles(m)
            dq, q_part = head_back(r.q_un[m], r.dq[n % 2, rows], cosine, sine, r.gain_q[...])
            both = jnp.where(c == 0, r.dk[n, rows], r.dv[n, rows])
            both = both + r.swap_got[n, rows].astype(F32)
            dk, k_part = head_back(r.k_un[m], both, cosine, sine, r.gain_k[...])
            grad = jnp.concatenate([dq, jnp.where(c == 0, dk, both)], 1).astype(BF)
            r.hg[0:1] += q_part
            r.hg[1:2] += jnp.where(c == 0, k_part, 0.0)
            r.dw[...] += t_dot(grad, first_in)
            part = dot_t(grad, r.w_two[...])
            r.x_all[2 * m : 2 * m + 2] = part.astype(BF).reshape(2, TOK, WIDTH)
            p_near[m] = net.put(r.x_all.at[2 * m + 1 - c], r.s_all.at[m // 2, m % 2], over)

    p_sems = net.take(8)

    def p_copy(m):
        return net.copy(
            r.s_all.at[m // 2, m % 2],
            r.p_y.at[m // 4, y],
            (z, xl, xh, m % 4, c),
            p_sems + m,
            p_sems + (m // 4) * 4 + y,
        )

    def send_parts(n):
        for m in (2 * n, 2 * n + 1):
            p_near[m].wait_recv()
            total = r.x_all[2 * m + c].astype(F32) + r.s_all[m // 2, m % 2].astype(F32)
            r.s_all[m // 2, m % 2] = total.astype(BF)

            @pl.when(y != m % 4)
            def _():
                p_copy(m).start()

            @pl.when(y == m % 4)
            def _():
                r.p_y[m // 4, m % 4] = r.s_all[m // 2, m % 2]

    attend_back(3)
    dwo_near.wait_recv()

    @pl.loop(0, 16)
    def _(a):
        for b in range(4):
            at = (a // 4, lax.rem(a, 4) // 2, lax.rem(a, 2), b)
            total = r.wo_all[(*at, c)].astype(F32) + r.dwo_got[at].astype(F32)
            r.dwo_got[at] = total.astype(BF)

    dwo_z = []
    for k, o in enumerate(Z_PEERS):
        to = moved(me, o)
        dwo_z.append(net.put(r.dwo_got.at[to[0]], r.dwo_z.at[k], to))
    attend_back(2)
    po_near.wait_recv()

    @pl.loop(0, 4)
    def _(n):
        r.po_got[n] = (r.pg[n, c].astype(F32) + r.po_got[n].astype(F32)).astype(BF)

    po_ring = []
    for k, o in enumerate(Z_PEERS):
        to = moved(me, o)
        po_ring.append(net.put(r.po_got.at[to[0]], r.po_ring.at[k], to))
    project_back(3)
    attend_back(1)
    send_parts(3)
    project_back(2)
    attend_back(0)
    send_parts(2)
    project_back(1)
    send_parts(1)
    project_back(0)
    send_parts(0)

    r.dw_low[...] = r.dw[...].astype(BF)
    dw_dp = []
    for k, o in enumerate(DP_ALL):
        to = moved(me, o)
        dw_dp.append(net.put(r.dw_low.at[:, columns(dp_of(to))], r.dw_got.at[k], to))
    hg_ctx = [net.put(r.hg, r.hg_got.at[k], moved(me, o)) for k, o in enumerate(CTX_ALL)]

    arrived(dgu_x)

    @pl.loop(0, 4)
    def _(a):
        for b in range(4):
            total = r.dgu[a, (xl * 2 + xh) * 4 + b].astype(F32)
            for k in range(3):
                total = total + r.dgu_x[k, a, b].astype(F32)
            r.dgu_x[0, a, b] = total.astype(BF)

    dgu_y = []
    for k, o in enumerate(Y_PEERS):
        to = moved(me, o)
        dgu_y.append(net.put(r.dgu_x.at[0, :, to[3]], r.dgu_y.at[k], to))
    dwdy_sems = net.take(4)

    def dwdy_copy(k):
        to = moved(me, Y_PEERS[k])
        return net.copy(r.dwd_x.at[0, to[3]], r.dwd_y.at[k], to, dwdy_sems + k, dwdy_sems + k)

    @pl.when(xl == c)
    def _():
        for k in range(3):
            dwd_copy(k).wait_recv()
        for b in range(4):
            total = r.dwd[xh * 4 + b].astype(F32)
            for k in range(3):
                total = total + r.dwd_x[k, b].astype(F32)
            r.dwd_x[0, b] = total.astype(BF)
        for k in range(3):
            dwdy_copy(k).start()

    arrived(dwo_z)

    @pl.loop(0, 4)
    def _(a):
        for b in range(4):
            at = (a // 2, lax.rem(a, 2), b)
            total = r.dwo_got[(z, *at)].astype(F32)
            for k in range(3):
                total = total + r.dwo_z[(k, *at)].astype(F32)
            r.dwo_z[(0, *at)] = total.astype(BF)

    dwo_x = []
    for k, o in enumerate(X_PEERS):
        to = moved(me, o)
        dwo_x.append(net.put(r.dwo_z.at[0, to[1], to[2]], r.dwo_x.at[k], to))

    def wait_parts(half):
        for o in Y_PEERS:
            k = p_sems + half * 4 + before(me, o)[3]
            net.copy(r.s_all.at[0, 0], r.p_y.at[0, 0], over, k, k).wait_recv()

    def sum_parts(half):
        total = r.p_y[half, 0].astype(F32)
        for b in range(1, 4):
            total = total + r.p_y[half, b].astype(F32)
        return total

    wait_parts(1 - xh)
    r.pg_got[0] = sum_parts(1 - xh).astype(BF)
    p_x = net.put(r.pg_got.at[0], r.p_x, moved(me, X_HALF))

    arrived(hg_ctx)
    total = r.hg[...]
    for k in range(15):
        total = total + r.hg_got[k]
    r.hg_mid[...] = total
    hg_dp = [net.put(r.hg_mid, r.hg_dp.at[k], moved(me, o)) for k, o in enumerate(DP_ALL)]

    arrived(dw_dp)
    total = r.dw_low[:, columns(here)].astype(F32)
    for k in range(7):
        total = total + r.dw_got[k].astype(F32)
    r.dw_sum[...] = total.T.reshape(16, 8, 2 * HEAD)
    second_at = pl.ds(pl.multiple_of(KEY_AT + c * (VALUE_AT - KEY_AT) + chip * HEAD, HEAD), HEAD)
    dw_ctx = []
    for o in CTX_ALL:
        to = moved(me, o)
        at = r.dw_sum.at[ctx_of(to)]
        dw_ctx.append(net.put(at.at[:, :HEAD], r.dwq_out.at[:, columns(mine)], to))
        dw_ctx.append(net.put(at.at[:, HEAD:], r.dwq_out.at[:, second_at], to))
    at = r.dw_sum.at[mine]
    keeps = [
        net.local(at.at[:, :HEAD], r.dwq_out.at[:, columns(mine)]),
        net.local(at.at[:, HEAD:], r.dwq_out.at[:, second_at]),
    ]

    arrived(dgu_y)
    for a in range(4):
        total = r.dgu_x[0, a, y].astype(F32)
        for k in range(3):
            total = total + r.dgu_y[k, a].astype(F32)
        r.dgu_sum[2 * a] = total[:8]
        r.dgu_sum[2 * a + 1] = total[8:]
    up_at = pl.ds(pl.multiple_of(FF + ring * SLICE, HEAD), SLICE)
    gate_at = pl.ds(pl.multiple_of(ring * SLICE, HEAD), SLICE)
    dgu_ring = []
    for o in RING_ALL:
        to = moved(me, o)
        at = r.dgu_sum.at[ring_of(to)]
        dgu_ring.append(net.put(at.at[:, :SLICE], r.dgu_out.at[:, gate_at], to))
        dgu_ring.append(net.put(at.at[:, SLICE:], r.dgu_out.at[:, up_at], to))
    at = r.dgu_sum.at[ring]
    keeps.append(net.local(at.at[:, :SLICE], r.dgu_out.at[:, gate_at]))
    keeps.append(net.local(at.at[:, SLICE:], r.dgu_out.at[:, up_at]))

    def half_copy():
        return net.copy(r.dwd_sum.at[1 - c], r.dwd_half, over, dwdy_sems + 3, dwdy_sems + 3)

    @pl.when(xl == c)
    def _():
        for k in range(3):
            dwdy_copy(k).wait_recv()
        total = r.dwd_x[0, y].astype(F32)
        for k in range(3):
            total = total + r.dwd_y[k].astype(F32)
        r.dwd_sum[0] = total[:24]
        r.dwd_sum[1] = total[24:]
        half_copy().start()
        r.dwd_out[...] = r.dwd_sum[c]

    arrived(dwo_x)
    for b in range(4):
        total = r.dwo_z[0, xl, xh, b].astype(F32)
        for k in range(3):
            total = total + r.dwo_x[k, b].astype(F32)
        r.dwo_x[0, b] = total.astype(BF)
    dwo_y = []
    for k, o in enumerate(Y_PEERS):
        to = moved(me, o)
        dwo_y.append(net.put(r.dwo_x.at[0, to[3]], r.dwo_y.at[k], to))

    arrived(po_ring)
    total = r.resid[...] + r.po_got[z].astype(F32)
    for k in range(3):
        total = total + r.po_ring[k].astype(F32)
    r.output[...] = total

    wait_parts(xh)
    total = sum_parts(xh)
    p_x.wait_recv()
    total = total + r.p_x[...].astype(F32)
    inputs = r.tok[...].astype(F32)
    r.input_grad[...] = r.grad_resid[...] + norm_back(
        inputs, inverse_root(inputs), total * r.gain_one[...]
    )

    arrived(dwo_y)
    total = r.dwo_x[0, y].astype(F32)
    for k in range(3):
        total = total + r.dwo_y[k].astype(F32)
    r.dwo_out[...] = total

    arrived(hg_dp)
    total = r.hg_mid[...]
    for k in range(7):
        total = total + r.hg_dp[k]
    r.head_gains[...] = total

    @pl.when(xl != c)
    def _():
        half_copy().wait_recv()
        r.dwd_out[...] = r.dwd_half[...]

    for copy in keeps:
        copy.wait()
    arrived(dgu_ring)
    total = jnp.sum(r.dgu_out[...] * r.wgu[...].astype(F32), 1, keepdims=True)
    r.two_gains[...] = jnp.broadcast_to(total, (8, 128))
    arrived(dw_ctx)
    total = jnp.sum(r.dwq_out[...] * r.wqkv[...].astype(F32), 1, keepdims=True)
    r.one_gains[...] = jnp.broadcast_to(total, (8, 128))

    for o in CTX_ALL:
        t = ctx_of(moved(me, o))
        net.copy(r.att.at[t], r.att_all.at[:, columns(mine)], over, att_send + t, att_send).wait_send()
    for m in range(8):

        @pl.when(y != m % 4)
        def _():
            p_copy(m).wait_send()

    @pl.when(xl == c)
    def _():
        for k, o in enumerate(Y_PEERS):
            at = r.wd_all.at[xh, y]
            net.copy(at, at, over, wd_sems + k, wd_sems + k).wait_send()
        for k, o in enumerate(X_PEERS):
            at = r.wd_all.at[xh]
            net.copy(at, at, over, wdx_sems + k, wdx_sems + k).wait_send()
        dwd_copy(half_at).wait_send()
        for k in range(3):
            dwdy_copy(k).wait_send()
        half_copy().wait_send()

    @pl.when(xl != c)
    def _():
        for k in range(3):
            if k != half_at:
                dwd_copy(k).wait_send()

    net.drain()


def on_device(
    tokens, lengths, attn_gain, q_gain, k_gain, qkv, w_out, mlp_gain, w_gate_up, w_down, cotangent
):
    device = lax.axis_index(AXES)
    gains = jnp.concatenate([attn_gain, mlp_gain, q_gain, k_gain]).astype(F32)
    gains = jnp.broadcast_to(jnp.pad(gains, (0, 128 - 18))[None], (8, 128))
    half = np.arange(HEAD // 2, dtype=np.float32) * np.float32(2.0 / HEAD)
    freq = np.float32(THETA) ** (-half)
    freq = jnp.asarray(np.concatenate([freq, freq])[None].astype(np.float32))
    vmem = pl.BlockSpec(memory_space=pltpu.VMEM)
    outs = pl.pallas_call(
        body,
        name="layer",
        out_shape=tuple(jax.ShapeDtypeStruct(s, d) for s, d in OUTPUTS.values()),
        in_specs=[vmem] * 8 + [pl.BlockSpec(memory_space=pltpu.SMEM)],
        out_specs=(vmem,) * len(OUTPUTS),
        scratch_shapes=[pltpu.VMEM(s, d) for s, d in BUFFERS.values()]
        + [pltpu.SemaphoreType.DMA((SEMS,))] * 2,
        compiler_params=pltpu.CompilerParams(
            collective_id=1, has_side_effects=True, vmem_limit_bytes=VMEM_LIMIT
        ),
    )(tokens, qkv, w_out, w_gate_up, w_down, cotangent, gains, freq, lengths)
    o = dict(zip(OUTPUTS, outs))
    heads = lax.dynamic_slice_in_dim(o["head_gains"], device, 1, 1)
    return (
        o["output"],
        o["input_grad"],
        o["one_gains"][:, 0] / attn_gain.astype(F32),
        heads[0],
        heads[1],
        o["dwq_out"],
        o["dwo_out"],
        o["two_gains"][:, 0] / mlp_gain.astype(F32),
        o["dgu_out"],
        o["dwd_out"],
    )


def solution(mesh):
    torus = Mesh(mesh.devices.reshape(SIZES), AXES)
    rows, line = P(AXES, None), P(AXES)
    return jax.shard_map(
        on_device,
        mesh=torus,
        in_specs=(rows, P(DP, None), line, line, line, rows, rows, line, rows, rows, rows),
        out_specs=(rows, rows, line, line, line, rows, rows, line, rows, rows),
        check_vma=False,
    )
```

```python
import math
import types

import jax
import jax.numpy as jnp
import numpy as np
from jax import lax
from jax.experimental import pallas as pl
from jax.experimental.pallas import tpu as pltpu
from jax.sharding import Mesh
from jax.sharding import PartitionSpec as P

QUERY_HEADS = 16
KEY_VALUE_HEADS = 8
HEAD = 128
WIDTH = 1024
FF = 3072
TOK = 128
GROUP = 2048
BLOCK = 256
WIDE = 512
SLICE = FF // 8
CUT = 640
EPS = 1e-06
THETA = 1000000.0
SCALE = 1.0 / math.sqrt(HEAD)
SCALE2 = SCALE / math.log(2.0)
KEY_AT = QUERY_HEADS * HEAD
VALUE_AT = KEY_AT + KEY_VALUE_HEADS * HEAD

AXES = ("z", "xl", "xh", "y", "c")
SIZES = (4, 2, 2, 4, 2)
DP = ("z", "xl")
BF = jnp.bfloat16
F32 = jnp.float32
BY_MESH = pl.DeviceIdType.MESH
MIB = 2**20


def offsets(*axes):
    out = [()]
    for size, name in zip(SIZES, AXES):
        out = [o + (k,) for o in out for k in (range(size) if name in axes else (0,))]
    return out[1:]


SIBLING = (0, 0, 0, 0, 1)
CTX = offsets("xh", "y")
DP_ALL = offsets("z", "xl")
X_PEERS = offsets("xl", "xh")
X_HALF = (0, 0, 1, 0, 0)
X_LOW = (0, 1, 0, 0, 0)
Y_PEERS = [(0, 0, 0, k, 0) for k in (1, 3, 2)]
Z_PEERS = [(k, 0, 0, 0, 0) for k in (1, 3, 2)]
PEERS = sorted(set(CTX + DP_ALL + X_PEERS + [SIBLING]))


def moved(me, offset):
    return tuple(lax.rem(m + o, s) if o else m for m, o, s in zip(me, offset, SIZES))


def before(me, offset):
    return tuple(lax.rem(m + s - o, s) if o else m for m, o, s in zip(me, offset, SIZES))


def ctx_of(at):
    return at[2] * 8 + at[3] * 2 + at[4]


def dp_of(at):
    return at[0] * 2 + at[1]


def chip_of(at):
    return at[2] * 4 + at[3]


def columns(k, width=HEAD):
    return pl.ds(pl.multiple_of(k * width, width), width)


class Net:
    def __init__(self, send, recv):
        self.send, self.recv, self.count, self.sent = send, recv, 0, []

    def take(self, n=1):
        k = self.count
        self.count += n
        return k

    def copy(self, src, dst, device, send, recv):
        return pltpu.make_async_remote_copy(
            src_ref=src,
            dst_ref=dst,
            send_sem=self.send.at[send],
            recv_sem=self.recv.at[recv],
            device_id=device,
            device_id_type=BY_MESH,
        )

    def put(self, src, dst, device):
        k = self.take()
        copy = self.copy(src, dst, device, k, k)
        copy.start()
        self.sent.append(copy)
        return copy

    def put_all(self, triples, total):
        k = self.take()
        for src, dst, device in triples:
            self.copy(src, dst, device, k, k).start()
        group = self.copy(total, total, triples[0][2], k, k)
        self.sent.append(group)
        return group

    def local(self, src, dst):
        copy = pltpu.make_async_copy(src, dst, self.send.at[self.take()])
        copy.start()
        return copy

    def drain(self):
        for copy in self.sent:
            copy.wait_send()
        self.sent = []


def arrived(copies):
    for copy in copies:
        copy.wait_recv()


def dot(a, b):
    return jnp.dot(a, b, preferred_element_type=F32)


def dot_t(a, b):
    return lax.dot_general(a, b, (((1,), (1,)), ((), ())), preferred_element_type=F32)


def t_dot(a, b):
    return lax.dot_general(a, b, (((0,), (0,)), ((), ())), preferred_element_type=F32)


def turned(v):
    return pltpu.roll(v, HEAD // 2, 1)


def inverse_root(v):
    return lax.rsqrt(jnp.mean(v * v, -1, keepdims=True) + EPS)


def head_back(unnormed, grad, cosine, sine, gain):
    inverse = inverse_root(unnormed)
    hat = unnormed * inverse
    back = grad * cosine - turned(grad) * sine
    g = back * gain
    raw = inverse * (g - hat * jnp.mean(g * hat, -1, keepdims=True))
    return raw, jnp.sum(back * hat, 0, keepdims=True)


def norm_back(values, inverse, grad):
    cubed = inverse * inverse * inverse
    return inverse * grad - values * cubed * jnp.mean(grad * values, -1, keepdims=True)


BUFFERS = dict(
    tok=((TOK, WIDTH), BF),
    wqkv=((8, VALUE_AT + KEY_VALUE_HEADS * HEAD), BF),
    wgu=((8, 2 * FF), BF),
    wd=((24, WIDTH), BF),
    gains=((8, 128), F32),
    freq=((1, HEAD), F32),
    gains_out=((8, 128), F32),
    dwq_out=((8, VALUE_AT + KEY_VALUE_HEADS * HEAD), F32),
    dwo_out=((16, WIDTH), F32),
    dgu_out=((8, 2 * FF), F32),
    dwd_out=((24, WIDTH), F32),
    wq_src=((8, 2, 8, 2 * HEAD), F32),
    wq_pair=((8, 2, 8, 2 * HEAD), F32),
    wq_tmp=((8, 2, 8, 2 * HEAD), F32),
    w_low=((TOK, 2 * HEAD), BF),
    w_got=((8, TOK, HEAD), BF),
    w_all=((8, TOK, 2 * HEAD), BF),
    g_pair=((2, 8, 128), F32),
    g_tmp=((8, 2, 8, 128), F32),
    g_row=((16, 128), F32),
    g_all=((8, 16, 128), F32),
    gain_one=((1, WIDTH), F32),
    gain_two=((1, WIDTH), F32),
    gain_q=((1, HEAD), F32),
    gain_k=((1, HEAD), F32),
    gu_src=((4, 2, 8, 2 * SLICE), F32),
    gu_pair=((4, 2, 8, 2 * SLICE), F32),
    gu_tmp=((4, 2, 8, 2 * SLICE), F32),
    gu_low=((4, 16, 2 * SLICE), BF),
    gu_all=((4, 2, 2, 4, 16, 2 * SLICE), BF),
    wd_src=((24, WIDTH), F32),
    wd_tmp=((2, 24, WIDTH), F32),
    wd_all=((2, 4, 48, WIDTH), BF),
    wo_all=((4, 2, 2, 4, 2, 16, WIDTH), BF),
    cot_all=((4, 2, TOK, WIDTH), BF),
    x_all=((16, TOK, WIDTH), BF),
    angle=((8, BLOCK, HEAD), F32),
    q=((8, BLOCK, HEAD), BF),
    k=((8, BLOCK, HEAD), BF),
    v=((8, BLOCK, HEAD), BF),
    k_turned=((8, HEAD, BLOCK), BF),
    v_turned=((8, HEAD, BLOCK), BF),
    q_un=((8, BLOCK, HEAD), F32),
    k_un=((8, BLOCK, HEAD), F32),
    full=((8, HEAD, BLOCK), F32),
    norm=((8, 1, BLOCK), F32),
    att=((8, 2, TOK, HEAD), BF),
    att_pair=((8, TOK, 2 * HEAD), BF),
    att_all=((TOK, QUERY_HEADS * HEAD), BF),
    resid=((TOK, WIDTH), F32),
    s_all=((4, 2, TOK, WIDTH), BF),
    hidden=((4, BLOCK, SLICE), BF),
    grad_gu=((4, BLOCK, 2 * SLICE), BF),
    pg=((4, 2, TOK, WIDTH), BF),
    pg_got=((4, TOK, WIDTH), BF),
    pg_ring=((3, TOK, WIDTH), BF),
    po_got=((4, TOK, WIDTH), BF),
    po_ring=((3, TOK, WIDTH), BF),
    dgu=((4, 4, 4, 16, 2 * SLICE), BF),
    dgu_x=((3, 4, 4, 16, SLICE), BF),
    dgu_y=((3, 4, 16, SLICE), BF),
    dgv_y=((3, 4, 4, 16, SLICE), BF),
    dgv_x=((3, 4, 16, SLICE), BF),
    dgu_sum=((4, 2, 8, 2 * SLICE), F32),
    dgu_pair=((4, 2, 8, 2 * SLICE), F32),
    dgu_got=((4, 2, 8, 2 * SLICE), F32),
    dwd=((8, 48, WIDTH), BF),
    dwd_x=((3, 4, 48, WIDTH), BF),
    dwd_y=((3, 48, WIDTH), BF),
    dwd_sum=((2, 24, WIDTH), F32),
    dwd_half=((24, WIDTH), F32),
    dwo_got=((4, 2, 2, 4, 16, WIDTH), BF),
    dwo_z=((3, 2, 2, 4, 16, CUT), BF),
    dwo_y=((3, 2, 2, 16, CUT), BF),
    dwo_x=((3, 16, CUT), BF),
    dwp_y=((3, 4, 2, 2, 16, WIDTH - CUT), BF),
    dwp_z=((3, 2, 2, 16, WIDTH - CUT), BF),
    dwp_x=((3, 16, WIDTH - CUT), BF),
    grad_resid=((TOK, WIDTH), F32),
    gh_pair=((8, TOK, 2 * HEAD), BF),
    gh_all=((8, 2, TOK, HEAD), BF),
    dk=((4, WIDE, HEAD), F32),
    dv=((4, WIDE, HEAD), F32),
    swap_got=((4, 2, 2, TOK, HEAD), BF),
    dq=((2, WIDE, HEAD), F32),
    p_x=((TOK, WIDTH // 2), BF),
    p_x_src=((TOK, WIDTH // 2), BF),
    dw=((2 * HEAD, WIDTH), F32),
    dw_low=((2 * HEAD, WIDTH), BF),
    dw_got=((3, 2 * HEAD, 2 * TOK), BF),
    dw_mid=((2, 2 * HEAD, TOK), BF),
    dw_xl=((2 * HEAD, TOK), BF),
    dw_sum=((8, 2, 8, 2 * HEAD), F32),
    dw_pair=((8, 2, 8, 2 * HEAD), F32),
    dw_rows=((8, 2, 8, 2 * HEAD), F32),
    hg=((8, 128), F32),
    hg_near=((8, 128), F32),
    hg_two=((8, 128), F32),
    hg_got=((7, 8, 128), F32),
    hg_mid=((8, 128), F32),
    hg_dp=((7, 8, 128), F32),
)
INPUTS = ("tok_in", "wqkv_in", "wo_in", "wgu_in", "wd_in", "cot_in", "gains_in", "freq_in", "lengths")
OUTPUTS = dict(
    output=((TOK, WIDTH), F32),
    input_grad=((TOK, WIDTH), F32),
    gain_grads=((8, 128), F32),
    grad_qkv=((8, VALUE_AT + KEY_VALUE_HEADS * HEAD), F32),
    grad_out=((16, WIDTH), F32),
    grad_up=((8, 2 * FF), F32),
    grad_down=((24, WIDTH), F32),
)
SEMS = 180
VMEM_LIMIT = 60 * MIB


def body(*refs):
    names = list(INPUTS) + list(OUTPUTS) + list(BUFFERS) + ["send", "recv"]
    r = types.SimpleNamespace(**dict(zip(names, refs, strict=True)))
    me = tuple(lax.axis_index(a) for a in AXES)
    z, xl, xh, y, c = me
    chip = xh * 4 + y
    mine, here = ctx_of(me), dp_of(me)
    over = moved(me, SIBLING)
    net = Net(r.send, r.recv)

    own_wo = (z, xl, xh, y, c)
    loads = [
        net.local(r.wqkv_in, r.wqkv),
        net.local(r.gains_in, r.gains),
        net.local(r.wgu_in, r.wgu),
        net.local(r.wd_in, r.wd),
        net.local(r.tok_in, r.tok),
        net.local(r.wo_in, r.wo_all.at[own_wo]),
        net.local(r.freq_in, r.freq),
        net.local(r.cot_in, r.cot_all.at[z, c]),
    ]
    barrier = pltpu.get_barrier_semaphore()
    for o in PEERS:
        pl.semaphore_signal(barrier, inc=1, device_id=moved(me, o), device_id_type=BY_MESH)
    for copy in loads:
        copy.wait()

    w = r.wqkv[...].astype(F32)
    for j in range(16):
        extra = (KEY_AT, VALUE_AT)[j % 2] + j // 2 * HEAD
        r.wq_src[j // 2, j % 2, :, :HEAD] = w[:, j * HEAD : (j + 1) * HEAD]
        r.wq_src[j // 2, j % 2, :, HEAD:] = w[:, extra : extra + HEAD]
    w = r.wgu[...].astype(F32)
    for j in range(8):
        r.gu_src[j // 2, j % 2, :, :SLICE] = w[:, j * SLICE : (j + 1) * SLICE]
        r.gu_src[j // 2, j % 2, :, SLICE:] = w[:, FF + j * SLICE : FF + (j + 1) * SLICE]
    r.wd_src[...] = r.wd[...].astype(F32)
    r.wq_pair[:, c] = r.wq_src[:, c]
    r.gu_pair[:, c] = r.gu_src[:, c]
    r.g_pair[c] = r.gains[...]
    r.wd_tmp[c] = r.wd_src[...]
    r.x_all[mine] = r.tok[...]
    pl.semaphore_wait(barrier, len(PEERS))

    small = [
        net.put(r.wq_src.at[:, 1 - c], r.wq_pair.at[:, c], over),
        net.put(r.gains, r.g_pair.at[c], over),
        net.put(r.gu_src.at[:, 1 - c], r.gu_pair.at[:, c], over),
        net.put(r.wd_src, r.wd_tmp.at[c], over),
    ]
    tok_x = net.put(r.tok, r.x_all.at[mine], moved(me, X_HALF))
    tok_y = [net.put(r.tok, r.x_all.at[mine], moved(me, o)) for o in Y_PEERS]
    wo_own = r.wo_all.at[own_wo]
    wo_x = net.put_all(
        [(wo_own, wo_own, moved(me, o)) for o in X_PEERS], r.wo_all.at[0, 0, 0, pl.ds(0, 3), 0]
    )
    tok_own = net.put(r.tok, r.x_all.at[mine], over)
    at = r.cot_all.at[z, c]
    cot_near = [net.put(at, at, over)]
    arrived(small)
    w_ctx = net.put_all(
        [(r.wq_pair.at[chip_of(to)], r.wq_tmp.at[chip], to) for to in (moved(me, o) for o in CTX)],
        r.wq_tmp.at[pl.ds(0, 7)],
    )
    g_ctx = net.put_all(
        [(r.g_pair, r.g_tmp.at[chip], moved(me, o)) for o in CTX], r.g_tmp.at[pl.ds(0, 7)]
    )
    gu_z = net.put_all(
        [(r.gu_pair.at[to[0]], r.gu_tmp.at[z], to) for to in (moved(me, o) for o in Z_PEERS)],
        r.gu_tmp.at[pl.ds(0, 3)],
    )
    r.wq_tmp[chip] = r.wq_pair[chip]
    r.g_tmp[chip] = r.g_pair[...]
    r.gu_tmp[z] = r.gu_pair[z]
    wd_sems = net.take(3)

    @pl.when(xl == c)
    def _():
        r.wd_all[xh, y] = r.wd_tmp[...].reshape(48, WIDTH).astype(BF)
        for k, o in enumerate(Y_PEERS):
            at = r.wd_all.at[xh, y]
            net.copy(at, at, moved(me, o), wd_sems + k, wd_sems + k).start()

    ends, starts = [], []
    total = 0
    for d in range(8):
        starts.append(total)
        total = total + r.lengths[0, d]

    def begin_of(index):
        out = jnp.zeros_like(index)
        for s in starts[1:]:
            out = jnp.where(index >= s, s, out)
        return out

    low = lax.broadcasted_iota(jnp.int32, (BLOCK, HEAD), 1) < HEAD // 2
    shift = jnp.where(low, 0.0, 0.5 * math.pi)

    @pl.loop(0, 8)
    def _(n):
        index = n * BLOCK + lax.broadcasted_iota(jnp.int32, (BLOCK, HEAD), 0)
        phase = (index - begin_of(index)).astype(F32) * r.freq[...]
        r.angle[n] = jnp.cos(phase - shift)

    def angles(n):
        both = r.angle[n]
        other = turned(both)
        return jnp.where(low, both, other), jnp.where(low, -other, both)

    w_ctx.wait_recv()
    r.w_low[...] = r.wq_tmp[...].reshape(TOK, 2 * HEAD).astype(BF)
    w_xl = net.put(r.w_low, r.w_all.at[here], moved(me, X_LOW))
    g_ctx.wait_recv()
    r.g_row[...] = r.g_tmp[:, :, 0, :].reshape(16, 128)
    g_dp = net.put_all(
        [(r.g_row, r.g_all.at[here], moved(me, o)) for o in DP_ALL], r.g_all.at[pl.ds(0, 7)]
    )
    r.w_all[here] = r.w_low[...]
    r.g_all[here] = r.g_row[...]

    def pass_on(ref, at):
        return net.put(ref.at[at], ref.at[at], over)

    def same(ref, peers, total):
        return net.put_all([(ref, ref, moved(me, o)) for o in peers], total)

    left, right = slice(0, SLICE), slice(SLICE, 2 * SLICE)
    wo_x.wait_recv()
    wo_y = same(r.wo_all.at[z, :, :, y, c], Y_PEERS, r.wo_all.at[pl.ds(0, 3), :, :, 0, 0])
    gu_z.wait_recv()
    r.gu_low[...] = r.gu_tmp[...].reshape(4, 16, 2 * SLICE).astype(BF)
    r.gu_all[:, xl, xh, y] = r.gu_low[...]
    gu_y = net.put_all(
        [
            (r.gu_low.at[:, :, left], r.gu_all.at[:, xl, xh, y, :, left], moved(me, o))
            for o in Y_PEERS
        ],
        r.gu_all.at[:, 0, 0, pl.ds(0, 3), :, left],
    )
    gu_x = net.put_all(
        [
            (r.gu_low.at[:, :, right], r.gu_all.at[:, xl, xh, y, :, right], moved(me, o))
            for o in X_PEERS
        ],
        r.gu_all.at[:, 0, 0, pl.ds(0, 3), :, right],
    )

    first, last = slice(0, WIDTH // 2), slice(WIDTH // 2, WIDTH)
    w_xl.wait_recv()
    w_z = same(r.w_all.at[pl.ds(2 * z, 2)], Z_PEERS, r.w_all.at[pl.ds(0, 6)])
    tok_x.wait_recv()
    at_x = ctx_of(before(me, X_HALF))
    near = {(1, 0): pass_on(r.x_all, at_x)}
    at = r.x_all.at[at_x, :, first]
    tok_xy = [net.put(at, at, moved(me, o)) for o in Y_PEERS]
    tok_yx = []
    for o, copy in zip(Y_PEERS, tok_y):
        copy.wait_recv()
        source = ctx_of(before(me, o))
        at = r.x_all.at[source, :, last]
        tok_yx.append(net.put(at, at, moved(me, X_HALF)))
        near[(0, o[3])] = pass_on(r.x_all, source)
    wo_y.wait_recv()
    at = r.wo_all.at[z, :, :, :, c]
    wo_z = [net.put(at, at, moved(me, o)) for o in Z_PEERS[:2]]
    wo_near = [net.put(at, at, over)]
    gu_y.wait_recv()
    gu_x.wait_recv()
    gu_yx = same(r.gu_all.at[:, xl, xh, :, :, left], X_PEERS, r.gu_all.at[pl.ds(0, 3), :, :, :, :, left])
    gu_xy = same(r.gu_all.at[:, :, :, y, :, right], Y_PEERS, r.gu_all.at[pl.ds(0, 3), :, :, :, :, right])
    wdx_sems = net.take(3)

    @pl.when(xl == c)
    def _():
        at = r.wd_all.at[xh, y]
        for k, o in enumerate(Y_PEERS):
            net.copy(at, at, moved(me, o), wd_sems + k, wd_sems + k).wait_recv()
        at = r.wd_all.at[xh]
        for k, o in enumerate(X_PEERS):
            net.copy(at, at, moved(me, o), wdx_sems + k, wdx_sems + k).start()

    at = r.cot_all.at[z, c]
    cot_z = [net.put(at, at, moved(me, o)) for o in Z_PEERS[:2]]

    w_z.wait_recv()
    w_near = net.put(r.w_all.at[:, :, HEAD:], r.w_got, over)
    g_dp.wait_recv()
    gains = r.g_all[...].reshape(128, 128).astype(BF)
    dev = lax.broadcasted_iota(jnp.int32, (128, WIDTH), 0)
    lane = lax.broadcasted_iota(jnp.int32, (128, WIDTH), 1)
    spread = t_dot(gains, (lane // 8 == dev).astype(F32).astype(BF))
    pick = lax.broadcasted_iota(jnp.int32, (8, WIDTH), 1) % 8 == lax.broadcasted_iota(
        jnp.int32, (8, WIDTH), 0
    )
    r.gain_one[...] = jnp.sum(jnp.where(pick, spread[:8], 0.0), 0, keepdims=True)
    r.gain_two[...] = jnp.sum(jnp.where(pick, spread[8:16], 0.0), 0, keepdims=True)
    eye = lax.broadcasted_iota(jnp.int32, (128, 128), 0) == lax.broadcasted_iota(
        jnp.int32, (128, 128), 1
    )
    spread = t_dot(gains, eye.astype(F32).astype(BF))
    r.gain_q[...] = spread[16:17]
    r.gain_k[...] = spread[17:18]
    w_near.wait_recv()

    def project(n):
        inputs = r.x_all[pl.ds(2 * n, 2)].reshape(BLOCK, WIDTH).astype(F32)
        first_in = (inputs * inverse_root(inputs) * r.gain_one[...]).astype(BF)
        projected = dot(first_in, r.w_all[...].reshape(WIDTH, 2 * HEAD))
        second = dot(first_in, r.w_got[...].reshape(WIDTH, HEAD))
        q_un, own = projected[:, :HEAD], projected[:, HEAD:]
        k_un = jnp.where(c == 0, own, second)
        value = jnp.where(c == 0, second, own)
        r.v[n] = value.astype(BF)
        r.v_turned[n] = value.T.astype(BF)
        r.q_un[n] = q_un
        r.k_un[n] = k_un
        cosine, sine = angles(n)
        q = q_un * inverse_root(q_un) * r.gain_q[...]
        r.q[n] = (q * cosine + turned(q) * sine).astype(BF)
        key = k_un * inverse_root(k_un) * r.gain_k[...]
        key = key * cosine + turned(key) * sine
        r.k[n] = key.astype(BF)
        r.k_turned[n] = key.T.astype(BF)

    tok_own.wait_recv()
    project(chip)
    waiting = [(1, 0)]

    def next_project():
        a, b = waiting.pop(0)
        near[(a, b)].wait_recv()
        project(chip_of(before(me, (0, 0, a, b, 0))))

    for o in Y_PEERS:
        next_project()
        waiting.append((0, o[3]))
    for o, one, two in zip(Y_PEERS, tok_xy, tok_yx):
        one.wait_recv()
        two.wait_recv()
        key = (1, o[3])
        near[key] = pass_on(r.x_all, ctx_of(before(me, (0, 0, 1, o[3], 0))))
        next_project()
        waiting.append(key)
    next_project()
    wo_far, cot_far = [], []
    for k in range(2):
        wo_z[k].wait_recv()
        source = before(me, Z_PEERS[k])[0]
        at = r.wo_all.at[source, :, :, :, c, :, (first, last)[k]]
        wo_far.append(net.put(at, at, moved(me, Z_PEERS[k])))
        at = r.wo_all.at[source, :, :, :, c]
        wo_near.append(net.put(at, at, over))

    def visible(q_at, k_at, q_size, k_size):
        query = q_at + lax.broadcasted_iota(jnp.int32, (1, q_size), 1)
        start = begin_of(query)
        keys = k_at + lax.broadcasted_iota(jnp.int32, (k_size, q_size), 0)
        seen = keys >= start
        if k_at + k_size > q_at:
            seen = seen & (keys <= query)
        return seen

    att_send = net.take(8)
    att_near = []

    def att_copy(i):
        return net.copy(
            r.att_pair.at[i],
            r.att_all.at[:, columns(chip, 2 * HEAD)],
            (z, xl, i // 4, i % 4, c),
            att_send + i,
            att_send + chip,
        )

    def send_pair(i):
        for copy in att_near[i]:
            copy.wait_recv() if copy is att_near[i][0] else copy.wait()

        @pl.when(chip != i)
        def _():
            att_copy(i).start()

    for i in range(8):
        q = r.q[i]
        rows = jnp.zeros((1, BLOCK), F32)
        acc = jnp.zeros((HEAD, BLOCK), F32)
        for b in range(i + 1):
            e = jnp.exp2(dot_t(r.k[b], q) * SCALE2)
            e = jnp.where(visible(i * BLOCK, b * BLOCK, BLOCK, BLOCK), e, 0.0)
            rows = rows + jnp.sum(e, 0, keepdims=True)
            acc = acc + dot(r.v_turned[b], e.astype(BF))
        norm = 1.0 / rows
        acc = acc * norm
        r.full[i] = acc
        r.norm[i] = norm
        r.att[i] = acc.T.astype(BF).reshape(2, TOK, HEAD)
        att_near.append(
            (
                net.put(r.att.at[i, 1 - c], r.att_pair.at[i, :, columns(c)], over),
                net.local(r.att.at[i, c], r.att_pair.at[i, :, columns(c)]),
            )
        )
        if i:
            send_pair(i - 1)
    send_pair(7)
    keep = net.local(r.att_pair.at[chip], r.att_all.at[:, columns(chip, 2 * HEAD)])
    far = lax.rem(z + 2, 4)
    arrived(wo_far)
    at = r.wo_all.at[far, :, :, :, c]
    wo_near.append(net.put(at, at, over))
    for k in range(2):
        cot_z[k].wait_recv()
        source = before(me, Z_PEERS[k])[0]
        at = r.cot_all.at[source, c, :, (first, last)[k]]
        cot_far.append(net.put(at, at, moved(me, Z_PEERS[k])))
        cot_near.append(pass_on(r.cot_all, (source, c)))
    for o in CTX:
        k = att_send + chip_of(before(me, o))
        net.copy(r.att_pair.at[0], r.att_pair.at[0], over, k, k).wait_recv()
    keep.wait()
    arrived(wo_near)

    inputs = r.tok[...].astype(F32)
    residual = inputs + dot(r.att_all[...], r.wo_all[...].reshape(QUERY_HEADS * HEAD, WIDTH))
    r.resid[...] = residual
    inverse_two = inverse_root(residual)
    r.s_all[z, c] = (residual * inverse_two * r.gain_two[...]).astype(BF)
    s_mine = r.s_all.at[z, c]
    s_near = {0: net.put(s_mine, s_mine, over)}
    s_z = [net.put(s_mine, s_mine, moved(me, o)) for o in Z_PEERS[:2]]

    arrived(cot_far)
    cot_near.append(pass_on(r.cot_all, (far, c)))
    arrived([gu_yx, gu_xy] + cot_near)
    at = r.wd_all.at[0]

    @pl.when(xl == c)
    def _():
        net.copy(at, at, over, wdx_sems, wdx_sems + X_PEERS.index(X_HALF)).wait_recv()

    @pl.when(xl != c)
    def _():
        for k, o in enumerate(X_PEERS):
            if o != X_HALF:
                net.copy(at, at, over, wdx_sems, wdx_sems + k).wait_recv()

    def feed_forward(n):
        w_gu = r.gu_all[...].reshape(WIDTH, 2 * SLICE)
        gu = dot(r.s_all[n].reshape(BLOCK, WIDTH), w_gu)
        grad_hidden = dot_t(r.cot_all[n].reshape(BLOCK, WIDTH), r.wd_all[...].reshape(SLICE, WIDTH))
        gate, up = gu[:, :SLICE], gu[:, SLICE:]
        sigma = 1.0 / (1.0 + jnp.exp(-gate))
        swish = gate * sigma
        r.hidden[n] = (swish * up).astype(BF)
        grad_gate = grad_hidden * up * sigma * (1.0 + gate * (1.0 - sigma))
        grad_gu = jnp.concatenate([grad_gate, grad_hidden * swish], 1).astype(BF)
        r.grad_gu[n] = grad_gu
        r.pg[n] = dot_t(grad_gu, w_gu).astype(BF).reshape(2, TOK, WIDTH)
        return net.put(r.pg.at[n, 1 - c], r.pg_got.at[n], over)

    pg_near, pg_ring = {}, []

    def mix(n, got):
        r.pg_got[n] = (r.pg[n, c].astype(F32) + r.pg_got[n].astype(F32)).astype(BF)

    def send_mixed(k):
        o = Z_PEERS[k]
        to = moved(me, o)
        pg_near[k].wait_recv()
        mix(to[0], None)
        pg_ring.append(net.put(r.pg_got.at[to[0]], r.pg_ring.at[k], to))

    s_near[0].wait_recv()
    pg_own = feed_forward(z)
    s_far = []
    for k in range(2):
        s_z[k].wait_recv()
        source = before(me, Z_PEERS[k])[0]
        s_near[k + 1] = pass_on(r.s_all, (source, c))
        at = r.s_all.at[source, c, :, (first, last)[k]]
        s_far.append(net.put(at, at, moved(me, Z_PEERS[k])))
    for k in range(2):
        s_near[k + 1].wait_recv()
        pg_near[1 - k] = feed_forward(before(me, Z_PEERS[k])[0])
        if k:
            send_mixed(1)
    arrived(s_far)
    s_near[3] = pass_on(r.s_all, (far, c))
    send_mixed(0)
    s_near[3].wait_recv()
    pg_near[2] = feed_forward(far)
    done = [2]
    send_mixed(done[-1])
    pg_own.wait_recv()
    mix(z, None)

    s_rows = r.s_all[...].reshape(4 * BLOCK, WIDTH)
    grad_gu = r.grad_gu[...].reshape(4 * BLOCK, 2 * SLICE)
    for a in range(4):
        part = t_dot(s_rows[:, a * BLOCK : (a + 1) * BLOCK], grad_gu)
        r.dgu[a] = part.astype(BF).reshape(4, 4, 16, 2 * SLICE)

    def scattered(peers, source, out):
        to = [moved(me, o) for o in peers]
        return net.put_all([(source(t), out.at[k], t) for k, t in enumerate(to)], out)

    dgu_one = scattered(X_PEERS, lambda to: r.dgu.at[:, to[1] * 2 + to[2], :, :, left], r.dgu_x)
    dgu_two = scattered(Y_PEERS, lambda to: r.dgu.at[:, :, to[3], :, right], r.dgv_y)
    hidden = r.hidden[...].reshape(4 * BLOCK, SLICE)
    for a in range(4):
        cols = slice(a * BLOCK, (a + 1) * BLOCK)
        part = t_dot(hidden, r.cot_all[:, :, :, cols].reshape(4 * BLOCK, BLOCK))
        r.dwd[:, :, cols] = part.astype(BF).reshape(8, 48, BLOCK)
    dwd_sems = net.take(3)
    half_at = X_PEERS.index(X_HALF)

    def dwd_copy(k):
        to = moved(me, X_PEERS[k])
        return net.copy(
            r.dwd.at[pl.ds(to[2] * 4, 4)], r.dwd_x.at[k], to, dwd_sems + k, dwd_sems + k
        )

    @pl.when(xl == c)
    def _():
        dwd_copy(half_at).start()

    @pl.when(xl != c)
    def _():
        for k in range(3):
            if k != half_at:
                dwd_copy(k).start()

    for copy in [pg_own, *pg_near.values()]:
        copy.wait_send()
    gone = [pg_own, *pg_near.values()]
    net.sent = [copy for copy in net.sent if all(copy is not g for g in gone)]
    for n in range(4):
        part = dot(r.hidden[n], r.wd_all[...].reshape(SLICE, WIDTH))
        r.pg[n] = part.astype(BF).reshape(2, TOK, WIDTH)
    po_near = net.put(r.pg.at[:, 1 - c], r.po_got, over)

    arrived(pg_ring)
    grad_second = r.pg_got[z].astype(F32)
    for k in range(3):
        grad_second = grad_second + r.pg_ring[k].astype(F32)
    residual = r.resid[...]
    inverse_two = inverse_root(residual)
    grad_resid = r.cot_all[z, c].astype(F32) + norm_back(
        residual, inverse_two, grad_second * r.gain_two[...]
    )
    r.grad_resid[...] = grad_resid
    resid_low = grad_resid.astype(BF)
    for i in range(8):

        @pl.when(chip != i)
        def _():
            att_copy(i).wait_send()

    for j in range(8):
        part = dot_t(resid_low, r.wo_all[j // 2, j % 2].reshape(BLOCK, WIDTH))
        r.att_pair[j] = part.astype(BF)
    net.drain()
    gh = net.put_all(
        [
            (r.att_pair.at[chip_of(to)], r.gh_pair.at[chip], to)
            for to in (moved(me, o) for o in CTX)
        ],
        r.gh_pair.at[pl.ds(0, 7)],
    )
    keep = net.local(r.att_pair.at[chip], r.gh_pair.at[chip])

    for j in range(8):
        part = t_dot(r.att_all[:, j * BLOCK : (j + 1) * BLOCK], resid_low)
        r.wo_all[j // 2, j % 2] = part.astype(BF).reshape(2, 4, 2, 16, WIDTH)
    dwo_near = net.put(r.wo_all.at[:, :, :, :, 1 - c], r.dwo_got, over)
    po_near.wait_recv()

    @pl.loop(0, 4)
    def _(n):
        r.po_got[n] = r.pg[n, c] + r.po_got[n]

    po_ring = scattered(Z_PEERS, lambda to: r.po_got.at[to[0]], r.po_ring)
    dwo_near.wait_recv()

    @pl.loop(0, 16)
    def _(a):
        for b in range(4):
            at = (a // 4, lax.rem(a, 4) // 2, lax.rem(a, 2), b)
            r.dwo_got[at] = r.wo_all[(*at, c)] + r.dwo_got[at]

    more, less = slice(0, CUT), slice(CUT, WIDTH)
    dwo_one = scattered(Z_PEERS, lambda to: r.dwo_got.at[to[0], :, :, :, :, more], r.dwo_z)
    dwo_two = scattered(Y_PEERS, lambda to: r.dwo_got.at[:, :, :, to[3], :, less], r.dwp_y)

    gh.wait_recv()
    keep.wait()
    gh_near = net.put(r.gh_pair.at[:, :, columns(1 - c)], r.gh_all.at[:, c], over)
    keep = net.local(r.gh_pair.at[:, :, columns(c)], r.gh_all.at[:, c])
    gh_near.wait_recv()
    keep.wait()

    def pair(ref, n):
        return ref[2 * n : 2 * n + 2].reshape(WIDE, HEAD)

    def beside(ref, n):
        return jnp.concatenate([ref[2 * n], ref[2 * n + 1]], 1)

    swaps = {}

    def attend_back(n):
        q = pair(r.q, n)
        g = r.gh_all[2 * n : 2 * n + 2].reshape(WIDE, HEAD)
        norm = beside(r.norm, n)
        inner = jnp.sum(g.T.astype(F32) * beside(r.full, n), 0, keepdims=True)
        acc = jnp.zeros((HEAD, WIDE), F32)
        for b in range(n + 1):
            key = pair(r.k, b)
            p = jnp.exp2(dot_t(key, q) * SCALE2) * norm
            p = jnp.where(visible(n * WIDE, b * WIDE, WIDE, WIDE), p, 0.0)
            dp = dot_t(pair(r.v, b), g)
            ds = (p * (dp - inner)).astype(BF)
            dv, dk = dot(p.astype(BF), g), dot(ds, q)
            r.dv[b] = dv if n == 3 else r.dv[b] + dv
            r.dk[b] = dk if n == 3 else r.dk[b] + dk
            acc = acc + dot(beside(r.k_turned, b), ds)
        r.dq[n % 2] = (acc * SCALE).T
        r.dk[n] = r.dk[n] * SCALE
        sent = jnp.where(c == 0, r.dv[n], r.dk[n]).astype(BF)
        r.att[2 * n : 2 * n + 2] = sent.reshape(2, 2, TOK, HEAD)
        swaps[n] = net.put(r.att.at[pl.ds(2 * n, 2)], r.swap_got.at[n], over)

    p_near = {}
    r.dw[...] = jnp.zeros_like(r.dw)
    r.hg[...] = jnp.zeros_like(r.hg)

    def project_back(n):
        swaps[n].wait_recv()
        for half in range(2):
            m = 2 * n + half
            rows = slice(half * BLOCK, (half + 1) * BLOCK)
            inputs = r.x_all[2 * m : 2 * m + 2].reshape(BLOCK, WIDTH).astype(F32)
            first_in = (inputs * inverse_root(inputs) * r.gain_one[...]).astype(BF)
            cosine, sine = angles(m)
            dq, q_part = head_back(r.q_un[m], r.dq[n % 2, rows], cosine, sine, r.gain_q[...])
            both = jnp.where(c == 0, r.dk[n, rows], r.dv[n, rows])
            both = both + r.swap_got[n, half].reshape(BLOCK, HEAD).astype(F32)
            dk, k_part = head_back(r.k_un[m], both, cosine, sine, r.gain_k[...])
            grad = jnp.concatenate([dq, jnp.where(c == 0, dk, both)], 1).astype(BF)
            r.hg[0:1] += q_part
            r.hg[1:2] += jnp.where(c == 0, k_part, 0.0)
            r.dw[...] += t_dot(grad, first_in)
            part = dot_t(grad, r.w_all[...].reshape(WIDTH, 2 * HEAD))
            r.x_all[2 * m : 2 * m + 2] = part.astype(BF).reshape(2, TOK, WIDTH)
            p_near[m] = net.put(r.x_all.at[2 * m + 1 - c], r.s_all.at[m // 2, m % 2], over)

    p_sems, r_sems = net.take(8), net.take(8)

    def p_copy(m):
        return net.copy(
            r.s_all.at[m // 2, m % 2, :, first],
            r.cot_all.at[y, m // 4, :, first],
            (z, xl, xh, m % 4, c),
            p_sems + m,
            p_sems + (m // 4) * 4 + y,
        )

    def r_copy(m):
        return net.copy(
            r.s_all.at[m // 2, m % 2, :, last],
            r.cot_all.at[m % 4, 0, :, last],
            (z, xl, m // 4, y, c),
            r_sems + m,
            r_sems + m % 4,
        )

    def send_parts(n):
        for m in (2 * n, 2 * n + 1):
            p_near[m].wait_recv()
            r.s_all[m // 2, m % 2] = r.x_all[2 * m + c] + r.s_all[m // 2, m % 2]

            @pl.when(y != m % 4)
            def _():
                p_copy(m).start()

            @pl.when(y == m % 4)
            def _():
                r.cot_all[m % 4, m // 4, :, first] = r.s_all[m // 2, m % 2, :, first]

            @pl.when(xh != m // 4)
            def _():
                r_copy(m).start()

    attend_back(3)
    attend_back(2)
    project_back(3)
    attend_back(1)
    send_parts(3)
    project_back(2)
    attend_back(0)
    send_parts(2)
    project_back(1)
    send_parts(1)
    project_back(0)
    send_parts(0)

    r.dw_low[...] = r.dw[...].astype(BF)
    dw_z = scattered(Z_PEERS, lambda to: r.dw_low.at[:, columns(to[0], 2 * TOK)], r.dw_got)
    hg_near = net.put(r.hg, r.hg_near, over)
    hg_near.wait_recv()
    r.hg_two[...] = r.hg[...] + r.hg_near[...]
    hg_ctx = scattered(CTX, lambda to: r.hg_two, r.hg_got)

    at_x = xl * 2 + xh
    dgu_one.wait_recv()

    @pl.loop(0, 4)
    def _(a):
        for b in range(4):
            total = r.dgu[a, at_x, b, :, left].astype(F32)
            for k in range(3):
                total = total + r.dgu_x[k, a, b].astype(F32)
            r.dgu_x[0, a, b] = total.astype(BF)

    dgu_one = scattered(Y_PEERS, lambda to: r.dgu_x.at[0, :, to[3]], r.dgu_y)
    dgu_two.wait_recv()

    @pl.loop(0, 4)
    def _(a):
        for b in range(4):
            total = r.dgu[a, b, y, :, right].astype(F32)
            for k in range(3):
                total = total + r.dgv_y[k, a, b].astype(F32)
            r.dgv_y[0, a, b] = total.astype(BF)

    dgu_two = scattered(X_PEERS, lambda to: r.dgv_y.at[0, :, to[1] * 2 + to[2]], r.dgv_x)
    dwdy_sems = net.take(4)

    def dwdy_copy(k):
        to = moved(me, Y_PEERS[k])
        return net.copy(r.dwd_x.at[0, to[3]], r.dwd_y.at[k], to, dwdy_sems + k, dwdy_sems + k)

    @pl.when(xl == c)
    def _():
        for k in range(3):
            dwd_copy(k).wait_recv()
        for b in range(4):
            total = r.dwd[xh * 4 + b].astype(F32)
            for k in range(3):
                total = total + r.dwd_x[k, b].astype(F32)
            r.dwd_x[0, b] = total.astype(BF)
        for k in range(3):
            dwdy_copy(k).start()

    dw_z.wait_recv()
    total = r.dw_low[:, columns(z, 2 * TOK)].astype(F32)
    for k in range(3):
        total = total + r.dw_got[k].astype(F32)
    r.dw_mid[0] = total[:, :TOK].astype(BF)
    r.dw_mid[1] = total[:, TOK:].astype(BF)
    dw_xl = net.put(r.dw_mid.at[1 - xl], r.dw_xl, moved(me, X_LOW))

    dwo_one.wait_recv()

    @pl.loop(0, 4)
    def _(a):
        for b in range(4):
            at = (a // 2, lax.rem(a, 2), b)
            total = r.dwo_got[(z, *at, slice(None), more)].astype(F32)
            for k in range(3):
                total = total + r.dwo_z[(k, *at)].astype(F32)
            r.dwo_z[(0, *at)] = total.astype(BF)

    dwo_one = scattered(Y_PEERS, lambda to: r.dwo_z.at[0, :, :, to[3]], r.dwo_y)
    dwo_two.wait_recv()

    @pl.loop(0, 4)
    def _(a):
        for b in range(4):
            at = (a, b // 2, b % 2)
            total = r.dwo_got[(*at, y, slice(None), less)].astype(F32)
            for k in range(3):
                total = total + r.dwp_y[(k, *at)].astype(F32)
            r.dwp_y[(0, *at)] = total.astype(BF)

    dwo_two = scattered(Z_PEERS, lambda to: r.dwp_y.at[0, to[0]], r.dwp_z)

    def wait_left(half):
        for o in Y_PEERS:
            k = p_sems + half * 4 + before(me, o)[3]
            net.copy(r.p_x_src, r.p_x, over, k, k).wait_recv()

    def sum_left(half):
        total = r.cot_all[0, half, :, first].astype(F32)
        for b in range(1, 4):
            total = total + r.cot_all[b, half, :, first].astype(F32)
        return total

    def sum_right(b):
        at = xh * 2 + b // 2
        return r.s_all[at, lax.rem(b, 2), :, last].astype(F32) + r.cot_all[b, 0, :, last].astype(F32)

    wait_left(1 - xh)
    r.p_x_src[...] = sum_left(1 - xh).astype(BF)
    p_x = net.put(r.p_x_src, r.p_x, moved(me, X_HALF))
    for b in range(4):
        net.copy(r.p_x_src, r.p_x, over, r_sems + b, r_sems + b).wait_recv()
    for o in Y_PEERS:
        b = moved(me, o)[3]
        r.cot_all[b, 0, :, last] = sum_right(b).astype(BF)
    r_y = scattered(
        Y_PEERS, lambda to: r.cot_all.at[to[3], 0, :, last], r.cot_all.at[pl.ds(0, 3), 1, :, last]
    )

    hg_ctx.wait_recv()
    total = r.hg_two[...]
    for k in range(7):
        total = total + r.hg_got[k]
    r.hg_mid[...] = total
    hg_dp = scattered(DP_ALL, lambda to: r.hg_mid, r.hg_dp)

    def paired(source, pair, got, peers, index):
        near_copy = net.put(source.at[:, 1 - c], pair.at[:, c], over)
        pair[:, c] = source[:, c]
        near_copy.wait_recv()
        got[index(me)] = pair[index(me)]
        to = [moved(me, o) for o in peers]
        return net.put_all(
            [(pair.at[index(t)], got.at[index(me)], t) for t in to], got.at[pl.ds(0, len(peers))]
        )

    dw_xl.wait_recv()
    total = r.dw_mid[xl].astype(F32) + r.dw_xl[...].astype(F32)
    r.dw_sum[...] = total.T.reshape(8, 2, 8, 2 * HEAD)
    dw_ctx = paired(r.dw_sum, r.dw_pair, r.dw_rows, CTX, chip_of)

    dgu_one.wait_recv()
    dgu_two.wait_recv()
    for a in range(4):
        one = r.dgu_x[0, a, y].astype(F32)
        two = r.dgv_y[0, a, at_x].astype(F32)
        for k in range(3):
            one = one + r.dgu_y[k, a].astype(F32)
            two = two + r.dgv_x[k, a].astype(F32)
        r.dgu_sum[a, :, :, left] = one.reshape(2, 8, SLICE)
        r.dgu_sum[a, :, :, right] = two.reshape(2, 8, SLICE)
    dgu_z = paired(r.dgu_sum, r.dgu_pair, r.dgu_got, Z_PEERS, lambda at: at[0])

    def half_copy():
        return net.copy(r.dwd_sum.at[1 - c], r.dwd_half, over, dwdy_sems + 3, dwdy_sems + 3)

    @pl.when(xl == c)
    def _():
        for k in range(3):
            dwdy_copy(k).wait_recv()
        total = r.dwd_x[0, y].astype(F32)
        for k in range(3):
            total = total + r.dwd_y[k].astype(F32)
        r.dwd_sum[0] = total[:24]
        r.dwd_sum[1] = total[24:]
        half_copy().start()
        r.dwd_out[...] = r.dwd_sum[c]

    dwo_one.wait_recv()
    for b in range(4):
        at = (b // 2, b % 2)
        total = r.dwo_z[(0, *at, y)].astype(F32)
        for k in range(3):
            total = total + r.dwo_y[(k, *at)].astype(F32)
        r.dwo_y[(0, *at)] = total.astype(BF)
    dwo_one = scattered(X_PEERS, lambda to: r.dwo_y.at[0, to[1], to[2]], r.dwo_x)
    dwo_two.wait_recv()
    for b in range(4):
        at = (b // 2, b % 2)
        total = r.dwp_y[(0, z, *at)].astype(F32)
        for k in range(3):
            total = total + r.dwp_z[(k, *at)].astype(F32)
        r.dwp_z[(0, *at)] = total.astype(BF)
    dwo_two = scattered(X_PEERS, lambda to: r.dwp_z.at[0, to[1], to[2]], r.dwp_x)

    po_ring.wait_recv()
    total = r.resid[...] + r.po_got[z].astype(F32)
    for k in range(3):
        total = total + r.po_ring[k].astype(F32)
    r.resid[...] = total
    outs = [net.local(r.resid, r.output)]

    wait_left(xh)
    p_x.wait_recv()
    total = sum_left(xh) + r.p_x[...].astype(F32)
    r_y.wait_recv()
    other = sum_right(y)
    for k in range(3):
        other = other + r.cot_all[k, 1, :, last].astype(F32)
    total = jnp.concatenate([total, other], 1)
    inputs = r.tok[...].astype(F32)
    r.grad_resid[...] += norm_back(
        inputs, inverse_root(inputs), total * r.gain_one[...]
    )
    outs.append(net.local(r.grad_resid, r.input_grad))

    dwo_one.wait_recv()
    total = r.dwo_y[0, xl, xh].astype(F32)
    for k in range(3):
        total = total + r.dwo_x[k].astype(F32)
    r.dwo_out[:, more] = total
    dwo_two.wait_recv()
    total = r.dwp_z[0, xl, xh].astype(F32)
    for k in range(3):
        total = total + r.dwp_x[k].astype(F32)
    r.dwo_out[:, less] = total
    outs.append(net.local(r.dwo_out, r.grad_out))

    @pl.when(xl != c)
    def _():
        half_copy().wait_recv()
        r.dwd_out[...] = r.dwd_half[...]

    outs.append(net.local(r.dwd_out, r.grad_down))
    dgu_z.wait_recv()
    for j in range(8):
        r.dgu_out[:, j * SLICE : (j + 1) * SLICE] = r.dgu_got[j // 2, j % 2, :, :SLICE]
        r.dgu_out[:, FF + j * SLICE : FF + (j + 1) * SLICE] = r.dgu_got[j // 2, j % 2, :, SLICE:]
    outs.append(net.local(r.dgu_out, r.grad_up))
    lane = lax.broadcasted_iota(jnp.int32, (8, 128), 1)
    row = lax.broadcasted_iota(jnp.int32, (8, 128), 0)

    def picked(values, at):
        return jnp.sum(jnp.where(lane == at, values, 0.0), 1, keepdims=True)

    two = jnp.sum(r.dgu_out[...] * r.wgu[...].astype(F32), 1, keepdims=True)
    two = two / picked(r.gains[...], row + 8)
    dw_ctx.wait_recv()
    for j in range(16):
        extra = (KEY_AT, VALUE_AT)[j % 2] + j // 2 * HEAD
        r.dwq_out[:, j * HEAD : (j + 1) * HEAD] = r.dw_rows[j // 2, j % 2, :, :HEAD]
        r.dwq_out[:, extra : extra + HEAD] = r.dw_rows[j // 2, j % 2, :, HEAD:]
    outs.append(net.local(r.dwq_out, r.grad_qkv))
    one = jnp.sum(r.dwq_out[...] * r.wqkv[...].astype(F32), 1, keepdims=True)
    one = one / picked(r.gains[...], row)
    hg_dp.wait_recv()
    total = r.hg_mid[...]
    for k in range(7):
        total = total + r.hg_dp[k]
    heads = picked(total, here * 16 + mine)
    r.gains_out[...] = jnp.where(lane == 0, one, jnp.where(lane == 1, two, heads))
    outs.append(net.local(r.gains_out, r.gain_grads))

    for m in range(8):

        @pl.when(y != m % 4)
        def _():
            p_copy(m).wait_send()

        @pl.when(xh != m // 4)
        def _():
            r_copy(m).wait_send()

    @pl.when(xl == c)
    def _():
        for k, o in enumerate(Y_PEERS):
            at = r.wd_all.at[xh, y]
            net.copy(at, at, over, wd_sems + k, wd_sems + k).wait_send()
        for k, o in enumerate(X_PEERS):
            at = r.wd_all.at[xh]
            net.copy(at, at, over, wdx_sems + k, wdx_sems + k).wait_send()
        dwd_copy(half_at).wait_send()
        for k in range(3):
            dwdy_copy(k).wait_send()
        half_copy().wait_send()

    @pl.when(xl != c)
    def _():
        for k in range(3):
            if k != half_at:
                dwd_copy(k).wait_send()

    net.drain()
    for copy in outs:
        copy.wait()


def finish(*refs):
    ins, gains, outs = refs[:6], refs[6], refs[7:13]
    (attn, q, k, mlp), held, sems = refs[13:17], refs[17:23], refs[23]
    for i in range(6):
        pltpu.make_async_copy(ins[i], held[i], sems.at[i]).start()
    for i in range(8):
        attn[i] = gains[i, 0]
        mlp[i] = gains[i, 1]
    q[0] = gains[0, 2]
    k[0] = gains[1, 2]
    for i in range(6):
        pltpu.make_async_copy(ins[i], held[i], sems.at[i]).wait()
        pltpu.make_async_copy(held[i], outs[i], sems.at[i]).start()
    for i in range(6):
        pltpu.make_async_copy(held[i], outs[i], sems.at[i]).wait()


def on_device(
    tokens, lengths, attn_gain, q_gain, k_gain, qkv, w_out, mlp_gain, w_gate_up, w_down, cotangent
):
    gains = jnp.concatenate([attn_gain, mlp_gain, q_gain, k_gain]).astype(F32)
    gains = jnp.broadcast_to(jnp.pad(gains, (0, 128 - 18))[None], (8, 128))
    half = np.arange(HEAD // 2, dtype=np.float32) * np.float32(2.0 / HEAD)
    freq = np.float32(THETA) ** (-half)
    freq = jnp.asarray(np.concatenate([freq, freq])[None].astype(np.float32))
    hbm, smem = pl.BlockSpec(memory_space=pl.ANY), pl.BlockSpec(memory_space=pltpu.SMEM)
    outs = pl.pallas_call(
        body,
        name="layer",
        out_shape=tuple(jax.ShapeDtypeStruct(s, d) for s, d in OUTPUTS.values()),
        in_specs=[hbm] * 8 + [smem],
        out_specs=(hbm,) * len(OUTPUTS),
        scratch_shapes=[pltpu.VMEM(s, d) for s, d in BUFFERS.values()]
        + [pltpu.SemaphoreType.DMA((SEMS,))] * 2,
        compiler_params=pltpu.CompilerParams(
            collective_id=1, has_side_effects=True, vmem_limit_bytes=VMEM_LIMIT
        ),
    )(tokens, qkv, w_out, w_gate_up, w_down, cotangent, gains, freq, lengths)
    o = dict(zip(OUTPUTS, outs))
    wide = [o[n] for n in ("output", "input_grad", "grad_qkv", "grad_out", "grad_up", "grad_down")]
    small = [jax.ShapeDtypeStruct((n,), F32) for n in (8, 1, 1, 8)]
    done = pl.pallas_call(
        finish,
        name="finish",
        out_shape=tuple(jax.ShapeDtypeStruct(a.shape, F32) for a in wide) + tuple(small),
        in_specs=[hbm] * 6 + [smem],
        out_specs=(hbm,) * 6 + (smem,) * 4,
        scratch_shapes=[pltpu.VMEM(a.shape, F32) for a in wide] + [pltpu.SemaphoreType.DMA((6,))],
    )(*wide, o["gain_grads"])
    output, input_grad, grad_qkv, grad_out, grad_up, grad_down, attn, q, k, mlp = done
    return output, input_grad, attn, q, k, grad_qkv, grad_out, mlp, grad_up, grad_down


def solution(mesh):
    torus = Mesh(mesh.devices.reshape(SIZES), AXES)
    rows, line = P(AXES, None), P(AXES)
    return jax.shard_map(
        on_device,
        mesh=torus,
        in_specs=(rows, P(DP, None), line, line, line, rows, rows, line, rows, rows, rows),
        out_specs=(rows, rows, line, line, line, rows, rows, line, rows, rows),
        check_vma=False,
    )
```

```python
import math
import types

import jax
import jax.numpy as jnp
import numpy as np
from jax import lax
from jax.experimental import pallas as pl
from jax.experimental.pallas import tpu as pltpu
from jax.sharding import Mesh
from jax.sharding import PartitionSpec as P

QUERY_HEADS = 16
KEY_VALUE_HEADS = 8
HEAD = 128
WIDTH = 1024
FF = 3072
TOK = 128
GROUP = 2048
BLOCK = 256
WIDE = 512
SLICE = FF // 8
CUT = 640
EPS = 1e-06
FAR = 256.0
LN2 = math.log(2.0)
THETA = 1000000.0
SCALE = 1.0 / math.sqrt(HEAD)
SCALE2 = SCALE / math.log(2.0)
KEY_AT = QUERY_HEADS * HEAD
VALUE_AT = KEY_AT + KEY_VALUE_HEADS * HEAD

AXES = ("z", "xl", "xh", "y", "c")
SIZES = (4, 2, 2, 4, 2)
DP = ("z", "xl")
BF = jnp.bfloat16
F32 = jnp.float32
BY_MESH = pl.DeviceIdType.MESH
MIB = 2**20


def offsets(*axes):
    out = [()]
    for size, name in zip(SIZES, AXES):
        out = [o + (k,) for o in out for k in (range(size) if name in axes else (0,))]
    return out[1:]


SIBLING = (0, 0, 0, 0, 1)
CTX = offsets("xh", "y")
DP_ALL = offsets("z", "xl")
X_PEERS = offsets("xl", "xh")
X_HALF = (0, 0, 1, 0, 0)
X_LOW = (0, 1, 0, 0, 0)
Y_PEERS = [(0, 0, 0, k, 0) for k in (1, 3, 2)]
Z_PEERS = [(k, 0, 0, 0, 0) for k in (1, 3, 2)]
PEERS = sorted(set(CTX + DP_ALL + X_PEERS + [SIBLING]))


def moved(me, offset):
    return tuple(lax.rem(m + o, s) if o else m for m, o, s in zip(me, offset, SIZES))


def before(me, offset):
    return tuple(lax.rem(m + s - o, s) if o else m for m, o, s in zip(me, offset, SIZES))


def ctx_of(at):
    return at[2] * 8 + at[3] * 2 + at[4]


def dp_of(at):
    return at[0] * 2 + at[1]


def chip_of(at):
    return at[2] * 4 + at[3]


def columns(k, width=HEAD):
    return pl.ds(pl.multiple_of(k * width, width), width)


class Net:
    def __init__(self, send, recv):
        self.send, self.recv, self.count, self.sent = send, recv, 0, []

    def take(self, n=1):
        k = self.count
        self.count += n
        return k

    def copy(self, src, dst, device, send, recv):
        return pltpu.make_async_remote_copy(
            src_ref=src,
            dst_ref=dst,
            send_sem=self.send.at[send],
            recv_sem=self.recv.at[recv],
            device_id=device,
            device_id_type=BY_MESH,
        )

    def put(self, src, dst, device):
        k = self.take()
        copy = self.copy(src, dst, device, k, k)
        copy.start()
        self.sent.append(copy)
        return copy

    def put_all(self, triples, total):
        k = self.take()
        for src, dst, device in triples:
            self.copy(src, dst, device, k, k).start()
        group = self.copy(total, total, triples[0][2], k, k)
        self.sent.append(group)
        return group

    def local(self, src, dst):
        copy = pltpu.make_async_copy(src, dst, self.send.at[self.take()])
        copy.start()
        return copy

    def drain(self):
        for copy in self.sent:
            copy.wait_send()
        self.sent = []


def arrived(copies):
    for copy in copies:
        copy.wait_recv()


def dot(a, b):
    return jnp.dot(a, b, preferred_element_type=F32)


def dot_t(a, b):
    return lax.dot_general(a, b, (((1,), (1,)), ((), ())), preferred_element_type=F32)


def t_dot(a, b):
    return lax.dot_general(a, b, (((0,), (0,)), ((), ())), preferred_element_type=F32)


def turned(v):
    return pltpu.roll(v, HEAD // 2, 1)


def inverse_root(v):
    return lax.rsqrt(jnp.mean(v * v, -1, keepdims=True) + EPS)


def head_back(unnormed, grad, cosine, sine, gain):
    inverse = inverse_root(unnormed)
    hat = unnormed * inverse
    back = grad * cosine - turned(grad) * sine
    g = back * gain
    raw = inverse * (g - hat * jnp.mean(g * hat, -1, keepdims=True))
    return raw, jnp.sum(back * hat, 0, keepdims=True)


def norm_back(values, inverse, grad):
    cubed = inverse * inverse * inverse
    return inverse * grad - values * cubed * jnp.mean(grad * values, -1, keepdims=True)


BUFFERS = dict(
    tok=((TOK, WIDTH), BF),
    wqkv=((8, VALUE_AT + KEY_VALUE_HEADS * HEAD), BF),
    wgu=((8, 2 * FF), BF),
    wd=((24, WIDTH), BF),
    gains=((8, 128), F32),
    freq=((1, HEAD), F32),
    gains_out=((8, 128), F32),
    dwq_out=((8, VALUE_AT + KEY_VALUE_HEADS * HEAD), F32),
    dwo_out=((16, WIDTH), F32),
    dgu_out=((8, 2 * FF), F32),
    dwd_out=((24, WIDTH), F32),
    wq_src=((8, 2, 8, 2 * HEAD), F32),
    wq_pair=((8, 2, 8, 2 * HEAD), F32),
    wq_tmp=((8, 2, 8, 2 * HEAD), F32),
    w_low=((TOK, 2 * HEAD), BF),
    w_got=((8, TOK, HEAD), BF),
    w_all=((8, TOK, 2 * HEAD), BF),
    g_pair=((2, 8, 128), F32),
    g_tmp=((8, 2, 8, 128), F32),
    g_row=((16, 128), F32),
    g_all=((8, 16, 128), F32),
    gain_one=((1, WIDTH), F32),
    gain_two=((1, WIDTH), F32),
    gain_q=((1, HEAD), F32),
    gain_k=((1, HEAD), F32),
    gu_src=((4, 2, 8, 2 * SLICE), F32),
    gu_pair=((4, 2, 8, 2 * SLICE), F32),
    gu_tmp=((4, 2, 8, 2 * SLICE), F32),
    gu_low=((4, 16, 2 * SLICE), BF),
    gu_all=((4, 2, 2, 4, 16, 2 * SLICE), BF),
    wd_src=((24, WIDTH), F32),
    wd_tmp=((2, 24, WIDTH), F32),
    wd_all=((2, 4, 48, WIDTH), BF),
    wo_all=((4, 2, 2, 4, 2, 16, WIDTH), BF),
    cot_all=((4, 2, TOK, WIDTH), BF),
    x_all=((16, TOK, WIDTH), BF),
    angle=((8, BLOCK, HEAD), F32),
    q=((8, BLOCK, 2 * HEAD), BF),
    k=((8, BLOCK, 2 * HEAD), BF),
    v=((8, BLOCK, HEAD), BF),
    k_turned=((8, HEAD, BLOCK), BF),
    v_turned=((8, HEAD, BLOCK), BF),
    q_un=((8, BLOCK, HEAD), F32),
    k_un=((8, BLOCK, HEAD), F32),
    full=((8, HEAD, BLOCK), F32),
    norm=((8, 1, BLOCK), F32),
    att=((8, 2, TOK, HEAD), BF),
    att_pair=((8, TOK, 2 * HEAD), BF),
    att_all=((TOK, QUERY_HEADS * HEAD), BF),
    resid=((TOK, WIDTH), F32),
    s_all=((4, 2, TOK, WIDTH), BF),
    hidden=((4, BLOCK, SLICE), BF),
    grad_gu=((4, BLOCK, 2 * SLICE), BF),
    pg=((4, 2, TOK, WIDTH), BF),
    pg_got=((4, TOK, WIDTH), BF),
    pg_ring=((3, TOK, WIDTH), BF),
    po_got=((4, TOK, WIDTH), BF),
    po_ring=((3, TOK, WIDTH), BF),
    dgu=((4, 4, 4, 16, 2 * SLICE), BF),
    dgu_x=((3, 4, 4, 16, SLICE), BF),
    dgu_y=((3, 4, 16, SLICE), BF),
    dgv_y=((3, 4, 4, 16, SLICE), BF),
    dgv_x=((3, 4, 16, SLICE), BF),
    dwd=((8, 48, WIDTH), BF),
    dwd_x=((3, 4, 48, WIDTH), BF),
    dwd_y=((3, 48, WIDTH), BF),
    dwd_sum=((2, 24, WIDTH), F32),
    dwd_half=((24, WIDTH), F32),
    dwo_got=((4, 2, 2, 4, 16, WIDTH), BF),
    dwo_z=((3, 2, 2, 4, 16, CUT), BF),
    dwo_y=((3, 2, 2, 16, CUT), BF),
    dwo_x=((3, 16, CUT), BF),
    dwp_y=((3, 4, 2, 2, 16, WIDTH - CUT), BF),
    dwp_z=((3, 2, 2, 16, WIDTH - CUT), BF),
    dwp_x=((3, 16, WIDTH - CUT), BF),
    grad_resid=((TOK, WIDTH), F32),
    gh_pair=((8, TOK, 2 * HEAD), BF),
    gh_all=((8, 2, TOK, HEAD), BF),
    dk=((4, WIDE, HEAD), F32),
    dv=((4, WIDE, HEAD), F32),
    swap_got=((4, 2, 2, TOK, HEAD), BF),
    dq=((2, WIDE, HEAD), F32),
    p_x=((TOK, WIDTH // 2), BF),
    p_x_src=((TOK, WIDTH // 2), BF),
    dw=((2 * HEAD, WIDTH), F32),
    dw_low=((2 * HEAD, WIDTH), BF),
    dw_got=((3, 2 * HEAD, 2 * TOK), BF),
    dw_mid=((2, 2 * HEAD, TOK), BF),
    dw_xl=((2 * HEAD, TOK), BF),
    hg=((8, 128), F32),
    hg_near=((8, 128), F32),
    hg_two=((8, 128), F32),
    hg_got=((7, 8, 128), F32),
    hg_mid=((8, 128), F32),
    hg_dp=((7, 8, 128), F32),
)
INPUTS = ("tok_in", "wqkv_in", "wo_in", "wgu_in", "wd_in", "cot_in", "gains_in", "freq_in", "lengths")
OUTPUTS = dict(
    output=((TOK, WIDTH), F32),
    input_grad=((TOK, WIDTH), F32),
    gain_grads=((8, 128), F32),
    grad_qkv=((8, VALUE_AT + KEY_VALUE_HEADS * HEAD), F32),
    grad_out=((16, WIDTH), F32),
    grad_up=((8, 2 * FF), F32),
    grad_down=((24, WIDTH), F32),
)
SEMS = 180
VMEM_LIMIT = 60 * MIB


def body(*refs):
    names = list(INPUTS) + list(OUTPUTS) + list(BUFFERS) + ["send", "recv"]
    r = types.SimpleNamespace(**dict(zip(names, refs, strict=True)))
    me = tuple(lax.axis_index(a) for a in AXES)
    z, xl, xh, y, c = me
    chip = xh * 4 + y
    mine, here = ctx_of(me), dp_of(me)
    over = moved(me, SIBLING)
    net = Net(r.send, r.recv)

    own_wo = (z, xl, xh, y, c)
    loads = [
        net.local(r.wqkv_in, r.wqkv),
        net.local(r.gains_in, r.gains),
        net.local(r.wgu_in, r.wgu),
        net.local(r.wd_in, r.wd),
        net.local(r.tok_in, r.tok),
        net.local(r.wo_in, r.wo_all.at[own_wo]),
        net.local(r.freq_in, r.freq),
        net.local(r.cot_in, r.cot_all.at[z, c]),
    ]
    barrier = pltpu.get_barrier_semaphore()
    for o in PEERS:
        pl.semaphore_signal(barrier, inc=1, device_id=moved(me, o), device_id_type=BY_MESH)
    for copy in loads:
        copy.wait()

    w = r.wqkv[...].astype(F32)
    for j in range(16):
        extra = (KEY_AT, VALUE_AT)[j % 2] + j // 2 * HEAD
        r.wq_src[j // 2, j % 2, :, :HEAD] = w[:, j * HEAD : (j + 1) * HEAD]
        r.wq_src[j // 2, j % 2, :, HEAD:] = w[:, extra : extra + HEAD]
    w = r.wgu[...].astype(F32)
    for j in range(8):
        r.gu_src[j // 2, j % 2, :, :SLICE] = w[:, j * SLICE : (j + 1) * SLICE]
        r.gu_src[j // 2, j % 2, :, SLICE:] = w[:, FF + j * SLICE : FF + (j + 1) * SLICE]
    r.wd_src[...] = r.wd[...].astype(F32)
    r.wq_pair[:, c] = r.wq_src[:, c]
    r.gu_pair[:, c] = r.gu_src[:, c]
    r.g_pair[c] = r.gains[...]
    r.wd_tmp[c] = r.wd_src[...]
    r.x_all[mine] = r.tok[...]
    pl.semaphore_wait(barrier, len(PEERS))

    small = [
        net.put(r.wq_src.at[:, 1 - c], r.wq_pair.at[:, c], over),
        net.put(r.gains, r.g_pair.at[c], over),
        net.put(r.gu_src.at[:, 1 - c], r.gu_pair.at[:, c], over),
        net.put(r.wd_src, r.wd_tmp.at[c], over),
    ]
    wo_own = r.wo_all.at[own_wo]
    wo_x = net.put_all(
        [(wo_own, wo_own, moved(me, o)) for o in X_PEERS], r.wo_all.at[0, 0, 0, pl.ds(0, 3), 0]
    )
    at = r.cot_all.at[z, c]
    cot_z = [net.put(at, at, moved(me, o)) for o in Z_PEERS[:2]]
    arrived(small)
    w_ctx = net.put_all(
        [(r.wq_pair.at[chip_of(to)], r.wq_tmp.at[chip], to) for to in (moved(me, o) for o in CTX)],
        r.wq_tmp.at[pl.ds(0, 7)],
    )
    g_ctx = net.put_all(
        [(r.g_pair, r.g_tmp.at[chip], moved(me, o)) for o in CTX], r.g_tmp.at[pl.ds(0, 7)]
    )
    gu_z = net.put_all(
        [(r.gu_pair.at[to[0]], r.gu_tmp.at[z], to) for to in (moved(me, o) for o in Z_PEERS)],
        r.gu_tmp.at[pl.ds(0, 3)],
    )
    r.wq_tmp[chip] = r.wq_pair[chip]
    r.g_tmp[chip] = r.g_pair[...]
    r.gu_tmp[z] = r.gu_pair[z]
    wd_sems = net.take(3)

    @pl.when(xl == c)
    def _():
        r.wd_all[xh, y] = r.wd_tmp[...].reshape(48, WIDTH).astype(BF)
        for k, o in enumerate(Y_PEERS):
            at = r.wd_all.at[xh, y]
            net.copy(at, at, moved(me, o), wd_sems + k, wd_sems + k).start()

    tok_x = net.put(r.tok, r.x_all.at[mine], moved(me, X_HALF))
    tok_y = [net.put(r.tok, r.x_all.at[mine], moved(me, o)) for o in Y_PEERS]
    tok_own = net.put(r.tok, r.x_all.at[mine], over)
    at = r.cot_all.at[z, c]
    cot_near = [net.put(at, at, over)]

    ends, starts = [], []
    total = 0
    for d in range(8):
        starts.append(total)
        total = total + r.lengths[0, d]

    def begin_of(index):
        out = jnp.zeros_like(index)
        for s in starts[1:]:
            out = jnp.where(index >= s, s, out)
        return out

    def pass_on(ref, at):
        return net.put(ref.at[at], ref.at[at], over)

    def same(ref, peers, total):
        return net.put_all([(ref, ref, moved(me, o)) for o in peers], total)

    first, last = slice(0, WIDTH // 2), slice(WIDTH // 2, WIDTH)
    left, right = slice(0, SLICE), slice(SLICE, 2 * SLICE)
    wo_x.wait_recv()
    wo_y = same(r.wo_all.at[z, :, :, y, c], Y_PEERS, r.wo_all.at[pl.ds(0, 3), :, :, 0, 0])
    gu_z.wait_recv()
    r.gu_low[...] = r.gu_tmp[...].reshape(4, 16, 2 * SLICE).astype(BF)
    r.gu_all[:, xl, xh, y] = r.gu_low[...]
    gu_y = net.put_all(
        [
            (r.gu_low.at[:, :, left], r.gu_all.at[:, xl, xh, y, :, left], moved(me, o))
            for o in Y_PEERS
        ],
        r.gu_all.at[:, 0, 0, pl.ds(0, 3), :, left],
    )
    gu_x = net.put_all(
        [
            (r.gu_low.at[:, :, right], r.gu_all.at[:, xl, xh, y, :, right], moved(me, o))
            for o in X_PEERS
        ],
        r.gu_all.at[:, 0, 0, pl.ds(0, 3), :, right],
    )

    w_ctx.wait_recv()
    r.w_low[...] = r.wq_tmp[...].reshape(TOK, 2 * HEAD).astype(BF)
    w_xl = net.put(r.w_low, r.w_all.at[here], moved(me, X_LOW))
    g_ctx.wait_recv()
    r.g_row[...] = r.g_tmp[:, :, 0, :].reshape(16, 128)
    g_dp = net.put_all(
        [(r.g_row, r.g_all.at[here], moved(me, o)) for o in DP_ALL], r.g_all.at[pl.ds(0, 7)]
    )
    r.w_all[here] = r.w_low[...]
    r.g_all[here] = r.g_row[...]

    low = lax.broadcasted_iota(jnp.int32, (BLOCK, HEAD), 1) < HEAD // 2
    shift = jnp.where(low, 0.0, 0.5 * math.pi)

    @pl.loop(0, 8)
    def _(n):
        index = n * BLOCK + lax.broadcasted_iota(jnp.int32, (BLOCK, HEAD), 0)
        phase = (index - begin_of(index)).astype(F32) * r.freq[...]
        r.angle[n] = jnp.cos(phase - shift)
        document = jnp.zeros_like(index)
        for s in starts[1:]:
            document = document + (index >= s).astype(jnp.int32)
        place = lax.broadcasted_iota(jnp.int32, (BLOCK, HEAD), 1)
        same_doc = jnp.where(document == place, 1.0, 0.0)
        r.q[n, :, HEAD:] = jnp.where(place == 8, 1.0, same_doc).astype(BF)
        r.k[n, :, HEAD:] = jnp.where(place == 8, -FAR, FAR * same_doc).astype(BF)

    def angles(n):
        both = r.angle[n]
        other = turned(both)
        return jnp.where(low, both, other), jnp.where(low, -other, both)

    w_xl.wait_recv()
    w_z = same(r.w_all.at[pl.ds(2 * z, 2)], Z_PEERS, r.w_all.at[pl.ds(0, 6)])
    tok_x.wait_recv()
    at_x = ctx_of(before(me, X_HALF))
    near = {(1, 0): pass_on(r.x_all, at_x)}
    at = r.x_all.at[at_x, :, first]
    tok_xy = [net.put(at, at, moved(me, o)) for o in Y_PEERS]
    tok_yx = []
    for o, copy in zip(Y_PEERS, tok_y):
        copy.wait_recv()
        source = ctx_of(before(me, o))
        at = r.x_all.at[source, :, last]
        tok_yx.append(net.put(at, at, moved(me, X_HALF)))
        near[(0, o[3])] = pass_on(r.x_all, source)
    cot_far = []
    for k in range(2):
        cot_z[k].wait_recv()
        source = before(me, Z_PEERS[k])[0]
        at = r.cot_all.at[source, c, :, (first, last)[k]]
        cot_far.append(net.put(at, at, moved(me, Z_PEERS[k])))
        cot_near.append(pass_on(r.cot_all, (source, c)))
    wo_y.wait_recv()
    at = r.wo_all.at[z, :, :, :, c]
    wo_z = [net.put(at, at, moved(me, o)) for o in Z_PEERS[:2]]
    wo_near = [net.put(at, at, over)]
    gu_y.wait_recv()
    gu_x.wait_recv()
    gu_yx = same(r.gu_all.at[:, xl, xh, :, :, left], X_PEERS, r.gu_all.at[pl.ds(0, 3), :, :, :, :, left])
    gu_xy = same(r.gu_all.at[:, :, :, y, :, right], Y_PEERS, r.gu_all.at[pl.ds(0, 3), :, :, :, :, right])
    wdx_sems = net.take(3)

    @pl.when(xl == c)
    def _():
        at = r.wd_all.at[xh, y]
        for k, o in enumerate(Y_PEERS):
            net.copy(at, at, moved(me, o), wd_sems + k, wd_sems + k).wait_recv()
        at = r.wd_all.at[xh]
        for k, o in enumerate(X_PEERS):
            net.copy(at, at, moved(me, o), wdx_sems + k, wdx_sems + k).start()

    w_z.wait_recv()
    w_near = net.put(r.w_all.at[:, :, HEAD:], r.w_got, over)
    g_dp.wait_recv()
    gains = r.g_all[...].reshape(128, 128).astype(BF)
    dev = lax.broadcasted_iota(jnp.int32, (128, WIDTH), 0)
    lane = lax.broadcasted_iota(jnp.int32, (128, WIDTH), 1)
    spread = t_dot(gains, (lane // 8 == dev).astype(F32).astype(BF))
    pick = lax.broadcasted_iota(jnp.int32, (8, WIDTH), 1) % 8 == lax.broadcasted_iota(
        jnp.int32, (8, WIDTH), 0
    )
    r.gain_one[...] = jnp.sum(jnp.where(pick, spread[:8], 0.0), 0, keepdims=True)
    r.gain_two[...] = jnp.sum(jnp.where(pick, spread[8:16], 0.0), 0, keepdims=True)
    eye = lax.broadcasted_iota(jnp.int32, (128, 128), 0) == lax.broadcasted_iota(
        jnp.int32, (128, 128), 1
    )
    spread = t_dot(gains, eye.astype(F32).astype(BF))
    r.gain_q[...] = spread[16:17]
    r.gain_k[...] = spread[17:18]
    w_near.wait_recv()

    def project(n):
        inputs = r.x_all[pl.ds(2 * n, 2)].reshape(BLOCK, WIDTH).astype(F32)
        first_in = (inputs * inverse_root(inputs) * r.gain_one[...]).astype(BF)
        projected = dot(first_in, r.w_all[...].reshape(WIDTH, 2 * HEAD))
        second = dot(first_in, r.w_got[...].reshape(WIDTH, HEAD))
        q_un, own = projected[:, :HEAD], projected[:, HEAD:]
        k_un = jnp.where(c == 0, own, second)
        value = jnp.where(c == 0, second, own)
        r.v[n] = value.astype(BF)
        r.v_turned[n] = value.T.astype(BF)
        r.q_un[n] = q_un
        r.k_un[n] = k_un
        cosine, sine = angles(n)
        q = q_un * inverse_root(q_un) * r.gain_q[...]
        r.q[n, :, :HEAD] = ((q * cosine + turned(q) * sine) * SCALE2).astype(BF)
        key = k_un * inverse_root(k_un) * r.gain_k[...]
        key = key * cosine + turned(key) * sine
        r.k[n, :, :HEAD] = key.astype(BF)
        r.k_turned[n] = key.T.astype(BF)

    tok_own.wait_recv()
    project(chip)
    waiting = [(1, 0)]

    def next_project():
        a, b = waiting.pop(0)
        near[(a, b)].wait_recv()
        project(chip_of(before(me, (0, 0, a, b, 0))))

    for o in Y_PEERS:
        next_project()
        waiting.append((0, o[3]))
    for o, one, two in zip(Y_PEERS, tok_xy, tok_yx):
        one.wait_recv()
        two.wait_recv()
        key = (1, o[3])
        near[key] = pass_on(r.x_all, ctx_of(before(me, (0, 0, 1, o[3], 0))))
        next_project()
        waiting.append(key)
    next_project()
    def causal(size):
        keys = lax.broadcasted_iota(jnp.int32, (size, size), 0)
        return keys <= lax.broadcasted_iota(jnp.int32, (size, size), 1)

    wo_far = []

    def wo_on(k):
        wo_z[k].wait_recv()
        source = before(me, Z_PEERS[k])[0]
        at = r.wo_all.at[source, :, :, :, c, :, (first, last)[k]]
        wo_far.append(net.put(at, at, moved(me, Z_PEERS[k])))
        at = r.wo_all.at[source, :, :, :, c]
        wo_near.append(net.put(at, at, over))

    att_send = net.take(8)
    att_near = []

    def att_copy(i):
        return net.copy(
            r.att_pair.at[i],
            r.att_all.at[:, columns(chip, 2 * HEAD)],
            (z, xl, i // 4, i % 4, c),
            att_send + i,
            att_send + chip,
        )

    def send_pair(i):
        for copy in att_near[i]:
            copy.wait_recv() if copy is att_near[i][0] else copy.wait()

        @pl.when(chip != i)
        def _():
            att_copy(i).start()

    for i in range(8):
        q = r.q[i]
        rows = jnp.zeros((1, BLOCK), F32)
        acc = jnp.zeros((HEAD, BLOCK), F32)
        for b in range(i + 1):
            e = jnp.exp2(dot_t(r.k[b], q))
            if b == i:
                e = jnp.where(causal(BLOCK), e, 0.0)
            rows = rows + jnp.sum(e, 0, keepdims=True)
            acc = acc + dot(r.v_turned[b], e.astype(BF))
        norm = 1.0 / rows
        acc = acc * norm
        r.full[i] = acc
        r.norm[i] = norm
        r.att[i] = acc.T.astype(BF).reshape(2, TOK, HEAD)
        att_near.append(
            (
                net.put(r.att.at[i, 1 - c], r.att_pair.at[i, :, columns(c)], over),
                net.local(r.att.at[i, c], r.att_pair.at[i, :, columns(c)]),
            )
        )
        if i:
            send_pair(i - 1)
        if i in (3, 4):
            wo_on(i - 3)
    send_pair(7)
    keep = net.local(r.att_pair.at[chip], r.att_all.at[:, columns(chip, 2 * HEAD)])
    far = lax.rem(z + 2, 4)
    arrived(wo_far)
    at = r.wo_all.at[far, :, :, :, c]
    wo_near.append(net.put(at, at, over))
    for o in CTX:
        k = att_send + chip_of(before(me, o))
        net.copy(r.att_pair.at[0], r.att_pair.at[0], over, k, k).wait_recv()
    keep.wait()
    arrived(wo_near)

    inputs = r.tok[...].astype(F32)
    residual = inputs + dot(r.att_all[...], r.wo_all[...].reshape(QUERY_HEADS * HEAD, WIDTH))
    r.resid[...] = residual
    inverse_two = inverse_root(residual)
    r.s_all[z, c] = (residual * inverse_two * r.gain_two[...]).astype(BF)
    s_mine = r.s_all.at[z, c]
    s_near = {0: net.put(s_mine, s_mine, over)}
    s_z = [net.put(s_mine, s_mine, moved(me, o)) for o in Z_PEERS[:2]]

    arrived(cot_far)
    cot_near.append(pass_on(r.cot_all, (far, c)))
    arrived([gu_yx, gu_xy] + cot_near)
    at = r.wd_all.at[0]

    @pl.when(xl == c)
    def _():
        net.copy(at, at, over, wdx_sems, wdx_sems + X_PEERS.index(X_HALF)).wait_recv()

    @pl.when(xl != c)
    def _():
        for k, o in enumerate(X_PEERS):
            if o != X_HALF:
                net.copy(at, at, over, wdx_sems, wdx_sems + k).wait_recv()

    def feed_forward(n):
        w_gu = r.gu_all[...].reshape(WIDTH, 2 * SLICE)
        gu = dot(r.s_all[n].reshape(BLOCK, WIDTH), w_gu)
        grad_hidden = dot_t(r.cot_all[n].reshape(BLOCK, WIDTH), r.wd_all[...].reshape(SLICE, WIDTH))
        gate, up = gu[:, :SLICE], gu[:, SLICE:]
        sigma = 1.0 / (1.0 + jnp.exp(-gate))
        swish = gate * sigma
        r.hidden[n] = (swish * up).astype(BF)
        grad_gate = grad_hidden * up * sigma * (1.0 + gate * (1.0 - sigma))
        grad_gu = jnp.concatenate([grad_gate, grad_hidden * swish], 1).astype(BF)
        r.grad_gu[n] = grad_gu
        r.pg[n] = dot_t(grad_gu, w_gu).astype(BF).reshape(2, TOK, WIDTH)
        return net.put(r.pg.at[n, 1 - c], r.pg_got.at[n], over)

    pg_near, pg_ring = {}, []

    def mix(n, got):
        r.pg_got[n] = (r.pg[n, c].astype(F32) + r.pg_got[n].astype(F32)).astype(BF)

    def send_mixed(k):
        o = Z_PEERS[k]
        to = moved(me, o)
        pg_near[k].wait_recv()
        mix(to[0], None)
        pg_ring.append(net.put(r.pg_got.at[to[0]], r.pg_ring.at[k], to))

    s_near[0].wait_recv()
    pg_own = feed_forward(z)
    s_far = []
    for k in range(2):
        s_z[k].wait_recv()
        source = before(me, Z_PEERS[k])[0]
        s_near[k + 1] = pass_on(r.s_all, (source, c))
        at = r.s_all.at[source, c, :, (first, last)[k]]
        s_far.append(net.put(at, at, moved(me, Z_PEERS[k])))
    for k in range(2):
        s_near[k + 1].wait_recv()
        pg_near[1 - k] = feed_forward(before(me, Z_PEERS[k])[0])
        if k:
            send_mixed(1)
    arrived(s_far)
    s_near[3] = pass_on(r.s_all, (far, c))
    send_mixed(0)
    s_near[3].wait_recv()
    pg_near[2] = feed_forward(far)
    done = [2]
    send_mixed(done[-1])
    pg_own.wait_recv()
    mix(z, None)

    gone = [pg_own, *pg_near.values(), *pg_ring]
    early = [copy for copy in net.sent if all(copy is not g for g in gone)]
    net.sent = list(pg_ring)
    s_rows = r.s_all[...].reshape(4 * BLOCK, WIDTH)
    grad_gu = r.grad_gu[...].reshape(4 * BLOCK, 2 * SLICE)
    for a in range(4):
        part = t_dot(s_rows[:, a * BLOCK : (a + 1) * BLOCK], grad_gu)
        r.dgu[a] = part.astype(BF).reshape(4, 4, 16, 2 * SLICE)

    def scattered(peers, source, out):
        to = [moved(me, o) for o in peers]
        return net.put_all([(source(t), out.at[k], t) for k, t in enumerate(to)], out)

    dgu_one = scattered(X_PEERS, lambda to: r.dgu.at[:, to[1] * 2 + to[2], :, :, left], r.dgu_x)
    dgu_two = scattered(Y_PEERS, lambda to: r.dgu.at[:, :, to[3], :, right], r.dgv_y)
    hidden = r.hidden[...].reshape(4 * BLOCK, SLICE)
    for a in range(4):
        cols = slice(a * BLOCK, (a + 1) * BLOCK)
        part = t_dot(hidden, r.cot_all[:, :, :, cols].reshape(4 * BLOCK, BLOCK))
        r.dwd[:, :, cols] = part.astype(BF).reshape(8, 48, BLOCK)
    dwd_sems = net.take(3)
    half_at = X_PEERS.index(X_HALF)

    def dwd_copy(k):
        to = moved(me, X_PEERS[k])
        return net.copy(
            r.dwd.at[pl.ds(to[2] * 4, 4)], r.dwd_x.at[k], to, dwd_sems + k, dwd_sems + k
        )

    for copy in [pg_own, *pg_near.values()]:
        copy.wait_send()
    for n in range(4):
        part = dot(r.hidden[n], r.wd_all[...].reshape(SLICE, WIDTH))
        r.pg[n] = part.astype(BF).reshape(2, TOK, WIDTH)
    po_near = net.put(r.pg.at[:, 1 - c], r.po_got, over)

    po_near.wait_recv()

    @pl.loop(0, 4)
    def _(n):
        r.po_got[n] = r.pg[n, c] + r.po_got[n]

    po_ring = scattered(Z_PEERS, lambda to: r.po_got.at[to[0]], r.po_ring)

    arrived(pg_ring)
    grad_second = r.pg_got[z].astype(F32)
    for k in range(3):
        grad_second = grad_second + r.pg_ring[k].astype(F32)
    residual = r.resid[...]
    inverse_two = inverse_root(residual)
    grad_resid = r.cot_all[z, c].astype(F32) + norm_back(
        residual, inverse_two, grad_second * r.gain_two[...]
    )
    r.grad_resid[...] = grad_resid
    resid_low = grad_resid.astype(BF)
    for i in range(8):

        @pl.when(chip != i)
        def _():
            att_copy(i).wait_send()

    for j in range(8):
        part = dot_t(resid_low, r.wo_all[j // 2, j % 2].reshape(BLOCK, WIDTH))
        r.att_pair[j] = part.astype(BF)
    for copy in early:
        copy.wait_send()
    gh = net.put_all(
        [
            (r.att_pair.at[chip_of(to)], r.gh_pair.at[chip], to)
            for to in (moved(me, o) for o in CTX)
        ],
        r.gh_pair.at[pl.ds(0, 7)],
    )
    keep = net.local(r.att_pair.at[chip], r.gh_pair.at[chip])

    for j in range(8):
        part = t_dot(r.att_all[:, j * BLOCK : (j + 1) * BLOCK], resid_low)
        r.wo_all[j // 2, j % 2] = part.astype(BF).reshape(2, 4, 2, 16, WIDTH)
    dwo_near = net.put(r.wo_all.at[:, :, :, :, 1 - c], r.dwo_got, over)
    at_x = xl * 2 + xh
    dgu_one.wait_recv()

    @pl.loop(0, 4)
    def _(a):
        for b in range(4):
            total = r.dgu[a, at_x, b, :, left].astype(F32)
            for k in range(3):
                total = total + r.dgu_x[k, a, b].astype(F32)
            r.dgu_x[0, a, b] = total.astype(BF)

    dgu_two.wait_recv()

    @pl.loop(0, 4)
    def _(a):
        for b in range(4):
            total = r.dgu[a, b, y, :, right].astype(F32)
            for k in range(3):
                total = total + r.dgv_y[k, a, b].astype(F32)
            r.dgv_y[0, a, b] = total.astype(BF)

    dwo_near.wait_recv()

    @pl.loop(0, 16)
    def _(a):
        for b in range(4):
            at = (a // 4, lax.rem(a, 4) // 2, lax.rem(a, 2), b)
            r.dwo_got[at] = r.wo_all[(*at, c)] + r.dwo_got[at]

    more, less = slice(0, CUT), slice(CUT, WIDTH)
    dwo_one = scattered(Z_PEERS, lambda to: r.dwo_got.at[to[0], :, :, :, :, more], r.dwo_z)
    gh.wait_recv()
    keep.wait()
    dgu_one = scattered(Y_PEERS, lambda to: r.dgu_x.at[0, :, to[3]], r.dgu_y)
    dgu_two = scattered(X_PEERS, lambda to: r.dgv_y.at[0, :, to[1] * 2 + to[2]], r.dgv_x)
    dwo_two = scattered(Y_PEERS, lambda to: r.dwo_got.at[:, :, :, to[3], :, less], r.dwp_y)
    @pl.when(xl == c)
    def _():
        dwd_copy(half_at).start()

    @pl.when(xl != c)
    def _():
        for k in range(3):
            if k != half_at:
                dwd_copy(k).start()

    gh_near = net.put(r.gh_pair.at[:, :, columns(1 - c)], r.gh_all.at[:, c], over)
    keep = net.local(r.gh_pair.at[:, :, columns(c)], r.gh_all.at[:, c])
    gh_near.wait_recv()
    keep.wait()

    def pair(ref, n):
        return ref[2 * n : 2 * n + 2].reshape(WIDE, ref.shape[2])

    def beside(ref, n):
        return jnp.concatenate([ref[2 * n], ref[2 * n + 1]], 1)

    swaps = {}

    def attend_back(n):
        q = pair(r.q, n)
        g = r.gh_all[2 * n : 2 * n + 2].reshape(WIDE, HEAD)
        g_turned = (g.T.astype(F32) * beside(r.norm, n)).astype(BF)
        g = g_turned.T
        inner = jnp.sum(g_turned.astype(F32) * beside(r.full, n), 0, keepdims=True)
        acc = jnp.zeros((HEAD, WIDE), F32)
        for b in range(n + 1):
            key = pair(r.k, b)
            e = jnp.exp2(dot_t(key, q))
            if b == n:
                e = jnp.where(causal(WIDE), e, 0.0)
            dp = dot(pair(r.v, b), g_turned)
            ds = (e * (dp - inner)).astype(BF)
            dv, dk = dot(e.astype(BF), g), dot(ds, q[:, :HEAD])
            r.dv[b] = dv if n == 3 else r.dv[b] + dv
            r.dk[b] = dk if n == 3 else r.dk[b] + dk
            acc = acc + dot(beside(r.k_turned, b), ds)
        r.dq[n % 2] = (acc * SCALE).T
        r.dk[n] = r.dk[n] * LN2
        sent = jnp.where(c == 0, r.dv[n], r.dk[n]).astype(BF)
        r.att[2 * n : 2 * n + 2] = sent.reshape(2, 2, TOK, HEAD)
        swaps[n] = net.put(r.att.at[pl.ds(2 * n, 2)], r.swap_got.at[n], over)

    p_near = {}
    r.dw[...] = jnp.zeros_like(r.dw)
    r.hg[...] = jnp.zeros_like(r.hg)

    def project_back(n):
        swaps[n].wait_recv()
        for half in range(2):
            m = 2 * n + half
            rows = slice(half * BLOCK, (half + 1) * BLOCK)
            inputs = r.x_all[2 * m : 2 * m + 2].reshape(BLOCK, WIDTH).astype(F32)
            first_in = (inputs * inverse_root(inputs) * r.gain_one[...]).astype(BF)
            cosine, sine = angles(m)
            dq, q_part = head_back(r.q_un[m], r.dq[n % 2, rows], cosine, sine, r.gain_q[...])
            both = jnp.where(c == 0, r.dk[n, rows], r.dv[n, rows])
            both = both + r.swap_got[n, half].reshape(BLOCK, HEAD).astype(F32)
            dk, k_part = head_back(r.k_un[m], both, cosine, sine, r.gain_k[...])
            grad = jnp.concatenate([dq, jnp.where(c == 0, dk, both)], 1).astype(BF)
            r.hg[0:1] += q_part
            r.hg[1:2] += jnp.where(c == 0, k_part, 0.0)
            r.dw[...] += t_dot(grad, first_in)
            part = dot_t(grad, r.w_all[...].reshape(WIDTH, 2 * HEAD))
            r.x_all[2 * m : 2 * m + 2] = part.astype(BF).reshape(2, TOK, WIDTH)
            p_near[m] = net.put(r.x_all.at[2 * m + 1 - c], r.s_all.at[m // 2, m % 2], over)

    p_sems, r_sems = net.take(8), net.take(8)

    def p_copy(m):
        return net.copy(
            r.s_all.at[m // 2, m % 2, :, first],
            r.cot_all.at[y, m // 4, :, first],
            (z, xl, xh, m % 4, c),
            p_sems + m,
            p_sems + (m // 4) * 4 + y,
        )

    def r_copy(m):
        return net.copy(
            r.s_all.at[m // 2, m % 2, :, last],
            r.cot_all.at[m % 4, 0, :, last],
            (z, xl, m // 4, y, c),
            r_sems + m,
            r_sems + m % 4,
        )

    def send_parts(n):
        for m in (2 * n, 2 * n + 1):
            p_near[m].wait_recv()
            r.s_all[m // 2, m % 2] = r.x_all[2 * m + c] + r.s_all[m // 2, m % 2]

            @pl.when(y != m % 4)
            def _():
                p_copy(m).start()

            @pl.when(y == m % 4)
            def _():
                r.cot_all[m % 4, m // 4, :, first] = r.s_all[m // 2, m % 2, :, first]

            @pl.when(xh != m // 4)
            def _():
                r_copy(m).start()

    def paired(source, pair):
        copy = net.put(source.at[:, 1 - c], pair.at[:, c], over)
        pair[:, c] = source[:, c]
        return copy

    def dealt(copy, pair, got, peers, index):
        copy.wait_recv()
        got[index(me)] = pair[index(me)]
        to = [moved(me, o) for o in peers]
        return net.put_all(
            [(pair.at[index(t)], got.at[index(me)], t) for t in to], got.at[pl.ds(0, len(peers))]
        )

    def wait_left(half):
        for o in Y_PEERS:
            k = p_sems + half * 4 + before(me, o)[3]
            net.copy(r.p_x_src, r.p_x, over, k, k).wait_recv()

    def sum_left(half):
        total = r.cot_all[0, half, :, first].astype(F32)
        for b in range(1, 4):
            total = total + r.cot_all[b, half, :, first].astype(F32)
        return total

    def sum_right(b):
        at = xh * 2 + b // 2
        return r.s_all[at, lax.rem(b, 2), :, last].astype(F32) + r.cot_all[b, 0, :, last].astype(F32)

    attend_back(3)
    attend_back(2)
    project_back(3)
    attend_back(1)
    send_parts(3)
    project_back(2)
    dwo_two.wait_recv()

    @pl.loop(0, 4)
    def _(a):
        for b in range(4):
            at = (a, b // 2, b % 2)
            total = r.dwo_got[(*at, y, slice(None), less)].astype(F32)
            for k in range(3):
                total = total + r.dwp_y[(k, *at)].astype(F32)
            r.dwp_y[(0, *at)] = total.astype(BF)

    dwo_two = scattered(Z_PEERS, lambda to: r.dwp_y.at[0, to[0]], r.dwp_z)

    attend_back(0)
    send_parts(2)
    dwdy_sems = net.take(4)

    def dwdy_copy(k):
        to = moved(me, Y_PEERS[k])
        return net.copy(r.dwd_x.at[0, to[3]], r.dwd_y.at[k], to, dwdy_sems + k, dwdy_sems + k)

    @pl.when(xl == c)
    def _():
        for k in range(3):
            dwd_copy(k).wait_recv()
        for b in range(4):
            total = r.dwd[xh * 4 + b].astype(F32)
            for k in range(3):
                total = total + r.dwd_x[k, b].astype(F32)
            r.dwd_x[0, b] = total.astype(BF)
        for k in range(3):
            dwdy_copy(k).start()

    project_back(1)
    send_parts(1)
    dgu_one.wait_recv()
    dgu_two.wait_recv()
    for a in range(4):
        one = r.dgu_x[0, a, y].astype(F32)
        two = r.dgv_y[0, a, at_x].astype(F32)
        for k in range(3):
            one = one + r.dgu_y[k, a].astype(F32)
            two = two + r.dgv_x[k, a].astype(F32)
        r.gu_src[a, :, :, left] = one.reshape(2, 8, SLICE)
        r.gu_src[a, :, :, right] = two.reshape(2, 8, SLICE)
    dgu_near = paired(r.gu_src, r.gu_pair)

    dgu_z = dealt(dgu_near, r.gu_pair, r.gu_tmp, Z_PEERS, lambda at: at[0])
    project_back(0)
    r.dw_low[...] = r.dw[...].astype(BF)
    dw_z = scattered(Z_PEERS, lambda to: r.dw_low.at[:, columns(to[0], 2 * TOK)], r.dw_got)
    send_parts(0)
    hg_near = net.put(r.hg, r.hg_near, over)
    def half_copy():
        return net.copy(r.dwd_sum.at[1 - c], r.dwd_half, over, dwdy_sems + 3, dwdy_sems + 3)

    @pl.when(xl == c)
    def _():
        for k in range(3):
            dwdy_copy(k).wait_recv()
        total = r.dwd_x[0, y].astype(F32)
        for k in range(3):
            total = total + r.dwd_y[k].astype(F32)
        r.dwd_sum[0] = total[:24]
        r.dwd_sum[1] = total[24:]
        half_copy().start()
        r.dwd_out[...] = r.dwd_sum[c]

    hg_near.wait_recv()
    r.hg_two[...] = r.hg[...] + r.hg_near[...]
    hg_ctx = scattered(CTX, lambda to: r.hg_two, r.hg_got)

    dwo_one.wait_recv()

    @pl.loop(0, 4)
    def _(a):
        for b in range(4):
            at = (a // 2, lax.rem(a, 2), b)
            total = r.dwo_got[(z, *at, slice(None), more)].astype(F32)
            for k in range(3):
                total = total + r.dwo_z[(k, *at)].astype(F32)
            r.dwo_z[(0, *at)] = total.astype(BF)

    dwo_one = scattered(Y_PEERS, lambda to: r.dwo_z.at[0, :, :, to[3]], r.dwo_y)
    wait_left(1 - xh)
    r.p_x_src[...] = sum_left(1 - xh).astype(BF)
    p_x = net.put(r.p_x_src, r.p_x, moved(me, X_HALF))
    for b in range(4):
        net.copy(r.p_x_src, r.p_x, over, r_sems + b, r_sems + b).wait_recv()
    for o in Y_PEERS:
        b = moved(me, o)[3]
        r.cot_all[b, 0, :, last] = sum_right(b).astype(BF)
    r_y = scattered(
        Y_PEERS, lambda to: r.cot_all.at[to[3], 0, :, last], r.cot_all.at[pl.ds(0, 3), 1, :, last]
    )

    dw_z.wait_recv()
    total = r.dw_low[:, columns(z, 2 * TOK)].astype(F32)
    for k in range(3):
        total = total + r.dw_got[k].astype(F32)
    r.dw_mid[0] = total[:, :TOK].astype(BF)
    r.dw_mid[1] = total[:, TOK:].astype(BF)
    dw_xl = net.put(r.dw_mid.at[1 - xl], r.dw_xl, moved(me, X_LOW))

    hg_ctx.wait_recv()
    total = r.hg_two[...]
    for k in range(7):
        total = total + r.hg_got[k]
    r.hg_mid[...] = total
    hg_dp = scattered(DP_ALL, lambda to: r.hg_mid, r.hg_dp)

    dw_xl.wait_recv()
    total = r.dw_mid[xl].astype(F32) + r.dw_xl[...].astype(F32)
    r.wq_src[...] = total.T.reshape(8, 2, 8, 2 * HEAD)
    dw_near = paired(r.wq_src, r.wq_pair)
    dw_ctx = dealt(dw_near, r.wq_pair, r.wq_tmp, CTX, chip_of)

    dwo_one.wait_recv()
    for b in range(4):
        at = (b // 2, b % 2)
        total = r.dwo_z[(0, *at, y)].astype(F32)
        for k in range(3):
            total = total + r.dwo_y[(k, *at)].astype(F32)
        r.dwo_y[(0, *at)] = total.astype(BF)
    dwo_one = scattered(X_PEERS, lambda to: r.dwo_y.at[0, to[1], to[2]], r.dwo_x)
    dwo_two.wait_recv()
    for b in range(4):
        at = (b // 2, b % 2)
        total = r.dwp_y[(0, z, *at)].astype(F32)
        for k in range(3):
            total = total + r.dwp_z[(k, *at)].astype(F32)
        r.dwp_z[(0, *at)] = total.astype(BF)
    dwo_two = scattered(X_PEERS, lambda to: r.dwp_z.at[0, to[1], to[2]], r.dwp_x)

    po_ring.wait_recv()
    total = r.resid[...] + r.po_got[z].astype(F32)
    for k in range(3):
        total = total + r.po_ring[k].astype(F32)
    r.resid[...] = total
    outs = [net.local(r.resid, r.output)]

    wait_left(xh)
    p_x.wait_recv()
    total = sum_left(xh) + r.p_x[...].astype(F32)
    r_y.wait_recv()
    other = sum_right(y)
    for k in range(3):
        other = other + r.cot_all[k, 1, :, last].astype(F32)
    total = jnp.concatenate([total, other], 1)
    inputs = r.tok[...].astype(F32)
    r.grad_resid[...] += norm_back(
        inputs, inverse_root(inputs), total * r.gain_one[...]
    )
    outs.append(net.local(r.grad_resid, r.input_grad))

    dwo_one.wait_recv()
    total = r.dwo_y[0, xl, xh].astype(F32)
    for k in range(3):
        total = total + r.dwo_x[k].astype(F32)
    r.dwo_out[:, more] = total
    dwo_two.wait_recv()
    total = r.dwp_z[0, xl, xh].astype(F32)
    for k in range(3):
        total = total + r.dwp_x[k].astype(F32)
    r.dwo_out[:, less] = total
    outs.append(net.local(r.dwo_out, r.grad_out))

    @pl.when(xl != c)
    def _():
        half_copy().wait_recv()
        r.dwd_out[...] = r.dwd_half[...]

    outs.append(net.local(r.dwd_out, r.grad_down))
    dgu_z.wait_recv()
    for j in range(8):
        r.dgu_out[:, j * SLICE : (j + 1) * SLICE] = r.gu_tmp[j // 2, j % 2, :, :SLICE]
        r.dgu_out[:, FF + j * SLICE : FF + (j + 1) * SLICE] = r.gu_tmp[j // 2, j % 2, :, SLICE:]
    outs.append(net.local(r.dgu_out, r.grad_up))
    lane = lax.broadcasted_iota(jnp.int32, (8, 128), 1)
    row = lax.broadcasted_iota(jnp.int32, (8, 128), 0)

    def picked(values, at):
        return jnp.sum(jnp.where(lane == at, values, 0.0), 1, keepdims=True)

    two = jnp.sum(r.dgu_out[...] * r.wgu[...].astype(F32), 1, keepdims=True)
    two = two / picked(r.gains[...], row + 8)
    dw_ctx.wait_recv()
    for j in range(16):
        extra = (KEY_AT, VALUE_AT)[j % 2] + j // 2 * HEAD
        r.dwq_out[:, j * HEAD : (j + 1) * HEAD] = r.wq_tmp[j // 2, j % 2, :, :HEAD]
        r.dwq_out[:, extra : extra + HEAD] = r.wq_tmp[j // 2, j % 2, :, HEAD:]
    outs.append(net.local(r.dwq_out, r.grad_qkv))
    one = jnp.sum(r.dwq_out[...] * r.wqkv[...].astype(F32), 1, keepdims=True)
    one = one / picked(r.gains[...], row)
    hg_dp.wait_recv()
    total = r.hg_mid[...]
    for k in range(7):
        total = total + r.hg_dp[k]
    heads = picked(total, here * 16 + mine)
    r.gains_out[...] = jnp.where(lane == 0, one, jnp.where(lane == 1, two, heads))
    outs.append(net.local(r.gains_out, r.gain_grads))

    for m in range(8):

        @pl.when(y != m % 4)
        def _():
            p_copy(m).wait_send()

        @pl.when(xh != m // 4)
        def _():
            r_copy(m).wait_send()

    @pl.when(xl == c)
    def _():
        for k, o in enumerate(Y_PEERS):
            at = r.wd_all.at[xh, y]
            net.copy(at, at, over, wd_sems + k, wd_sems + k).wait_send()
        for k, o in enumerate(X_PEERS):
            at = r.wd_all.at[xh]
            net.copy(at, at, over, wdx_sems + k, wdx_sems + k).wait_send()
        dwd_copy(half_at).wait_send()
        for k in range(3):
            dwdy_copy(k).wait_send()
        half_copy().wait_send()

    @pl.when(xl != c)
    def _():
        for k in range(3):
            if k != half_at:
                dwd_copy(k).wait_send()

    net.drain()
    for copy in outs:
        copy.wait()


def finish(*refs):
    ins, gains, outs = refs[:6], refs[6], refs[7:13]
    (attn, q, k, mlp), held, sems = refs[13:17], refs[17:23], refs[23]
    for i in range(6):
        pltpu.make_async_copy(ins[i], held[i], sems.at[i]).start()
    for i in range(8):
        attn[i] = gains[i, 0]
        mlp[i] = gains[i, 1]
    q[0] = gains[0, 2]
    k[0] = gains[1, 2]
    for i in range(6):
        pltpu.make_async_copy(ins[i], held[i], sems.at[i]).wait()
        pltpu.make_async_copy(held[i], outs[i], sems.at[i]).start()
    for i in range(6):
        pltpu.make_async_copy(held[i], outs[i], sems.at[i]).wait()


def on_device(
    tokens, lengths, attn_gain, q_gain, k_gain, qkv, w_out, mlp_gain, w_gate_up, w_down, cotangent
):
    gains = jnp.concatenate([attn_gain, mlp_gain, q_gain, k_gain]).astype(F32)
    gains = jnp.broadcast_to(jnp.pad(gains, (0, 128 - 18))[None], (8, 128))
    half = np.arange(HEAD // 2, dtype=np.float32) * np.float32(2.0 / HEAD)
    freq = np.float32(THETA) ** (-half)
    freq = jnp.asarray(np.concatenate([freq, freq])[None].astype(np.float32))
    hbm, smem = pl.BlockSpec(memory_space=pl.ANY), pl.BlockSpec(memory_space=pltpu.SMEM)
    outs = pl.pallas_call(
        body,
        name="layer",
        out_shape=tuple(jax.ShapeDtypeStruct(s, d) for s, d in OUTPUTS.values()),
        in_specs=[hbm] * 8 + [smem],
        out_specs=(hbm,) * len(OUTPUTS),
        scratch_shapes=[pltpu.VMEM(s, d) for s, d in BUFFERS.values()]
        + [pltpu.SemaphoreType.DMA((SEMS,))] * 2,
        compiler_params=pltpu.CompilerParams(
            collective_id=1, has_side_effects=True, vmem_limit_bytes=VMEM_LIMIT
        ),
    )(tokens, qkv, w_out, w_gate_up, w_down, cotangent, gains, freq, lengths)
    o = dict(zip(OUTPUTS, outs))
    wide = [o[n] for n in ("output", "input_grad", "grad_qkv", "grad_out", "grad_up", "grad_down")]
    small = [jax.ShapeDtypeStruct((n,), F32) for n in (8, 1, 1, 8)]
    done = pl.pallas_call(
        finish,
        name="finish",
        out_shape=tuple(jax.ShapeDtypeStruct(a.shape, F32) for a in wide) + tuple(small),
        in_specs=[hbm] * 6 + [smem],
        out_specs=(hbm,) * 6 + (smem,) * 4,
        scratch_shapes=[pltpu.VMEM(a.shape, F32) for a in wide] + [pltpu.SemaphoreType.DMA((6,))],
    )(*wide, o["gain_grads"])
    output, input_grad, grad_qkv, grad_out, grad_up, grad_down, attn, q, k, mlp = done
    return output, input_grad, attn, q, k, grad_qkv, grad_out, mlp, grad_up, grad_down


def solution(mesh):
    torus = Mesh(mesh.devices.reshape(SIZES), AXES)
    rows, line = P(AXES, None), P(AXES)
    return jax.shard_map(
        on_device,
        mesh=torus,
        in_specs=(rows, P(DP, None), line, line, line, rows, rows, line, rows, rows, rows),
        out_specs=(rows, rows, line, line, line, rows, rows, line, rows, rows),
        check_vma=False,
    )
```

```python
import math
import types

import jax
import jax.numpy as jnp
import numpy as np
from jax import lax
from jax.experimental import pallas as pl
from jax.experimental.pallas import tpu as pltpu
from jax.sharding import Mesh
from jax.sharding import PartitionSpec as P

QUERY_HEADS = 16
KEY_VALUE_HEADS = 8
HEAD = 128
WIDTH = 1024
FF = 3072
TOK = 128
GROUP = 2048
BLOCK = 256
WIDE = 512
SLICE = FF // 8
CUT = 640
EPS = 1e-06
FAR = 256.0
LN2 = math.log(2.0)
THETA = 1000000.0
SCALE = 1.0 / math.sqrt(HEAD)
SCALE2 = SCALE / math.log(2.0)
KEY_AT = QUERY_HEADS * HEAD
VALUE_AT = KEY_AT + KEY_VALUE_HEADS * HEAD

AXES = ("z", "xl", "xh", "y", "c")
SIZES = (4, 2, 2, 4, 2)
DP = ("z", "xl")
BF = jnp.bfloat16
F32 = jnp.float32
BY_MESH = pl.DeviceIdType.MESH
MIB = 2**20


def offsets(*axes):
    out = [()]
    for size, name in zip(SIZES, AXES):
        out = [o + (k,) for o in out for k in (range(size) if name in axes else (0,))]
    return out[1:]


SIBLING = (0, 0, 0, 0, 1)
CTX = offsets("xh", "y")
DP_ALL = offsets("z", "xl")
X_PEERS = offsets("xl", "xh")
X_HALF = (0, 0, 1, 0, 0)
X_LOW = (0, 1, 0, 0, 0)
Y_PEERS = [(0, 0, 0, k, 0) for k in (1, 3, 2)]
Z_PEERS = [(k, 0, 0, 0, 0) for k in (1, 3, 2)]
PEERS = sorted(set(CTX + DP_ALL + X_PEERS + [SIBLING]))


def moved(me, offset):
    return tuple(lax.rem(m + o, s) if o else m for m, o, s in zip(me, offset, SIZES))


def before(me, offset):
    return tuple(lax.rem(m + s - o, s) if o else m for m, o, s in zip(me, offset, SIZES))


def ctx_of(at):
    return at[2] * 8 + at[3] * 2 + at[4]


def dp_of(at):
    return at[0] * 2 + at[1]


def chip_of(at):
    return at[2] * 4 + at[3]


def columns(k, width=HEAD):
    return pl.ds(pl.multiple_of(k * width, width), width)


class Net:
    def __init__(self, send, recv):
        self.send, self.recv, self.count, self.sent = send, recv, 0, []

    def take(self, n=1):
        k = self.count
        self.count += n
        return k

    def copy(self, src, dst, device, send, recv):
        return pltpu.make_async_remote_copy(
            src_ref=src,
            dst_ref=dst,
            send_sem=self.send.at[send],
            recv_sem=self.recv.at[recv],
            device_id=device,
            device_id_type=BY_MESH,
        )

    def put(self, src, dst, device):
        k = self.take()
        copy = self.copy(src, dst, device, k, k)
        copy.start()
        self.sent.append(copy)
        return copy

    def put_all(self, triples, total):
        k = self.take()
        for src, dst, device in triples:
            self.copy(src, dst, device, k, k).start()
        group = self.copy(total, total, triples[0][2], k, k)
        self.sent.append(group)
        return group

    def local(self, src, dst):
        copy = pltpu.make_async_copy(src, dst, self.send.at[self.take()])
        copy.start()
        return copy

    def drain(self):
        for copy in self.sent:
            copy.wait_send()
        self.sent = []


def arrived(copies):
    for copy in copies:
        copy.wait_recv()


def dot(a, b):
    return jnp.dot(a, b, preferred_element_type=F32)


def dot_t(a, b):
    return lax.dot_general(a, b, (((1,), (1,)), ((), ())), preferred_element_type=F32)


def t_dot(a, b):
    return lax.dot_general(a, b, (((0,), (0,)), ((), ())), preferred_element_type=F32)


def turned(v):
    return pltpu.roll(v, HEAD // 2, 1)


def inverse_root(v):
    return lax.rsqrt(jnp.mean(v * v, -1, keepdims=True) + EPS)


def head_back(unnormed, grad, cosine, sine, gain):
    inverse = inverse_root(unnormed)
    hat = unnormed * inverse
    back = grad * cosine - turned(grad) * sine
    g = back * gain
    raw = inverse * (g - hat * jnp.mean(g * hat, -1, keepdims=True))
    return raw, jnp.sum(back * hat, 0, keepdims=True)


def norm_back(values, inverse, grad):
    cubed = inverse * inverse * inverse
    return inverse * grad - values * cubed * jnp.mean(grad * values, -1, keepdims=True)


BUFFERS = dict(
    tok=((TOK, WIDTH), BF),
    wqkv=((8, VALUE_AT + KEY_VALUE_HEADS * HEAD), BF),
    wgu=((8, 2 * FF), BF),
    wd=((24, WIDTH), BF),
    gains=((8, 128), F32),
    freq=((1, HEAD), F32),
    gains_out=((8, 128), F32),
    dwq_out=((8, VALUE_AT + KEY_VALUE_HEADS * HEAD), F32),
    dwo_out=((16, WIDTH), F32),
    dgu_out=((8, 2 * FF), F32),
    dwd_out=((24, WIDTH), F32),
    wq_src=((8, 2, 8, 2 * HEAD), F32),
    wq_pair=((8, 2, 8, 2 * HEAD), F32),
    wq_tmp=((8, 2, 8, 2 * HEAD), F32),
    w_low=((TOK, 2 * HEAD), BF),
    w_got=((8, TOK, HEAD), BF),
    w_all=((8, TOK, 2 * HEAD), BF),
    g_pair=((2, 8, 128), F32),
    g_tmp=((8, 2, 8, 128), F32),
    g_row=((16, 128), F32),
    g_all=((8, 16, 128), F32),
    gain_one=((1, WIDTH), F32),
    gain_two=((1, WIDTH), F32),
    gain_q=((1, HEAD), F32),
    gain_k=((1, HEAD), F32),
    gu_src=((4, 2, 8, 2 * SLICE), F32),
    gu_pair=((4, 2, 8, 2 * SLICE), F32),
    gu_tmp=((4, 2, 8, 2 * SLICE), F32),
    gu_low=((4, 16, 2 * SLICE), BF),
    gu_all=((4, 2, 2, 4, 16, 2 * SLICE), BF),
    wd_src=((24, WIDTH), F32),
    wd_tmp=((2, 24, WIDTH), F32),
    wd_all=((2, 4, 48, WIDTH), BF),
    wo_all=((4, 2, 2, 4, 2, 16, WIDTH), BF),
    cot_all=((4, 2, TOK, WIDTH), BF),
    x_all=((16, TOK, WIDTH), BF),
    angle=((8, BLOCK, HEAD), F32),
    q=((8, BLOCK, 2 * HEAD), BF),
    k=((8, BLOCK, 2 * HEAD), BF),
    v=((8, BLOCK, HEAD), BF),
    k_turned=((8, HEAD, BLOCK), BF),
    v_turned=((8, HEAD, BLOCK), BF),
    q_un=((8, BLOCK, HEAD), F32),
    k_un=((8, BLOCK, HEAD), F32),
    full=((8, HEAD, BLOCK), F32),
    norm=((8, 1, BLOCK), F32),
    att=((8, 2, TOK, HEAD), BF),
    att_pair=((8, TOK, 2 * HEAD), BF),
    att_all=((TOK, QUERY_HEADS * HEAD), BF),
    resid=((TOK, WIDTH), F32),
    s_all=((4, 2, TOK, WIDTH), BF),
    hidden=((4, BLOCK, SLICE), BF),
    grad_gu=((4, BLOCK, 2 * SLICE), BF),
    pg=((4, 2, TOK, WIDTH), BF),
    pg_got=((4, TOK, WIDTH), BF),
    pg_ring=((3, TOK, WIDTH), BF),
    po_got=((4, TOK, WIDTH), BF),
    po_ring=((3, TOK, WIDTH), BF),
    dgu=((4, 4, 4, 16, 2 * SLICE), BF),
    dgu_x=((3, 4, 4, 16, SLICE), BF),
    dgu_y=((3, 4, 16, SLICE), BF),
    dgv_y=((3, 4, 4, 16, SLICE), BF),
    dgv_x=((3, 4, 16, SLICE), BF),
    dwd=((8, 48, WIDTH), BF),
    dwd_x=((3, 4, 48, WIDTH), BF),
    dwd_y=((3, 48, WIDTH), BF),
    dwd_sum=((2, 24, WIDTH), F32),
    dwd_half=((24, WIDTH), F32),
    dwo_got=((4, 2, 2, 4, 16, WIDTH), BF),
    dwo_z=((3, 2, 2, 4, 16, CUT), BF),
    dwo_y=((3, 2, 2, 16, CUT), BF),
    dwo_x=((3, 16, CUT), BF),
    dwp_y=((3, 4, 2, 2, 16, WIDTH - CUT), BF),
    dwp_z=((3, 2, 2, 16, WIDTH - CUT), BF),
    dwp_x=((3, 16, WIDTH - CUT), BF),
    grad_resid=((TOK, WIDTH), F32),
    gh_pair=((8, TOK, 2 * HEAD), BF),
    gh_all=((8, 2, TOK, HEAD), BF),
    dk=((4, WIDE, HEAD), F32),
    dv=((4, WIDE, HEAD), F32),
    swap_got=((4, 2, 2, TOK, HEAD), BF),
    dq=((2, WIDE, HEAD), F32),
    p_x=((TOK, WIDTH // 2), BF),
    p_x_src=((TOK, WIDTH // 2), BF),
    dw=((2 * HEAD, WIDTH), F32),
    dw_low=((2 * HEAD, WIDTH), BF),
    dw_got=((3, 2 * HEAD, 2 * TOK), BF),
    dw_mid=((2, 2 * HEAD, TOK), BF),
    dw_xl=((2 * HEAD, TOK), BF),
    hg=((8, 128), F32),
    hg_near=((8, 128), F32),
    hg_two=((8, 128), F32),
    hg_got=((7, 8, 128), F32),
    hg_mid=((8, 128), F32),
    hg_dp=((7, 8, 128), F32),
)
INPUTS = ("tok_in", "wqkv_in", "wo_in", "wgu_in", "wd_in", "cot_in", "gains_in", "freq_in", "lengths")
OUTPUTS = dict(
    output=((TOK, WIDTH), F32),
    input_grad=((TOK, WIDTH), F32),
    gain_grads=((8, 128), F32),
    grad_qkv=((8, VALUE_AT + KEY_VALUE_HEADS * HEAD), F32),
    grad_out=((16, WIDTH), F32),
    grad_up=((8, 2 * FF), F32),
    grad_down=((24, WIDTH), F32),
)
SEMS = 180
VMEM_LIMIT = 60 * MIB


def body(*refs):
    names = list(INPUTS) + list(OUTPUTS) + list(BUFFERS) + ["send", "recv"]
    r = types.SimpleNamespace(**dict(zip(names, refs, strict=True)))
    me = tuple(lax.axis_index(a) for a in AXES)
    z, xl, xh, y, c = me
    chip = xh * 4 + y
    mine, here = ctx_of(me), dp_of(me)
    over = moved(me, SIBLING)
    net = Net(r.send, r.recv)

    own_wo = (z, xl, xh, y, c)
    loads = [
        net.local(r.wqkv_in, r.wqkv),
        net.local(r.gains_in, r.gains),
        net.local(r.wgu_in, r.wgu),
        net.local(r.wd_in, r.wd),
        net.local(r.tok_in, r.tok),
        net.local(r.wo_in, r.wo_all.at[own_wo]),
        net.local(r.freq_in, r.freq),
        net.local(r.cot_in, r.cot_all.at[z, c]),
    ]
    barrier = pltpu.get_barrier_semaphore()
    for o in PEERS:
        pl.semaphore_signal(barrier, inc=1, device_id=moved(me, o), device_id_type=BY_MESH)
    for copy in loads:
        copy.wait()

    w = r.wqkv[...].astype(F32)
    for j in range(16):
        extra = (KEY_AT, VALUE_AT)[j % 2] + j // 2 * HEAD
        r.wq_src[j // 2, j % 2, :, :HEAD] = w[:, j * HEAD : (j + 1) * HEAD]
        r.wq_src[j // 2, j % 2, :, HEAD:] = w[:, extra : extra + HEAD]
    w = r.wgu[...].astype(F32)
    for j in range(8):
        r.gu_src[j // 2, j % 2, :, :SLICE] = w[:, j * SLICE : (j + 1) * SLICE]
        r.gu_src[j // 2, j % 2, :, SLICE:] = w[:, FF + j * SLICE : FF + (j + 1) * SLICE]
    r.wd_src[...] = r.wd[...].astype(F32)
    r.wq_pair[:, c] = r.wq_src[:, c]
    r.gu_pair[:, c] = r.gu_src[:, c]
    r.g_pair[c] = r.gains[...]
    r.wd_tmp[c] = r.wd_src[...]
    r.x_all[mine] = r.tok[...]
    pl.semaphore_wait(barrier, len(PEERS))

    small = [
        net.put(r.wq_src.at[:, 1 - c], r.wq_pair.at[:, c], over),
        net.put(r.gains, r.g_pair.at[c], over),
        net.put(r.gu_src.at[:, 1 - c], r.gu_pair.at[:, c], over),
        net.put(r.wd_src, r.wd_tmp.at[c], over),
    ]
    wo_own = r.wo_all.at[own_wo]
    wo_x = net.put_all(
        [(wo_own, wo_own, moved(me, o)) for o in X_PEERS], r.wo_all.at[0, 0, 0, pl.ds(0, 3), 0]
    )
    at = r.cot_all.at[z, c]
    cot_z = [net.put(at, at, moved(me, o)) for o in Z_PEERS[:2]]
    arrived(small)
    w_ctx = net.put_all(
        [(r.wq_pair.at[chip_of(to)], r.wq_tmp.at[chip], to) for to in (moved(me, o) for o in CTX)],
        r.wq_tmp.at[pl.ds(0, 7)],
    )
    g_ctx = net.put_all(
        [(r.g_pair, r.g_tmp.at[chip], moved(me, o)) for o in CTX], r.g_tmp.at[pl.ds(0, 7)]
    )
    gu_z = net.put_all(
        [(r.gu_pair.at[to[0]], r.gu_tmp.at[z], to) for to in (moved(me, o) for o in Z_PEERS)],
        r.gu_tmp.at[pl.ds(0, 3)],
    )
    r.wq_tmp[chip] = r.wq_pair[chip]
    r.g_tmp[chip] = r.g_pair[...]
    r.gu_tmp[z] = r.gu_pair[z]
    wd_sems = net.take(3)

    @pl.when(xl == c)
    def _():
        r.wd_all[xh, y] = r.wd_tmp[...].reshape(48, WIDTH).astype(BF)
        for k, o in enumerate(Y_PEERS):
            at = r.wd_all.at[xh, y]
            net.copy(at, at, moved(me, o), wd_sems + k, wd_sems + k).start()

    tok_x = net.put(r.tok, r.x_all.at[mine], moved(me, X_HALF))
    tok_y = [net.put(r.tok, r.x_all.at[mine], moved(me, o)) for o in Y_PEERS]
    tok_own = net.put(r.tok, r.x_all.at[mine], over)
    at = r.cot_all.at[z, c]
    cot_near = [net.put(at, at, over)]

    ends, starts = [], []
    total = 0
    for d in range(8):
        starts.append(total)
        total = total + r.lengths[0, d]

    def begin_of(index):
        out = jnp.zeros_like(index)
        for s in starts[1:]:
            out = jnp.where(index >= s, s, out)
        return out

    def pass_on(ref, at):
        return net.put(ref.at[at], ref.at[at], over)

    def same(ref, peers, total):
        return net.put_all([(ref, ref, moved(me, o)) for o in peers], total)

    first, last = slice(0, WIDTH // 2), slice(WIDTH // 2, WIDTH)
    left, right = slice(0, SLICE), slice(SLICE, 2 * SLICE)
    wo_x.wait_recv()
    wo_y = same(r.wo_all.at[z, :, :, y, c], Y_PEERS, r.wo_all.at[pl.ds(0, 3), :, :, 0, 0])
    gu_z.wait_recv()
    r.gu_low[...] = r.gu_tmp[...].reshape(4, 16, 2 * SLICE).astype(BF)
    r.gu_all[:, xl, xh, y] = r.gu_low[...]
    gu_y = net.put_all(
        [
            (r.gu_low.at[:, :, left], r.gu_all.at[:, xl, xh, y, :, left], moved(me, o))
            for o in Y_PEERS
        ],
        r.gu_all.at[:, 0, 0, pl.ds(0, 3), :, left],
    )
    gu_x = net.put_all(
        [
            (r.gu_low.at[:, :, right], r.gu_all.at[:, xl, xh, y, :, right], moved(me, o))
            for o in X_PEERS
        ],
        r.gu_all.at[:, 0, 0, pl.ds(0, 3), :, right],
    )

    w_ctx.wait_recv()
    r.w_low[...] = r.wq_tmp[...].reshape(TOK, 2 * HEAD).astype(BF)
    w_xl = net.put(r.w_low, r.w_all.at[here], moved(me, X_LOW))
    g_ctx.wait_recv()
    r.g_row[...] = r.g_tmp[:, :, 0, :].reshape(16, 128)
    g_dp = net.put_all(
        [(r.g_row, r.g_all.at[here], moved(me, o)) for o in DP_ALL], r.g_all.at[pl.ds(0, 7)]
    )
    r.w_all[here] = r.w_low[...]
    r.g_all[here] = r.g_row[...]

    low = lax.broadcasted_iota(jnp.int32, (BLOCK, HEAD), 1) < HEAD // 2
    shift = jnp.where(low, 0.0, 0.5 * math.pi)

    @pl.loop(0, 8)
    def _(n):
        index = n * BLOCK + lax.broadcasted_iota(jnp.int32, (BLOCK, HEAD), 0)
        phase = (index - begin_of(index)).astype(F32) * r.freq[...]
        r.angle[n] = jnp.cos(phase - shift)
        document = jnp.zeros_like(index)
        for s in starts[1:]:
            document = document + (index >= s).astype(jnp.int32)
        place = lax.broadcasted_iota(jnp.int32, (BLOCK, HEAD), 1)
        same_doc = jnp.where(document == place, 1.0, 0.0)
        r.q[n, :, HEAD:] = jnp.where(place == 8, 1.0, same_doc).astype(BF)
        r.k[n, :, HEAD:] = jnp.where(place == 8, -FAR, FAR * same_doc).astype(BF)

    def angles(n):
        both = r.angle[n]
        other = turned(both)
        return jnp.where(low, both, other), jnp.where(low, -other, both)

    w_xl.wait_recv()
    w_z = same(r.w_all.at[pl.ds(2 * z, 2)], Z_PEERS, r.w_all.at[pl.ds(0, 6)])
    tok_x.wait_recv()
    at_x = ctx_of(before(me, X_HALF))
    near = {(1, 0): pass_on(r.x_all, at_x)}
    at = r.x_all.at[at_x, :, first]
    tok_xy = [net.put(at, at, moved(me, o)) for o in Y_PEERS]
    tok_yx = []
    for o, copy in zip(Y_PEERS, tok_y):
        copy.wait_recv()
        source = ctx_of(before(me, o))
        at = r.x_all.at[source, :, last]
        tok_yx.append(net.put(at, at, moved(me, X_HALF)))
        near[(0, o[3])] = pass_on(r.x_all, source)
    cot_far = []
    for k in range(2):
        cot_z[k].wait_recv()
        source = before(me, Z_PEERS[k])[0]
        at = r.cot_all.at[source, c, :, (first, last)[k]]
        cot_far.append(net.put(at, at, moved(me, Z_PEERS[k])))
        cot_near.append(pass_on(r.cot_all, (source, c)))
    wo_y.wait_recv()
    at = r.wo_all.at[z, :, :, :, c]
    wo_z = [net.put(at, at, moved(me, o)) for o in Z_PEERS[:2]]
    wo_near = [net.put(at, at, over)]
    gu_y.wait_recv()
    gu_x.wait_recv()
    gu_yx = same(r.gu_all.at[:, xl, xh, :, :, left], X_PEERS, r.gu_all.at[pl.ds(0, 3), :, :, :, :, left])
    gu_xy = same(r.gu_all.at[:, :, :, y, :, right], Y_PEERS, r.gu_all.at[pl.ds(0, 3), :, :, :, :, right])
    wdx_sems = net.take(3)

    @pl.when(xl == c)
    def _():
        at = r.wd_all.at[xh, y]
        for k, o in enumerate(Y_PEERS):
            net.copy(at, at, moved(me, o), wd_sems + k, wd_sems + k).wait_recv()
        at = r.wd_all.at[xh]
        for k, o in enumerate(X_PEERS):
            net.copy(at, at, moved(me, o), wdx_sems + k, wdx_sems + k).start()

    w_z.wait_recv()
    w_near = net.put(r.w_all.at[:, :, HEAD:], r.w_got, over)
    g_dp.wait_recv()
    gains = r.g_all[...].reshape(128, 128).astype(BF)
    dev = lax.broadcasted_iota(jnp.int32, (128, WIDTH), 0)
    lane = lax.broadcasted_iota(jnp.int32, (128, WIDTH), 1)
    spread = t_dot(gains, (lane // 8 == dev).astype(F32).astype(BF))
    pick = lax.broadcasted_iota(jnp.int32, (8, WIDTH), 1) % 8 == lax.broadcasted_iota(
        jnp.int32, (8, WIDTH), 0
    )
    r.gain_one[...] = jnp.sum(jnp.where(pick, spread[:8], 0.0), 0, keepdims=True)
    r.gain_two[...] = jnp.sum(jnp.where(pick, spread[8:16], 0.0), 0, keepdims=True)
    eye = lax.broadcasted_iota(jnp.int32, (128, 128), 0) == lax.broadcasted_iota(
        jnp.int32, (128, 128), 1
    )
    spread = t_dot(gains, eye.astype(F32).astype(BF))
    r.gain_q[...] = spread[16:17]
    r.gain_k[...] = spread[17:18]
    w_near.wait_recv()

    def project(n):
        inputs = r.x_all[pl.ds(2 * n, 2)].reshape(BLOCK, WIDTH).astype(F32)
        first_in = (inputs * inverse_root(inputs) * r.gain_one[...]).astype(BF)
        projected = dot(first_in, r.w_all[...].reshape(WIDTH, 2 * HEAD))
        second = dot(first_in, r.w_got[...].reshape(WIDTH, HEAD))
        q_un, own = projected[:, :HEAD], projected[:, HEAD:]
        k_un = jnp.where(c == 0, own, second)
        value = jnp.where(c == 0, second, own)
        r.v[n] = value.astype(BF)
        r.v_turned[n] = value.T.astype(BF)
        r.q_un[n] = q_un
        r.k_un[n] = k_un
        cosine, sine = angles(n)
        q = q_un * inverse_root(q_un) * r.gain_q[...]
        r.q[n, :, :HEAD] = ((q * cosine + turned(q) * sine) * SCALE2).astype(BF)
        key = k_un * inverse_root(k_un) * r.gain_k[...]
        key = key * cosine + turned(key) * sine
        r.k[n, :, :HEAD] = key.astype(BF)
        r.k_turned[n] = key.T.astype(BF)

    tok_own.wait_recv()
    project(chip)
    waiting = [(1, 0)]

    def next_project():
        a, b = waiting.pop(0)
        near[(a, b)].wait_recv()
        project(chip_of(before(me, (0, 0, a, b, 0))))

    for o in Y_PEERS:
        next_project()
        waiting.append((0, o[3]))
    for o, one, two in zip(Y_PEERS, tok_xy, tok_yx):
        one.wait_recv()
        two.wait_recv()
        key = (1, o[3])
        near[key] = pass_on(r.x_all, ctx_of(before(me, (0, 0, 1, o[3], 0))))
        next_project()
        waiting.append(key)
    next_project()
    def causal(size):
        keys = lax.broadcasted_iota(jnp.int32, (size, size), 0)
        return keys <= lax.broadcasted_iota(jnp.int32, (size, size), 1)

    wo_far = []

    def wo_on(k):
        wo_z[k].wait_recv()
        source = before(me, Z_PEERS[k])[0]
        at = r.wo_all.at[source, :, :, :, c, :, (first, last)[k]]
        wo_far.append(net.put(at, at, moved(me, Z_PEERS[k])))
        at = r.wo_all.at[source, :, :, :, c]
        wo_near.append(net.put(at, at, over))

    att_send = net.take(8)
    att_near = []

    def att_copy(i):
        return net.copy(
            r.att_pair.at[i],
            r.att_all.at[:, columns(chip, 2 * HEAD)],
            (z, xl, i // 4, i % 4, c),
            att_send + i,
            att_send + chip,
        )

    def send_pair(i):
        for copy in att_near[i]:
            copy.wait_recv() if copy is att_near[i][0] else copy.wait()

        @pl.when(chip != i)
        def _():
            att_copy(i).start()

    for i in range(8):
        q = r.q[i]
        rows = jnp.zeros((1, BLOCK), F32)
        acc = jnp.zeros((HEAD, BLOCK), F32)
        for b in range(i + 1):
            e = jnp.exp2(dot_t(r.k[b], q))
            if b == i:
                e = jnp.where(causal(BLOCK), e, 0.0)
            rows = rows + jnp.sum(e, 0, keepdims=True)
            acc = acc + dot(r.v_turned[b], e.astype(BF))
        norm = 1.0 / rows
        acc = acc * norm
        r.full[i] = acc
        r.norm[i] = norm
        r.att[i] = acc.T.astype(BF).reshape(2, TOK, HEAD)
        att_near.append(
            (
                net.put(r.att.at[i, 1 - c], r.att_pair.at[i, :, columns(c)], over),
                net.local(r.att.at[i, c], r.att_pair.at[i, :, columns(c)]),
            )
        )
        if i:
            send_pair(i - 1)
        if i in (6, 7):
            wo_on(i - 6)
    send_pair(7)
    keep = net.local(r.att_pair.at[chip], r.att_all.at[:, columns(chip, 2 * HEAD)])
    far = lax.rem(z + 2, 4)
    arrived(wo_far)
    at = r.wo_all.at[far, :, :, :, c]
    wo_near.append(net.put(at, at, over))
    for o in CTX:
        k = att_send + chip_of(before(me, o))
        net.copy(r.att_pair.at[0], r.att_pair.at[0], over, k, k).wait_recv()
    keep.wait()
    arrived(wo_near)

    inputs = r.tok[...].astype(F32)
    residual = inputs + dot(r.att_all[...], r.wo_all[...].reshape(QUERY_HEADS * HEAD, WIDTH))
    r.resid[...] = residual
    inverse_two = inverse_root(residual)
    r.s_all[z, c] = (residual * inverse_two * r.gain_two[...]).astype(BF)
    s_mine = r.s_all.at[z, c]
    s_near = {0: net.put(s_mine, s_mine, over)}
    s_z = [net.put(s_mine, s_mine, moved(me, o)) for o in Z_PEERS[:2]]

    arrived(cot_far)
    cot_near.append(pass_on(r.cot_all, (far, c)))
    arrived([gu_yx, gu_xy] + cot_near)
    at = r.wd_all.at[0]

    @pl.when(xl == c)
    def _():
        net.copy(at, at, over, wdx_sems, wdx_sems + X_PEERS.index(X_HALF)).wait_recv()

    @pl.when(xl != c)
    def _():
        for k, o in enumerate(X_PEERS):
            if o != X_HALF:
                net.copy(at, at, over, wdx_sems, wdx_sems + k).wait_recv()

    def feed_forward(n):
        w_gu = r.gu_all[...].reshape(WIDTH, 2 * SLICE)
        gu = dot(r.s_all[n].reshape(BLOCK, WIDTH), w_gu)
        grad_hidden = dot_t(r.cot_all[n].reshape(BLOCK, WIDTH), r.wd_all[...].reshape(SLICE, WIDTH))
        gate, up = gu[:, :SLICE], gu[:, SLICE:]
        sigma = 1.0 / (1.0 + jnp.exp(-gate))
        swish = gate * sigma
        r.hidden[n] = (swish * up).astype(BF)
        grad_gate = grad_hidden * up * sigma * (1.0 + gate * (1.0 - sigma))
        grad_gu = jnp.concatenate([grad_gate, grad_hidden * swish], 1).astype(BF)
        r.grad_gu[n] = grad_gu
        r.pg[n] = dot_t(grad_gu, w_gu).astype(BF).reshape(2, TOK, WIDTH)
        return net.put(r.pg.at[n, 1 - c], r.pg_got.at[n], over)

    pg_near, pg_ring = {}, []

    def mix(n, got):
        r.pg_got[n] = (r.pg[n, c].astype(F32) + r.pg_got[n].astype(F32)).astype(BF)

    def send_mixed(k):
        o = Z_PEERS[k]
        to = moved(me, o)
        pg_near[k].wait_recv()
        mix(to[0], None)
        pg_ring.append(net.put(r.pg_got.at[to[0]], r.pg_ring.at[k], to))

    s_near[0].wait_recv()
    pg_own = feed_forward(z)
    s_far = []
    for k in range(2):
        s_z[k].wait_recv()
        source = before(me, Z_PEERS[k])[0]
        s_near[k + 1] = pass_on(r.s_all, (source, c))
        at = r.s_all.at[source, c, :, (first, last)[k]]
        s_far.append(net.put(at, at, moved(me, Z_PEERS[k])))
    for k in range(2):
        s_near[k + 1].wait_recv()
        pg_near[1 - k] = feed_forward(before(me, Z_PEERS[k])[0])
        if k:
            send_mixed(1)
    arrived(s_far)
    s_near[3] = pass_on(r.s_all, (far, c))
    send_mixed(0)
    s_near[3].wait_recv()
    pg_near[2] = feed_forward(far)
    done = [2]
    send_mixed(done[-1])
    pg_own.wait_recv()
    mix(z, None)

    gone = [pg_own, *pg_near.values(), *pg_ring]
    early = [copy for copy in net.sent if all(copy is not g for g in gone)]
    net.sent = list(pg_ring)
    s_rows = r.s_all[...].reshape(4 * BLOCK, WIDTH)
    grad_gu = r.grad_gu[...].reshape(4 * BLOCK, 2 * SLICE)
    for a in range(4):
        part = t_dot(s_rows[:, a * BLOCK : (a + 1) * BLOCK], grad_gu)
        r.dgu[a] = part.astype(BF).reshape(4, 4, 16, 2 * SLICE)

    def scattered(peers, source, out):
        to = [moved(me, o) for o in peers]
        return net.put_all([(source(t), out.at[k], t) for k, t in enumerate(to)], out)

    dgu_one = scattered(X_PEERS, lambda to: r.dgu.at[:, to[1] * 2 + to[2], :, :, left], r.dgu_x)
    dgu_two = scattered(Y_PEERS, lambda to: r.dgu.at[:, :, to[3], :, right], r.dgv_y)
    hidden = r.hidden[...].reshape(4 * BLOCK, SLICE)
    for a in range(4):
        cols = slice(a * BLOCK, (a + 1) * BLOCK)
        part = t_dot(hidden, r.cot_all[:, :, :, cols].reshape(4 * BLOCK, BLOCK))
        r.dwd[:, :, cols] = part.astype(BF).reshape(8, 48, BLOCK)
    dwd_sems = net.take(3)
    half_at = X_PEERS.index(X_HALF)

    def dwd_copy(k):
        to = moved(me, X_PEERS[k])
        return net.copy(
            r.dwd.at[pl.ds(to[2] * 4, 4)], r.dwd_x.at[k], to, dwd_sems + k, dwd_sems + k
        )

    for copy in [pg_own, *pg_near.values()]:
        copy.wait_send()
    for n in range(4):
        part = dot(r.hidden[n], r.wd_all[...].reshape(SLICE, WIDTH))
        r.pg[n] = part.astype(BF).reshape(2, TOK, WIDTH)
    po_near = net.put(r.pg.at[:, 1 - c], r.po_got, over)

    po_near.wait_recv()

    @pl.loop(0, 4)
    def _(n):
        r.po_got[n] = r.pg[n, c] + r.po_got[n]

    po_ring = scattered(Z_PEERS, lambda to: r.po_got.at[to[0]], r.po_ring)

    arrived(pg_ring)
    grad_second = r.pg_got[z].astype(F32)
    for k in range(3):
        grad_second = grad_second + r.pg_ring[k].astype(F32)
    residual = r.resid[...]
    inverse_two = inverse_root(residual)
    grad_resid = r.cot_all[z, c].astype(F32) + norm_back(
        residual, inverse_two, grad_second * r.gain_two[...]
    )
    r.grad_resid[...] = grad_resid
    resid_low = grad_resid.astype(BF)
    for i in range(8):

        @pl.when(chip != i)
        def _():
            att_copy(i).wait_send()

    for j in range(8):
        part = dot_t(resid_low, r.wo_all[j // 2, j % 2].reshape(BLOCK, WIDTH))
        r.att_pair[j] = part.astype(BF)
    for copy in early:
        copy.wait_send()
    gh = net.put_all(
        [
            (r.att_pair.at[chip_of(to)], r.gh_pair.at[chip], to)
            for to in (moved(me, o) for o in CTX)
        ],
        r.gh_pair.at[pl.ds(0, 7)],
    )
    keep = net.local(r.att_pair.at[chip], r.gh_pair.at[chip])

    for j in range(8):
        part = t_dot(r.att_all[:, j * BLOCK : (j + 1) * BLOCK], resid_low)
        r.wo_all[j // 2, j % 2] = part.astype(BF).reshape(2, 4, 2, 16, WIDTH)
    dwo_near = net.put(r.wo_all.at[:, :, :, :, 1 - c], r.dwo_got, over)
    at_x = xl * 2 + xh
    dgu_one.wait_recv()

    @pl.loop(0, 4)
    def _(a):
        for b in range(4):
            total = r.dgu[a, at_x, b, :, left].astype(F32)
            for k in range(3):
                total = total + r.dgu_x[k, a, b].astype(F32)
            r.dgu_x[0, a, b] = total.astype(BF)

    dgu_two.wait_recv()

    @pl.loop(0, 4)
    def _(a):
        for b in range(4):
            total = r.dgu[a, b, y, :, right].astype(F32)
            for k in range(3):
                total = total + r.dgv_y[k, a, b].astype(F32)
            r.dgv_y[0, a, b] = total.astype(BF)

    dwo_near.wait_recv()

    @pl.loop(0, 16)
    def _(a):
        for b in range(4):
            at = (a // 4, lax.rem(a, 4) // 2, lax.rem(a, 2), b)
            r.dwo_got[at] = r.wo_all[(*at, c)] + r.dwo_got[at]

    more, less = slice(0, CUT), slice(CUT, WIDTH)
    dwo_one = scattered(Z_PEERS, lambda to: r.dwo_got.at[to[0], :, :, :, :, more], r.dwo_z)
    gh.wait_recv()
    keep.wait()
    dgu_one = scattered(Y_PEERS, lambda to: r.dgu_x.at[0, :, to[3]], r.dgu_y)
    dgu_two = scattered(X_PEERS, lambda to: r.dgv_y.at[0, :, to[1] * 2 + to[2]], r.dgv_x)
    dwo_two = scattered(Y_PEERS, lambda to: r.dwo_got.at[:, :, :, to[3], :, less], r.dwp_y)
    @pl.when(xl == c)
    def _():
        dwd_copy(half_at).start()

    @pl.when(xl != c)
    def _():
        for k in range(3):
            if k != half_at:
                dwd_copy(k).start()

    gh_near = net.put(r.gh_pair.at[:, :, columns(1 - c)], r.gh_all.at[:, c], over)
    keep = net.local(r.gh_pair.at[:, :, columns(c)], r.gh_all.at[:, c])
    gh_near.wait_recv()
    keep.wait()

    def pair(ref, n):
        return ref[2 * n : 2 * n + 2].reshape(WIDE, ref.shape[2])

    def beside(ref, n):
        return jnp.concatenate([ref[2 * n], ref[2 * n + 1]], 1)

    swaps = {}

    def attend_back(n):
        q = pair(r.q, n)
        g = r.gh_all[2 * n : 2 * n + 2].reshape(WIDE, HEAD)
        g_turned = (g.T.astype(F32) * beside(r.norm, n)).astype(BF)
        g = g_turned.T
        inner = jnp.sum(g_turned.astype(F32) * beside(r.full, n), 0, keepdims=True)
        acc = jnp.zeros((HEAD, WIDE), F32)
        for b in range(n + 1):
            key = pair(r.k, b)
            e = jnp.exp2(dot_t(key, q))
            if b == n:
                e = jnp.where(causal(WIDE), e, 0.0)
            dp = dot(pair(r.v, b), g_turned)
            ds = (e * (dp - inner)).astype(BF)
            dv, dk = dot(e.astype(BF), g), dot(ds, q[:, :HEAD])
            r.dv[b] = dv if n == 3 else r.dv[b] + dv
            r.dk[b] = dk if n == 3 else r.dk[b] + dk
            acc = acc + dot(beside(r.k_turned, b), ds)
        r.dq[n % 2] = (acc * SCALE).T
        r.dk[n] = r.dk[n] * LN2
        sent = jnp.where(c == 0, r.dv[n], r.dk[n]).astype(BF)
        r.att[2 * n : 2 * n + 2] = sent.reshape(2, 2, TOK, HEAD)
        swaps[n] = net.put(r.att.at[pl.ds(2 * n, 2)], r.swap_got.at[n], over)

    p_near = {}
    r.dw[...] = jnp.zeros_like(r.dw)
    r.hg[...] = jnp.zeros_like(r.hg)

    def project_back(n):
        swaps[n].wait_recv()
        for half in range(2):
            m = 2 * n + half
            rows = slice(half * BLOCK, (half + 1) * BLOCK)
            inputs = r.x_all[2 * m : 2 * m + 2].reshape(BLOCK, WIDTH).astype(F32)
            first_in = (inputs * inverse_root(inputs) * r.gain_one[...]).astype(BF)
            cosine, sine = angles(m)
            dq, q_part = head_back(r.q_un[m], r.dq[n % 2, rows], cosine, sine, r.gain_q[...])
            both = jnp.where(c == 0, r.dk[n, rows], r.dv[n, rows])
            both = both + r.swap_got[n, half].reshape(BLOCK, HEAD).astype(F32)
            dk, k_part = head_back(r.k_un[m], both, cosine, sine, r.gain_k[...])
            grad = jnp.concatenate([dq, jnp.where(c == 0, dk, both)], 1).astype(BF)
            r.hg[0:1] += q_part
            r.hg[1:2] += jnp.where(c == 0, k_part, 0.0)
            r.dw[...] += t_dot(grad, first_in)
            part = dot_t(grad, r.w_all[...].reshape(WIDTH, 2 * HEAD))
            r.x_all[2 * m : 2 * m + 2] = part.astype(BF).reshape(2, TOK, WIDTH)
            p_near[m] = net.put(r.x_all.at[2 * m + 1 - c], r.s_all.at[m // 2, m % 2], over)

    p_sems, r_sems = net.take(8), net.take(8)

    def p_copy(m):
        return net.copy(
            r.s_all.at[m // 2, m % 2, :, first],
            r.cot_all.at[y, m // 4, :, first],
            (z, xl, xh, m % 4, c),
            p_sems + m,
            p_sems + (m // 4) * 4 + y,
        )

    def r_copy(m):
        return net.copy(
            r.s_all.at[m // 2, m % 2, :, last],
            r.cot_all.at[m % 4, 0, :, last],
            (z, xl, m // 4, y, c),
            r_sems + m,
            r_sems + m % 4,
        )

    def send_parts(n):
        for m in (2 * n, 2 * n + 1):
            p_near[m].wait_recv()
            r.s_all[m // 2, m % 2] = r.x_all[2 * m + c] + r.s_all[m // 2, m % 2]

            @pl.when(y != m % 4)
            def _():
                p_copy(m).start()

            @pl.when(y == m % 4)
            def _():
                r.cot_all[m % 4, m // 4, :, first] = r.s_all[m // 2, m % 2, :, first]

            @pl.when(xh != m // 4)
            def _():
                r_copy(m).start()

    def paired(source, pair):
        copy = net.put(source.at[:, 1 - c], pair.at[:, c], over)
        pair[:, c] = source[:, c]
        return copy

    def dealt(copy, pair, got, peers, index):
        copy.wait_recv()
        got[index(me)] = pair[index(me)]
        to = [moved(me, o) for o in peers]
        return net.put_all(
            [(pair.at[index(t)], got.at[index(me)], t) for t in to], got.at[pl.ds(0, len(peers))]
        )

    def wait_left(half):
        for o in Y_PEERS:
            k = p_sems + half * 4 + before(me, o)[3]
            net.copy(r.p_x_src, r.p_x, over, k, k).wait_recv()

    def sum_left(half):
        total = r.cot_all[0, half, :, first].astype(F32)
        for b in range(1, 4):
            total = total + r.cot_all[b, half, :, first].astype(F32)
        return total

    def sum_right(b):
        at = xh * 2 + b // 2
        return r.s_all[at, lax.rem(b, 2), :, last].astype(F32) + r.cot_all[b, 0, :, last].astype(F32)

    attend_back(3)
    attend_back(2)
    project_back(3)
    attend_back(1)
    send_parts(3)
    project_back(2)
    attend_back(0)
    send_parts(2)
    project_back(1)
    send_parts(1)
    project_back(0)
    r.dw_low[...] = r.dw[...].astype(BF)
    dw_z = scattered(Z_PEERS, lambda to: r.dw_low.at[:, columns(to[0], 2 * TOK)], r.dw_got)
    send_parts(0)
    hg_near = net.put(r.hg, r.hg_near, over)
    hg_near.wait_recv()
    r.hg_two[...] = r.hg[...] + r.hg_near[...]
    hg_ctx = scattered(CTX, lambda to: r.hg_two, r.hg_got)

    dwo_one.wait_recv()

    @pl.loop(0, 4)
    def _(a):
        for b in range(4):
            at = (a // 2, lax.rem(a, 2), b)
            total = r.dwo_got[(z, *at, slice(None), more)].astype(F32)
            for k in range(3):
                total = total + r.dwo_z[(k, *at)].astype(F32)
            r.dwo_z[(0, *at)] = total.astype(BF)

    dwo_one = scattered(Y_PEERS, lambda to: r.dwo_z.at[0, :, :, to[3]], r.dwo_y)
    dwo_two.wait_recv()

    @pl.loop(0, 4)
    def _(a):
        for b in range(4):
            at = (a, b // 2, b % 2)
            total = r.dwo_got[(*at, y, slice(None), less)].astype(F32)
            for k in range(3):
                total = total + r.dwp_y[(k, *at)].astype(F32)
            r.dwp_y[(0, *at)] = total.astype(BF)

    dwo_two = scattered(Z_PEERS, lambda to: r.dwp_y.at[0, to[0]], r.dwp_z)

    dwdy_sems = net.take(4)

    def dwdy_copy(k):
        to = moved(me, Y_PEERS[k])
        return net.copy(r.dwd_x.at[0, to[3]], r.dwd_y.at[k], to, dwdy_sems + k, dwdy_sems + k)

    @pl.when(xl == c)
    def _():
        for k in range(3):
            dwd_copy(k).wait_recv()
        for b in range(4):
            total = r.dwd[xh * 4 + b].astype(F32)
            for k in range(3):
                total = total + r.dwd_x[k, b].astype(F32)
            r.dwd_x[0, b] = total.astype(BF)
        for k in range(3):
            dwdy_copy(k).start()

    dgu_one.wait_recv()
    dgu_two.wait_recv()
    for a in range(4):
        one = r.dgu_x[0, a, y].astype(F32)
        two = r.dgv_y[0, a, at_x].astype(F32)
        for k in range(3):
            one = one + r.dgu_y[k, a].astype(F32)
            two = two + r.dgv_x[k, a].astype(F32)
        r.gu_src[a, :, :, left] = one.reshape(2, 8, SLICE)
        r.gu_src[a, :, :, right] = two.reshape(2, 8, SLICE)
    dgu_near = paired(r.gu_src, r.gu_pair)

    wait_left(1 - xh)
    r.p_x_src[...] = sum_left(1 - xh).astype(BF)
    p_x = net.put(r.p_x_src, r.p_x, moved(me, X_HALF))
    for b in range(4):
        net.copy(r.p_x_src, r.p_x, over, r_sems + b, r_sems + b).wait_recv()
    for o in Y_PEERS:
        b = moved(me, o)[3]
        r.cot_all[b, 0, :, last] = sum_right(b).astype(BF)
    r_y = scattered(
        Y_PEERS, lambda to: r.cot_all.at[to[3], 0, :, last], r.cot_all.at[pl.ds(0, 3), 1, :, last]
    )

    dw_z.wait_recv()
    total = r.dw_low[:, columns(z, 2 * TOK)].astype(F32)
    for k in range(3):
        total = total + r.dw_got[k].astype(F32)
    r.dw_mid[0] = total[:, :TOK].astype(BF)
    r.dw_mid[1] = total[:, TOK:].astype(BF)
    dw_xl = net.put(r.dw_mid.at[1 - xl], r.dw_xl, moved(me, X_LOW))

    dgu_z = dealt(dgu_near, r.gu_pair, r.gu_tmp, Z_PEERS, lambda at: at[0])
    dwo_one.wait_recv()
    for b in range(4):
        at = (b // 2, b % 2)
        total = r.dwo_z[(0, *at, y)].astype(F32)
        for k in range(3):
            total = total + r.dwo_y[(k, *at)].astype(F32)
        r.dwo_y[(0, *at)] = total.astype(BF)
    dwo_one = scattered(X_PEERS, lambda to: r.dwo_y.at[0, to[1], to[2]], r.dwo_x)
    dwo_two.wait_recv()
    for b in range(4):
        at = (b // 2, b % 2)
        total = r.dwp_y[(0, z, *at)].astype(F32)
        for k in range(3):
            total = total + r.dwp_z[(k, *at)].astype(F32)
        r.dwp_z[(0, *at)] = total.astype(BF)
    dwo_two = scattered(X_PEERS, lambda to: r.dwp_z.at[0, to[1], to[2]], r.dwp_x)

    dw_xl.wait_recv()
    total = r.dw_mid[xl].astype(F32) + r.dw_xl[...].astype(F32)
    r.wq_src[...] = total.T.reshape(8, 2, 8, 2 * HEAD)
    dw_near = paired(r.wq_src, r.wq_pair)
    dw_ctx = dealt(dw_near, r.wq_pair, r.wq_tmp, CTX, chip_of)

    hg_ctx.wait_recv()
    total = r.hg_two[...]
    for k in range(7):
        total = total + r.hg_got[k]
    r.hg_mid[...] = total
    hg_dp = scattered(DP_ALL, lambda to: r.hg_mid, r.hg_dp)

    def half_copy():
        return net.copy(r.dwd_sum.at[1 - c], r.dwd_half, over, dwdy_sems + 3, dwdy_sems + 3)

    @pl.when(xl == c)
    def _():
        for k in range(3):
            dwdy_copy(k).wait_recv()
        total = r.dwd_x[0, y].astype(F32)
        for k in range(3):
            total = total + r.dwd_y[k].astype(F32)
        r.dwd_sum[0] = total[:24]
        r.dwd_sum[1] = total[24:]
        half_copy().start()
        r.dwd_out[...] = r.dwd_sum[c]

    po_ring.wait_recv()
    total = r.resid[...] + r.po_got[z].astype(F32)
    for k in range(3):
        total = total + r.po_ring[k].astype(F32)
    r.resid[...] = total
    outs = [net.local(r.resid, r.output)]

    wait_left(xh)
    p_x.wait_recv()
    total = sum_left(xh) + r.p_x[...].astype(F32)
    r_y.wait_recv()
    other = sum_right(y)
    for k in range(3):
        other = other + r.cot_all[k, 1, :, last].astype(F32)
    total = jnp.concatenate([total, other], 1)
    inputs = r.tok[...].astype(F32)
    r.grad_resid[...] += norm_back(
        inputs, inverse_root(inputs), total * r.gain_one[...]
    )
    outs.append(net.local(r.grad_resid, r.input_grad))

    dwo_one.wait_recv()
    total = r.dwo_y[0, xl, xh].astype(F32)
    for k in range(3):
        total = total + r.dwo_x[k].astype(F32)
    r.dwo_out[:, more] = total
    dwo_two.wait_recv()
    total = r.dwp_z[0, xl, xh].astype(F32)
    for k in range(3):
        total = total + r.dwp_x[k].astype(F32)
    r.dwo_out[:, less] = total
    outs.append(net.local(r.dwo_out, r.grad_out))

    @pl.when(xl != c)
    def _():
        half_copy().wait_recv()
        r.dwd_out[...] = r.dwd_half[...]

    outs.append(net.local(r.dwd_out, r.grad_down))
    dgu_z.wait_recv()
    for j in range(8):
        r.dgu_out[:, j * SLICE : (j + 1) * SLICE] = r.gu_tmp[j // 2, j % 2, :, :SLICE]
        r.dgu_out[:, FF + j * SLICE : FF + (j + 1) * SLICE] = r.gu_tmp[j // 2, j % 2, :, SLICE:]
    outs.append(net.local(r.dgu_out, r.grad_up))
    lane = lax.broadcasted_iota(jnp.int32, (8, 128), 1)
    row = lax.broadcasted_iota(jnp.int32, (8, 128), 0)

    def picked(values, at):
        return jnp.sum(jnp.where(lane == at, values, 0.0), 1, keepdims=True)

    two = jnp.sum(r.dgu_out[...] * r.wgu[...].astype(F32), 1, keepdims=True)
    two = two / picked(r.gains[...], row + 8)
    dw_ctx.wait_recv()
    for j in range(16):
        extra = (KEY_AT, VALUE_AT)[j % 2] + j // 2 * HEAD
        r.dwq_out[:, j * HEAD : (j + 1) * HEAD] = r.wq_tmp[j // 2, j % 2, :, :HEAD]
        r.dwq_out[:, extra : extra + HEAD] = r.wq_tmp[j // 2, j % 2, :, HEAD:]
    outs.append(net.local(r.dwq_out, r.grad_qkv))
    one = jnp.sum(r.dwq_out[...] * r.wqkv[...].astype(F32), 1, keepdims=True)
    one = one / picked(r.gains[...], row)
    hg_dp.wait_recv()
    total = r.hg_mid[...]
    for k in range(7):
        total = total + r.hg_dp[k]
    heads = picked(total, here * 16 + mine)
    r.gains_out[...] = jnp.where(lane == 0, one, jnp.where(lane == 1, two, heads))
    outs.append(net.local(r.gains_out, r.gain_grads))

    for m in range(8):

        @pl.when(y != m % 4)
        def _():
            p_copy(m).wait_send()

        @pl.when(xh != m // 4)
        def _():
            r_copy(m).wait_send()

    @pl.when(xl == c)
    def _():
        for k, o in enumerate(Y_PEERS):
            at = r.wd_all.at[xh, y]
            net.copy(at, at, over, wd_sems + k, wd_sems + k).wait_send()
        for k, o in enumerate(X_PEERS):
            at = r.wd_all.at[xh]
            net.copy(at, at, over, wdx_sems + k, wdx_sems + k).wait_send()
        dwd_copy(half_at).wait_send()
        for k in range(3):
            dwdy_copy(k).wait_send()
        half_copy().wait_send()

    @pl.when(xl != c)
    def _():
        for k in range(3):
            if k != half_at:
                dwd_copy(k).wait_send()

    net.drain()
    for copy in outs:
        copy.wait()


def finish(*refs):
    ins, gains, outs = refs[:6], refs[6], refs[7:13]
    (attn, q, k, mlp), held, sems = refs[13:17], refs[17:23], refs[23]
    for i in range(6):
        pltpu.make_async_copy(ins[i], held[i], sems.at[i]).start()
    for i in range(8):
        attn[i] = gains[i, 0]
        mlp[i] = gains[i, 1]
    q[0] = gains[0, 2]
    k[0] = gains[1, 2]
    for i in range(6):
        pltpu.make_async_copy(ins[i], held[i], sems.at[i]).wait()
        pltpu.make_async_copy(held[i], outs[i], sems.at[i]).start()
    for i in range(6):
        pltpu.make_async_copy(held[i], outs[i], sems.at[i]).wait()


def on_device(
    tokens, lengths, attn_gain, q_gain, k_gain, qkv, w_out, mlp_gain, w_gate_up, w_down, cotangent
):
    gains = jnp.concatenate([attn_gain, mlp_gain, q_gain, k_gain]).astype(F32)
    gains = jnp.broadcast_to(jnp.pad(gains, (0, 128 - 18))[None], (8, 128))
    half = np.arange(HEAD // 2, dtype=np.float32) * np.float32(2.0 / HEAD)
    freq = np.float32(THETA) ** (-half)
    freq = jnp.asarray(np.concatenate([freq, freq])[None].astype(np.float32))
    hbm, smem = pl.BlockSpec(memory_space=pl.ANY), pl.BlockSpec(memory_space=pltpu.SMEM)
    outs = pl.pallas_call(
        body,
        name="layer",
        out_shape=tuple(jax.ShapeDtypeStruct(s, d) for s, d in OUTPUTS.values()),
        in_specs=[hbm] * 8 + [smem],
        out_specs=(hbm,) * len(OUTPUTS),
        scratch_shapes=[pltpu.VMEM(s, d) for s, d in BUFFERS.values()]
        + [pltpu.SemaphoreType.DMA((SEMS,))] * 2,
        compiler_params=pltpu.CompilerParams(
            collective_id=1, has_side_effects=True, vmem_limit_bytes=VMEM_LIMIT
        ),
    )(tokens, qkv, w_out, w_gate_up, w_down, cotangent, gains, freq, lengths)
    o = dict(zip(OUTPUTS, outs))
    wide = [o[n] for n in ("output", "input_grad", "grad_qkv", "grad_out", "grad_up", "grad_down")]
    small = [jax.ShapeDtypeStruct((n,), F32) for n in (8, 1, 1, 8)]
    done = pl.pallas_call(
        finish,
        name="finish",
        out_shape=tuple(jax.ShapeDtypeStruct(a.shape, F32) for a in wide) + tuple(small),
        in_specs=[hbm] * 6 + [smem],
        out_specs=(hbm,) * 6 + (smem,) * 4,
        scratch_shapes=[pltpu.VMEM(a.shape, F32) for a in wide] + [pltpu.SemaphoreType.DMA((6,))],
    )(*wide, o["gain_grads"])
    output, input_grad, grad_qkv, grad_out, grad_up, grad_down, attn, q, k, mlp = done
    return output, input_grad, attn, q, k, grad_qkv, grad_out, mlp, grad_up, grad_down


def solution(mesh):
    torus = Mesh(mesh.devices.reshape(SIZES), AXES)
    rows, line = P(AXES, None), P(AXES)
    return jax.shard_map(
        on_device,
        mesh=torus,
        in_specs=(rows, P(DP, None), line, line, line, rows, rows, line, rows, rows, rows),
        out_specs=(rows, rows, line, line, line, rows, rows, line, rows, rows),
        check_vma=False,
    )
```

```python
import math
import types

import jax
import jax.numpy as jnp
import numpy as np
from jax import lax
from jax.experimental import pallas as pl
from jax.experimental.pallas import tpu as pltpu
from jax.sharding import Mesh
from jax.sharding import PartitionSpec as P

QUERY_HEADS = 16
KEY_VALUE_HEADS = 8
HEAD = 128
WIDTH = 1024
FF = 3072
TOK = 128
GROUP = 2048
BLOCK = 256
WIDE = 512
SLICE = FF // 8
CUT = 640
EPS = 1e-06
FAR = 256.0
LN2 = math.log(2.0)
THETA = 1000000.0
SCALE = 1.0 / math.sqrt(HEAD)
SCALE2 = SCALE / math.log(2.0)
KEY_AT = QUERY_HEADS * HEAD
VALUE_AT = KEY_AT + KEY_VALUE_HEADS * HEAD

AXES = ("z", "xl", "xh", "y", "c")
SIZES = (4, 2, 2, 4, 2)
DP = ("z", "xl")
BF = jnp.bfloat16
F32 = jnp.float32
BY_MESH = pl.DeviceIdType.MESH
MIB = 2**20


def offsets(*axes):
    out = [()]
    for size, name in zip(SIZES, AXES):
        out = [o + (k,) for o in out for k in (range(size) if name in axes else (0,))]
    return out[1:]


SIBLING = (0, 0, 0, 0, 1)
CTX = offsets("xh", "y")
DP_ALL = offsets("z", "xl")
X_PEERS = offsets("xl", "xh")
X_HALF = (0, 0, 1, 0, 0)
X_LOW = (0, 1, 0, 0, 0)
Y_PEERS = [(0, 0, 0, k, 0) for k in (1, 3, 2)]
Z_PEERS = [(k, 0, 0, 0, 0) for k in (1, 3, 2)]
PEERS = sorted(set(CTX + DP_ALL + X_PEERS + [SIBLING]))


def moved(me, offset):
    return tuple(lax.rem(m + o, s) if o else m for m, o, s in zip(me, offset, SIZES))


def before(me, offset):
    return tuple(lax.rem(m + s - o, s) if o else m for m, o, s in zip(me, offset, SIZES))


def ctx_of(at):
    return at[2] * 8 + at[3] * 2 + at[4]


def dp_of(at):
    return at[0] * 2 + at[1]


def chip_of(at):
    return at[2] * 4 + at[3]


def columns(k, width=HEAD):
    return pl.ds(pl.multiple_of(k * width, width), width)


class Net:
    def __init__(self, send, recv, hold_send, hold_recv):
        self.send, self.recv, self.hold = send, recv, (hold_send, hold_recv)
        self.held, self.sends, self.recvs = 0, 0, 0
        self.sent, self.used, self.free = [], [], []

    def take(self, n=1):
        k = self.held
        self.held += n
        return k

    def slot(self):
        if self.free:
            return self.free.pop()
        self.sends += 1
        return self.sends - 1

    def made(self, src, dst, device, send, recv):
        return pltpu.make_async_remote_copy(
            src_ref=src,
            dst_ref=dst,
            send_sem=send,
            recv_sem=recv,
            device_id=device,
            device_id_type=BY_MESH,
        )

    def copy(self, src, dst, device, send, recv):
        return self.made(src, dst, device, self.hold[0].at[send], self.hold[1].at[recv])

    def pair(self):
        s, r = self.slot(), self.recvs
        self.recvs += 1
        return s, self.send.at[s], self.recv.at[r]

    def put(self, src, dst, device):
        s, send, recv = self.pair()
        copy = self.made(src, dst, device, send, recv)
        copy.start()
        self.sent.append(copy)
        self.used.append((copy, s))
        return copy

    def put_all(self, triples, total):
        s, send, recv = self.pair()
        for src, dst, device in triples:
            self.made(src, dst, device, send, recv).start()
        group = self.made(total, total, triples[0][2], send, recv)
        self.sent.append(group)
        self.used.append((group, s))
        return group

    def local(self, src, dst):
        copy = pltpu.make_async_copy(src, dst, self.send.at[self.slot()])
        copy.start()
        return copy

    def release(self, copies):
        self.free += [s for copy, s in self.used if any(copy is other for other in copies)]

    def drain(self):
        for copy in self.sent:
            copy.wait_send()
        self.sent = []


def arrived(copies):
    for copy in copies:
        copy.wait_recv()


def dot(a, b):
    return jnp.dot(a, b, preferred_element_type=F32)


def dot_t(a, b):
    return lax.dot_general(a, b, (((1,), (1,)), ((), ())), preferred_element_type=F32)


def t_dot(a, b):
    return lax.dot_general(a, b, (((0,), (0,)), ((), ())), preferred_element_type=F32)


def turned(v):
    return pltpu.roll(v, HEAD // 2, 1)


def inverse_root(v):
    return lax.rsqrt(jnp.mean(v * v, -1, keepdims=True) + EPS)


def head_back(unnormed, grad, cosine, sine, gain):
    inverse = inverse_root(unnormed)
    hat = unnormed * inverse
    back = grad * cosine - turned(grad) * sine
    g = back * gain
    raw = inverse * (g - hat * jnp.mean(g * hat, -1, keepdims=True))
    return raw, jnp.sum(back * hat, 0, keepdims=True)


def norm_back(values, inverse, grad):
    cubed = inverse * inverse * inverse
    return inverse * grad - values * cubed * jnp.mean(grad * values, -1, keepdims=True)


BUFFERS = dict(
    tok=((TOK, WIDTH), BF),
    wqkv=((8, VALUE_AT + KEY_VALUE_HEADS * HEAD), BF),
    wgu=((8, 2 * FF), BF),
    wd=((24, WIDTH), BF),
    gains=((8, 128), F32),
    freq=((1, HEAD), F32),
    gains_out=((8, 128), F32),
    dwq_out=((8, VALUE_AT + KEY_VALUE_HEADS * HEAD), F32),
    dwo_out=((16, WIDTH), F32),
    dgu_out=((8, 2 * FF), F32),
    dwd_out=((24, WIDTH), F32),
    wq_src=((8, 2, 8, 2 * HEAD), F32),
    wq_pair=((8, 2, 8, 2 * HEAD), F32),
    wq_tmp=((8, 2, 8, 2 * HEAD), F32),
    w_low=((TOK, 2 * HEAD), BF),
    w_got=((8, TOK, HEAD), BF),
    w_all=((8, TOK, 2 * HEAD), BF),
    g_pair=((2, 8, 128), F32),
    g_tmp=((8, 2, 8, 128), F32),
    g_row=((16, 128), F32),
    g_all=((8, 16, 128), F32),
    gain_one=((1, WIDTH), F32),
    gain_two=((1, WIDTH), F32),
    gain_q=((1, HEAD), F32),
    gain_k=((1, HEAD), F32),
    gu_src=((4, 2, 8, 2 * SLICE), F32),
    gu_pair=((4, 2, 8, 2 * SLICE), F32),
    gu_tmp=((4, 2, 8, 2 * SLICE), F32),
    gu_low=((4, 16, 2 * SLICE), BF),
    gu_all=((4, 2, 2, 4, 16, 2 * SLICE), BF),
    wd_src=((24, WIDTH), F32),
    wd_tmp=((2, 24, WIDTH), F32),
    wd_all=((2, 4, 48, WIDTH), BF),
    wo_all=((4, 2, 2, 4, 2, 16, WIDTH), BF),
    cot_all=((4, 2, TOK, WIDTH), BF),
    x_all=((16, TOK, WIDTH), BF),
    angle=((8, BLOCK, HEAD), F32),
    q=((8, BLOCK, 2 * HEAD), BF),
    k=((8, BLOCK, 2 * HEAD), BF),
    v=((8, BLOCK, HEAD), BF),
    k_turned=((8, HEAD, BLOCK), BF),
    v_turned=((8, HEAD, BLOCK), BF),
    q_un=((8, BLOCK, HEAD), F32),
    k_un=((8, BLOCK, HEAD), F32),
    full=((8, HEAD, BLOCK), F32),
    norm=((8, 1, BLOCK), F32),
    att=((8, 2, TOK, HEAD), BF),
    att_pair=((8, TOK, 2 * HEAD), BF),
    att_all=((TOK, QUERY_HEADS * HEAD), BF),
    resid=((TOK, WIDTH), F32),
    s_all=((4, 2, TOK, WIDTH), BF),
    hidden=((4, BLOCK, SLICE), BF),
    grad_gu=((4, BLOCK, 2 * SLICE), BF),
    pg=((4, 2, TOK, WIDTH), BF),
    pg_got=((4, TOK, WIDTH), BF),
    pg_ring=((3, TOK, WIDTH), BF),
    po_got=((4, TOK, WIDTH), BF),
    po_ring=((3, TOK, WIDTH), BF),
    dgu=((4, 4, 4, 16, 2 * SLICE), BF),
    dgu_x=((3, 4, 4, 16, SLICE), BF),
    dgu_y=((3, 4, 16, SLICE), BF),
    dgv_y=((3, 4, 4, 16, SLICE), BF),
    dgv_x=((3, 4, 16, SLICE), BF),
    dwd=((8, 48, WIDTH), BF),
    dwd_x=((3, 4, 48, WIDTH), BF),
    dwd_y=((3, 48, WIDTH), BF),
    dwd_sum=((2, 24, WIDTH), F32),
    dwd_half=((24, WIDTH), F32),
    dwo_got=((4, 2, 2, 4, 16, WIDTH), BF),
    dwo_z=((3, 2, 2, 4, 16, CUT), BF),
    dwo_y=((3, 2, 2, 16, CUT), BF),
    dwo_x=((3, 16, CUT), BF),
    dwp_y=((3, 4, 2, 2, 16, WIDTH - CUT), BF),
    dwp_z=((3, 2, 2, 16, WIDTH - CUT), BF),
    dwp_x=((3, 16, WIDTH - CUT), BF),
    grad_resid=((TOK, WIDTH), F32),
    gh_pair=((8, TOK, 2 * HEAD), BF),
    gh_all=((8, 2, TOK, HEAD), BF),
    dk=((4, WIDE, HEAD), F32),
    dv=((4, WIDE, HEAD), F32),
    swap_got=((4, 2, 2, TOK, HEAD), BF),
    dq=((2, WIDE, HEAD), F32),
    p_x=((TOK, WIDTH // 2), BF),
    p_x_src=((TOK, WIDTH // 2), BF),
    dw=((2 * HEAD, WIDTH), F32),
    dw_low=((2 * HEAD, WIDTH), BF),
    dw_got=((3, 2 * HEAD, 2 * TOK), BF),
    dw_mid=((2, 2 * HEAD, TOK), BF),
    dw_xl=((2 * HEAD, TOK), BF),
    hg=((8, 128), F32),
    hg_near=((8, 128), F32),
    hg_two=((8, 128), F32),
    hg_got=((7, 8, 128), F32),
    hg_mid=((8, 128), F32),
    hg_dp=((7, 8, 128), F32),
)
INPUTS = ("tok_in", "wqkv_in", "wo_in", "wgu_in", "wd_in", "cot_in", "gains_in", "freq_in", "lengths")
OUTPUTS = dict(
    output=((TOK, WIDTH), F32),
    input_grad=((TOK, WIDTH), F32),
    gain_grads=((8, 128), F32),
    grad_qkv=((8, VALUE_AT + KEY_VALUE_HEADS * HEAD), F32),
    grad_out=((16, WIDTH), F32),
    grad_up=((8, 2 * FF), F32),
    grad_down=((24, WIDTH), F32),
)
SEMS = (95, 112, 37, 37)
VMEM_LIMIT = 60 * MIB


def body(*refs):
    names = list(INPUTS) + list(OUTPUTS) + list(BUFFERS) + ["send", "recv", "hold_send", "hold_recv"]
    r = types.SimpleNamespace(**dict(zip(names, refs, strict=True)))
    me = tuple(lax.axis_index(a) for a in AXES)
    z, xl, xh, y, c = me
    chip = xh * 4 + y
    mine, here = ctx_of(me), dp_of(me)
    over = moved(me, SIBLING)
    net = Net(r.send, r.recv, r.hold_send, r.hold_recv)

    own_wo = (z, xl, xh, y, c)
    loads = [
        net.local(r.wqkv_in, r.wqkv),
        net.local(r.gains_in, r.gains),
        net.local(r.wgu_in, r.wgu),
        net.local(r.wd_in, r.wd),
        net.local(r.tok_in, r.tok),
        net.local(r.wo_in, r.wo_all.at[own_wo]),
        net.local(r.freq_in, r.freq),
        net.local(r.cot_in, r.cot_all.at[z, c]),
    ]
    barrier = pltpu.get_barrier_semaphore()
    for o in PEERS:
        pl.semaphore_signal(barrier, inc=1, device_id=moved(me, o), device_id_type=BY_MESH)
    for copy in loads:
        copy.wait()

    w = r.wqkv[...].astype(F32)
    for j in range(16):
        extra = (KEY_AT, VALUE_AT)[j % 2] + j // 2 * HEAD
        r.wq_src[j // 2, j % 2, :, :HEAD] = w[:, j * HEAD : (j + 1) * HEAD]
        r.wq_src[j // 2, j % 2, :, HEAD:] = w[:, extra : extra + HEAD]
    w = r.wgu[...].astype(F32)
    for j in range(8):
        r.gu_src[j // 2, j % 2, :, :SLICE] = w[:, j * SLICE : (j + 1) * SLICE]
        r.gu_src[j // 2, j % 2, :, SLICE:] = w[:, FF + j * SLICE : FF + (j + 1) * SLICE]
    r.wd_src[...] = r.wd[...].astype(F32)
    r.wq_pair[:, c] = r.wq_src[:, c]
    r.gu_pair[:, c] = r.gu_src[:, c]
    r.g_pair[c] = r.gains[...]
    r.wd_tmp[c] = r.wd_src[...]
    r.x_all[mine] = r.tok[...]
    pl.semaphore_wait(barrier, len(PEERS))

    small = [
        net.put(r.wq_src.at[:, 1 - c], r.wq_pair.at[:, c], over),
        net.put(r.gains, r.g_pair.at[c], over),
        net.put(r.gu_src.at[:, 1 - c], r.gu_pair.at[:, c], over),
        net.put(r.wd_src, r.wd_tmp.at[c], over),
    ]
    wo_own = r.wo_all.at[own_wo]
    wo_x = net.put_all(
        [(wo_own, wo_own, moved(me, o)) for o in X_PEERS], r.wo_all.at[0, 0, 0, pl.ds(0, 3), 0]
    )
    at = r.cot_all.at[z, c]
    cot_z = [net.put(at, at, moved(me, o)) for o in Z_PEERS[:2]]
    arrived(small)
    w_ctx = net.put_all(
        [(r.wq_pair.at[chip_of(to)], r.wq_tmp.at[chip], to) for to in (moved(me, o) for o in CTX)],
        r.wq_tmp.at[pl.ds(0, 7)],
    )
    g_ctx = net.put_all(
        [(r.g_pair, r.g_tmp.at[chip], moved(me, o)) for o in CTX], r.g_tmp.at[pl.ds(0, 7)]
    )
    gu_z = net.put_all(
        [(r.gu_pair.at[to[0]], r.gu_tmp.at[z], to) for to in (moved(me, o) for o in Z_PEERS)],
        r.gu_tmp.at[pl.ds(0, 3)],
    )
    r.wq_tmp[chip] = r.wq_pair[chip]
    r.g_tmp[chip] = r.g_pair[...]
    r.gu_tmp[z] = r.gu_pair[z]
    wd_sems = net.take(3)

    @pl.when(xl == c)
    def _():
        r.wd_all[xh, y] = r.wd_tmp[...].reshape(48, WIDTH).astype(BF)
        for k, o in enumerate(Y_PEERS):
            at = r.wd_all.at[xh, y]
            net.copy(at, at, moved(me, o), wd_sems + k, wd_sems + k).start()

    tok_x = net.put(r.tok, r.x_all.at[mine], moved(me, X_HALF))
    tok_y = [net.put(r.tok, r.x_all.at[mine], moved(me, o)) for o in Y_PEERS]
    tok_own = net.put(r.tok, r.x_all.at[mine], over)
    at = r.cot_all.at[z, c]
    cot_near = [net.put(at, at, over)]

    ends, starts = [], []
    total = 0
    for d in range(8):
        starts.append(total)
        total = total + r.lengths[0, d]

    def begin_of(index):
        out = jnp.zeros_like(index)
        for s in starts[1:]:
            out = jnp.where(index >= s, s, out)
        return out

    def pass_on(ref, at):
        return net.put(ref.at[at], ref.at[at], over)

    def same(ref, peers, total):
        return net.put_all([(ref, ref, moved(me, o)) for o in peers], total)

    first, last = slice(0, WIDTH // 2), slice(WIDTH // 2, WIDTH)
    left, right = slice(0, SLICE), slice(SLICE, 2 * SLICE)
    wo_x.wait_recv()
    wo_y = same(r.wo_all.at[z, :, :, y, c], Y_PEERS, r.wo_all.at[pl.ds(0, 3), :, :, 0, 0])
    gu_z.wait_recv()
    r.gu_low[...] = r.gu_tmp[...].reshape(4, 16, 2 * SLICE).astype(BF)
    r.gu_all[:, xl, xh, y] = r.gu_low[...]
    gu_y = net.put_all(
        [
            (r.gu_low.at[:, :, left], r.gu_all.at[:, xl, xh, y, :, left], moved(me, o))
            for o in Y_PEERS
        ],
        r.gu_all.at[:, 0, 0, pl.ds(0, 3), :, left],
    )
    gu_x = net.put_all(
        [
            (r.gu_low.at[:, :, right], r.gu_all.at[:, xl, xh, y, :, right], moved(me, o))
            for o in X_PEERS
        ],
        r.gu_all.at[:, 0, 0, pl.ds(0, 3), :, right],
    )

    w_ctx.wait_recv()
    r.w_low[...] = r.wq_tmp[...].reshape(TOK, 2 * HEAD).astype(BF)
    w_xl = net.put(r.w_low, r.w_all.at[here], moved(me, X_LOW))
    g_ctx.wait_recv()
    r.g_row[...] = r.g_tmp[:, :, 0, :].reshape(16, 128)
    g_dp = net.put_all(
        [(r.g_row, r.g_all.at[here], moved(me, o)) for o in DP_ALL], r.g_all.at[pl.ds(0, 7)]
    )
    r.w_all[here] = r.w_low[...]
    r.g_all[here] = r.g_row[...]

    low = lax.broadcasted_iota(jnp.int32, (BLOCK, HEAD), 1) < HEAD // 2
    shift = jnp.where(low, 0.0, 0.5 * math.pi)

    @pl.loop(0, 8)
    def _(n):
        index = n * BLOCK + lax.broadcasted_iota(jnp.int32, (BLOCK, HEAD), 0)
        phase = (index - begin_of(index)).astype(F32) * r.freq[...]
        r.angle[n] = jnp.cos(phase - shift)
        document = jnp.zeros_like(index)
        for s in starts[1:]:
            document = document + (index >= s).astype(jnp.int32)
        place = lax.broadcasted_iota(jnp.int32, (BLOCK, HEAD), 1)
        same_doc = jnp.where(document == place, 1.0, 0.0)
        r.q[n, :, HEAD:] = jnp.where(place == 8, 1.0, same_doc).astype(BF)
        r.k[n, :, HEAD:] = jnp.where(place == 8, -FAR, FAR * same_doc).astype(BF)

    def angles(n):
        both = r.angle[n]
        other = turned(both)
        return jnp.where(low, both, other), jnp.where(low, -other, both)

    w_xl.wait_recv()
    w_z = same(r.w_all.at[pl.ds(2 * z, 2)], Z_PEERS, r.w_all.at[pl.ds(0, 6)])
    tok_x.wait_recv()
    at_x = ctx_of(before(me, X_HALF))
    near = {(1, 0): pass_on(r.x_all, at_x)}
    at = r.x_all.at[at_x, :, first]
    tok_xy = [net.put(at, at, moved(me, o)) for o in Y_PEERS]
    tok_yx = []
    for o, copy in zip(Y_PEERS, tok_y):
        copy.wait_recv()
        source = ctx_of(before(me, o))
        at = r.x_all.at[source, :, last]
        tok_yx.append(net.put(at, at, moved(me, X_HALF)))
        near[(0, o[3])] = pass_on(r.x_all, source)
    cot_far = []
    for k in range(2):
        cot_z[k].wait_recv()
        source = before(me, Z_PEERS[k])[0]
        at = r.cot_all.at[source, c, :, (first, last)[k]]
        cot_far.append(net.put(at, at, moved(me, Z_PEERS[k])))
        cot_near.append(pass_on(r.cot_all, (source, c)))
    wo_y.wait_recv()
    at = r.wo_all.at[z, :, :, :, c]
    wo_z = [net.put(at, at, moved(me, o)) for o in Z_PEERS[:2]]
    wo_near = [net.put(at, at, over)]
    gu_y.wait_recv()
    gu_x.wait_recv()
    gu_yx = same(r.gu_all.at[:, xl, xh, :, :, left], X_PEERS, r.gu_all.at[pl.ds(0, 3), :, :, :, :, left])
    gu_xy = same(r.gu_all.at[:, :, :, y, :, right], Y_PEERS, r.gu_all.at[pl.ds(0, 3), :, :, :, :, right])
    wdx_sems = net.take(3)

    @pl.when(xl == c)
    def _():
        at = r.wd_all.at[xh, y]
        for k, o in enumerate(Y_PEERS):
            net.copy(at, at, moved(me, o), wd_sems + k, wd_sems + k).wait_recv()
        at = r.wd_all.at[xh]
        for k, o in enumerate(X_PEERS):
            net.copy(at, at, moved(me, o), wdx_sems + k, wdx_sems + k).start()

    w_z.wait_recv()
    w_near = net.put(r.w_all.at[:, :, HEAD:], r.w_got, over)
    g_dp.wait_recv()
    gains = r.g_all[...].reshape(128, 128).astype(BF)
    dev = lax.broadcasted_iota(jnp.int32, (128, WIDTH), 0)
    lane = lax.broadcasted_iota(jnp.int32, (128, WIDTH), 1)
    spread = t_dot(gains, (lane // 8 == dev).astype(F32).astype(BF))
    pick = lax.broadcasted_iota(jnp.int32, (8, WIDTH), 1) % 8 == lax.broadcasted_iota(
        jnp.int32, (8, WIDTH), 0
    )
    r.gain_one[...] = jnp.sum(jnp.where(pick, spread[:8], 0.0), 0, keepdims=True)
    r.gain_two[...] = jnp.sum(jnp.where(pick, spread[8:16], 0.0), 0, keepdims=True)
    eye = lax.broadcasted_iota(jnp.int32, (128, 128), 0) == lax.broadcasted_iota(
        jnp.int32, (128, 128), 1
    )
    spread = t_dot(gains, eye.astype(F32).astype(BF))
    r.gain_q[...] = spread[16:17]
    r.gain_k[...] = spread[17:18]
    w_near.wait_recv()

    def project(n):
        inputs = r.x_all[pl.ds(2 * n, 2)].reshape(BLOCK, WIDTH).astype(F32)
        first_in = (inputs * inverse_root(inputs) * r.gain_one[...]).astype(BF)
        projected = dot(first_in, r.w_all[...].reshape(WIDTH, 2 * HEAD))
        second = dot(first_in, r.w_got[...].reshape(WIDTH, HEAD))
        q_un, own = projected[:, :HEAD], projected[:, HEAD:]
        k_un = jnp.where(c == 0, own, second)
        value = jnp.where(c == 0, second, own)
        r.v[n] = value.astype(BF)
        r.v_turned[n] = value.T.astype(BF)
        r.q_un[n] = q_un
        r.k_un[n] = k_un
        cosine, sine = angles(n)
        q = q_un * inverse_root(q_un) * r.gain_q[...]
        r.q[n, :, :HEAD] = ((q * cosine + turned(q) * sine) * SCALE2).astype(BF)
        key = k_un * inverse_root(k_un) * r.gain_k[...]
        key = key * cosine + turned(key) * sine
        r.k[n, :, :HEAD] = key.astype(BF)
        r.k_turned[n] = key.T.astype(BF)

    tok_own.wait_recv()
    project(chip)
    waiting = [(1, 0)]

    def next_project():
        a, b = waiting.pop(0)
        near[(a, b)].wait_recv()
        project(chip_of(before(me, (0, 0, a, b, 0))))

    for o in Y_PEERS:
        next_project()
        waiting.append((0, o[3]))
    for o, one, two in zip(Y_PEERS, tok_xy, tok_yx):
        one.wait_recv()
        two.wait_recv()
        key = (1, o[3])
        near[key] = pass_on(r.x_all, ctx_of(before(me, (0, 0, 1, o[3], 0))))
        next_project()
        waiting.append(key)
    next_project()
    def causal(size):
        keys = lax.broadcasted_iota(jnp.int32, (size, size), 0)
        return keys <= lax.broadcasted_iota(jnp.int32, (size, size), 1)

    wo_far = []

    def wo_on(k):
        wo_z[k].wait_recv()
        source = before(me, Z_PEERS[k])[0]
        at = r.wo_all.at[source, :, :, :, c, :, (first, last)[k]]
        wo_far.append(net.put(at, at, moved(me, Z_PEERS[k])))
        at = r.wo_all.at[source, :, :, :, c]
        wo_near.append(net.put(at, at, over))

    att_send = net.take(8)
    att_near = []

    def att_copy(i):
        return net.copy(
            r.att_pair.at[i],
            r.att_all.at[:, columns(chip, 2 * HEAD)],
            (z, xl, i // 4, i % 4, c),
            att_send + i,
            att_send + chip,
        )

    def send_pair(i):
        for copy in att_near[i]:
            copy.wait_recv() if copy is att_near[i][0] else copy.wait()

        @pl.when(chip != i)
        def _():
            att_copy(i).start()

    for i in range(8):
        q = r.q[i]
        rows = jnp.zeros((1, BLOCK), F32)
        acc = jnp.zeros((HEAD, BLOCK), F32)
        for b in range(i + 1):
            e = jnp.exp2(dot_t(r.k[b], q))
            if b == i:
                e = jnp.where(causal(BLOCK), e, 0.0)
            rows = rows + jnp.sum(e, 0, keepdims=True)
            acc = acc + dot(r.v_turned[b], e.astype(BF))
        norm = 1.0 / rows
        acc = acc * norm
        r.full[i] = acc
        r.norm[i] = norm
        r.att[i] = acc.T.astype(BF).reshape(2, TOK, HEAD)
        att_near.append(
            (
                net.put(r.att.at[i, 1 - c], r.att_pair.at[i, :, columns(c)], over),
                net.local(r.att.at[i, c], r.att_pair.at[i, :, columns(c)]),
            )
        )
        if i:
            send_pair(i - 1)
        if i in (6, 7):
            wo_on(i - 6)
    send_pair(7)
    keep = net.local(r.att_pair.at[chip], r.att_all.at[:, columns(chip, 2 * HEAD)])
    far = lax.rem(z + 2, 4)
    arrived(wo_far)
    at = r.wo_all.at[far, :, :, :, c]
    wo_near.append(net.put(at, at, over))
    for o in CTX:
        k = att_send + chip_of(before(me, o))
        net.copy(r.att_pair.at[0], r.att_pair.at[0], over, k, k).wait_recv()
    keep.wait()
    arrived(wo_near)

    inputs = r.tok[...].astype(F32)
    residual = inputs + dot(r.att_all[...], r.wo_all[...].reshape(QUERY_HEADS * HEAD, WIDTH))
    r.resid[...] = residual
    inverse_two = inverse_root(residual)
    r.s_all[z, c] = (residual * inverse_two * r.gain_two[...]).astype(BF)
    s_mine = r.s_all.at[z, c]
    s_near = {0: net.put(s_mine, s_mine, over)}
    s_z = [net.put(s_mine, s_mine, moved(me, o)) for o in Z_PEERS[:2]]

    arrived(cot_far)
    cot_near.append(pass_on(r.cot_all, (far, c)))
    arrived([gu_yx, gu_xy] + cot_near)
    at = r.wd_all.at[0]

    @pl.when(xl == c)
    def _():
        net.copy(at, at, over, wdx_sems, wdx_sems + X_PEERS.index(X_HALF)).wait_recv()

    @pl.when(xl != c)
    def _():
        for k, o in enumerate(X_PEERS):
            if o != X_HALF:
                net.copy(at, at, over, wdx_sems, wdx_sems + k).wait_recv()

    def feed_forward(n):
        w_gu = r.gu_all[...].reshape(WIDTH, 2 * SLICE)
        gu = dot(r.s_all[n].reshape(BLOCK, WIDTH), w_gu)
        grad_hidden = dot_t(r.cot_all[n].reshape(BLOCK, WIDTH), r.wd_all[...].reshape(SLICE, WIDTH))
        gate, up = gu[:, :SLICE], gu[:, SLICE:]
        sigma = 1.0 / (1.0 + jnp.exp(-gate))
        swish = gate * sigma
        r.hidden[n] = (swish * up).astype(BF)
        grad_gate = grad_hidden * up * sigma * (1.0 + gate * (1.0 - sigma))
        grad_gu = jnp.concatenate([grad_gate, grad_hidden * swish], 1).astype(BF)
        r.grad_gu[n] = grad_gu
        r.pg[n] = dot_t(grad_gu, w_gu).astype(BF).reshape(2, TOK, WIDTH)
        return net.put(r.pg.at[n, 1 - c], r.pg_got.at[n], over)

    pg_near, pg_ring = {}, []

    def mix(n, got):
        r.pg_got[n] = (r.pg[n, c].astype(F32) + r.pg_got[n].astype(F32)).astype(BF)

    def send_mixed(k):
        o = Z_PEERS[k]
        to = moved(me, o)
        pg_near[k].wait_recv()
        mix(to[0], None)
        pg_ring.append(net.put(r.pg_got.at[to[0]], r.pg_ring.at[k], to))

    s_near[0].wait_recv()
    pg_own = feed_forward(z)
    s_far = []
    for k in range(2):
        s_z[k].wait_recv()
        source = before(me, Z_PEERS[k])[0]
        s_near[k + 1] = pass_on(r.s_all, (source, c))
        at = r.s_all.at[source, c, :, (first, last)[k]]
        s_far.append(net.put(at, at, moved(me, Z_PEERS[k])))
    for k in range(2):
        s_near[k + 1].wait_recv()
        pg_near[1 - k] = feed_forward(before(me, Z_PEERS[k])[0])
        if k:
            send_mixed(1)
    arrived(s_far)
    s_near[3] = pass_on(r.s_all, (far, c))
    send_mixed(0)
    s_near[3].wait_recv()
    pg_near[2] = feed_forward(far)
    done = [2]
    send_mixed(done[-1])
    pg_own.wait_recv()
    mix(z, None)

    gone = [pg_own, *pg_near.values(), *pg_ring]
    early = [copy for copy in net.sent if all(copy is not g for g in gone)]
    net.sent = list(pg_ring)
    s_rows = r.s_all[...].reshape(4 * BLOCK, WIDTH)
    grad_gu = r.grad_gu[...].reshape(4 * BLOCK, 2 * SLICE)
    for a in range(4):
        part = t_dot(s_rows[:, a * BLOCK : (a + 1) * BLOCK], grad_gu)
        r.dgu[a] = part.astype(BF).reshape(4, 4, 16, 2 * SLICE)

    def scattered(peers, source, out):
        to = [moved(me, o) for o in peers]
        return net.put_all([(source(t), out.at[k], t) for k, t in enumerate(to)], out)

    dgu_one = scattered(X_PEERS, lambda to: r.dgu.at[:, to[1] * 2 + to[2], :, :, left], r.dgu_x)
    dgu_two = scattered(Y_PEERS, lambda to: r.dgu.at[:, :, to[3], :, right], r.dgv_y)
    hidden = r.hidden[...].reshape(4 * BLOCK, SLICE)
    for a in range(4):
        cols = slice(a * BLOCK, (a + 1) * BLOCK)
        part = t_dot(hidden, r.cot_all[:, :, :, cols].reshape(4 * BLOCK, BLOCK))
        r.dwd[:, :, cols] = part.astype(BF).reshape(8, 48, BLOCK)
    dwd_sems = net.take(3)
    half_at = X_PEERS.index(X_HALF)

    def dwd_copy(k):
        to = moved(me, X_PEERS[k])
        return net.copy(
            r.dwd.at[pl.ds(to[2] * 4, 4)], r.dwd_x.at[k], to, dwd_sems + k, dwd_sems + k
        )

    for copy in [pg_own, *pg_near.values()]:
        copy.wait_send()
    for n in range(4):
        part = dot(r.hidden[n], r.wd_all[...].reshape(SLICE, WIDTH))
        r.pg[n] = part.astype(BF).reshape(2, TOK, WIDTH)
    po_near = net.put(r.pg.at[:, 1 - c], r.po_got, over)

    po_near.wait_recv()

    @pl.loop(0, 4)
    def _(n):
        r.po_got[n] = r.pg[n, c] + r.po_got[n]

    po_ring = scattered(Z_PEERS, lambda to: r.po_got.at[to[0]], r.po_ring)

    arrived(pg_ring)
    grad_second = r.pg_got[z].astype(F32)
    for k in range(3):
        grad_second = grad_second + r.pg_ring[k].astype(F32)
    residual = r.resid[...]
    inverse_two = inverse_root(residual)
    grad_resid = r.cot_all[z, c].astype(F32) + norm_back(
        residual, inverse_two, grad_second * r.gain_two[...]
    )
    r.grad_resid[...] = grad_resid
    resid_low = grad_resid.astype(BF)
    for i in range(8):

        @pl.when(chip != i)
        def _():
            att_copy(i).wait_send()

    for j in range(8):
        part = dot_t(resid_low, r.wo_all[j // 2, j % 2].reshape(BLOCK, WIDTH))
        r.att_pair[j] = part.astype(BF)
    for copy in early:
        copy.wait_send()
    net.release(early)
    gh = net.put_all(
        [
            (r.att_pair.at[chip_of(to)], r.gh_pair.at[chip], to)
            for to in (moved(me, o) for o in CTX)
        ],
        r.gh_pair.at[pl.ds(0, 7)],
    )
    keep = net.local(r.att_pair.at[chip], r.gh_pair.at[chip])

    for j in range(8):
        part = t_dot(r.att_all[:, j * BLOCK : (j + 1) * BLOCK], resid_low)
        r.wo_all[j // 2, j % 2] = part.astype(BF).reshape(2, 4, 2, 16, WIDTH)
    dwo_near = net.put(r.wo_all.at[:, :, :, :, 1 - c], r.dwo_got, over)
    at_x = xl * 2 + xh
    dgu_one.wait_recv()

    @pl.loop(0, 4)
    def _(a):
        for b in range(4):
            total = r.dgu[a, at_x, b, :, left].astype(F32)
            for k in range(3):
                total = total + r.dgu_x[k, a, b].astype(F32)
            r.dgu_x[0, a, b] = total.astype(BF)

    dgu_two.wait_recv()

    @pl.loop(0, 4)
    def _(a):
        for b in range(4):
            total = r.dgu[a, b, y, :, right].astype(F32)
            for k in range(3):
                total = total + r.dgv_y[k, a, b].astype(F32)
            r.dgv_y[0, a, b] = total.astype(BF)

    dwo_near.wait_recv()

    @pl.loop(0, 16)
    def _(a):
        for b in range(4):
            at = (a // 4, lax.rem(a, 4) // 2, lax.rem(a, 2), b)
            r.dwo_got[at] = r.wo_all[(*at, c)] + r.dwo_got[at]

    more, less = slice(0, CUT), slice(CUT, WIDTH)
    dwo_one = scattered(Z_PEERS, lambda to: r.dwo_got.at[to[0], :, :, :, :, more], r.dwo_z)
    gh.wait_recv()
    keep.wait()
    dgu_one = scattered(Y_PEERS, lambda to: r.dgu_x.at[0, :, to[3]], r.dgu_y)
    dgu_two = scattered(X_PEERS, lambda to: r.dgv_y.at[0, :, to[1] * 2 + to[2]], r.dgv_x)
    dwo_two = scattered(Y_PEERS, lambda to: r.dwo_got.at[:, :, :, to[3], :, less], r.dwp_y)
    @pl.when(xl == c)
    def _():
        dwd_copy(half_at).start()

    @pl.when(xl != c)
    def _():
        for k in range(3):
            if k != half_at:
                dwd_copy(k).start()

    gh_near = net.put(r.gh_pair.at[:, :, columns(1 - c)], r.gh_all.at[:, c], over)
    keep = net.local(r.gh_pair.at[:, :, columns(c)], r.gh_all.at[:, c])
    gh_near.wait_recv()
    keep.wait()

    def pair(ref, n):
        return ref[2 * n : 2 * n + 2].reshape(WIDE, ref.shape[2])

    def beside(ref, n):
        return jnp.concatenate([ref[2 * n], ref[2 * n + 1]], 1)

    swaps = {}

    def attend_back(n):
        q = pair(r.q, n)
        g = r.gh_all[2 * n : 2 * n + 2].reshape(WIDE, HEAD)
        g_turned = (g.T.astype(F32) * beside(r.norm, n)).astype(BF)
        g = g_turned.T
        inner = jnp.sum(g_turned.astype(F32) * beside(r.full, n), 0, keepdims=True)
        acc = jnp.zeros((HEAD, WIDE), F32)
        for b in range(n + 1):
            key = pair(r.k, b)
            e = jnp.exp2(dot_t(key, q))
            if b == n:
                e = jnp.where(causal(WIDE), e, 0.0)
            dp = dot(pair(r.v, b), g_turned)
            ds = (e * (dp - inner)).astype(BF)
            dv, dk = dot(e.astype(BF), g), dot(ds, q[:, :HEAD])
            r.dv[b] = dv if n == 3 else r.dv[b] + dv
            r.dk[b] = dk if n == 3 else r.dk[b] + dk
            acc = acc + dot(beside(r.k_turned, b), ds)
        r.dq[n % 2] = (acc * SCALE).T
        r.dk[n] = r.dk[n] * LN2
        sent = jnp.where(c == 0, r.dv[n], r.dk[n]).astype(BF)
        r.att[2 * n : 2 * n + 2] = sent.reshape(2, 2, TOK, HEAD)
        swaps[n] = net.put(r.att.at[pl.ds(2 * n, 2)], r.swap_got.at[n], over)

    p_near = {}
    r.dw[...] = jnp.zeros_like(r.dw)
    r.hg[...] = jnp.zeros_like(r.hg)

    def project_back(n):
        swaps[n].wait_recv()
        for half in range(2):
            m = 2 * n + half
            rows = slice(half * BLOCK, (half + 1) * BLOCK)
            inputs = r.x_all[2 * m : 2 * m + 2].reshape(BLOCK, WIDTH).astype(F32)
            first_in = (inputs * inverse_root(inputs) * r.gain_one[...]).astype(BF)
            cosine, sine = angles(m)
            dq, q_part = head_back(r.q_un[m], r.dq[n % 2, rows], cosine, sine, r.gain_q[...])
            both = jnp.where(c == 0, r.dk[n, rows], r.dv[n, rows])
            both = both + r.swap_got[n, half].reshape(BLOCK, HEAD).astype(F32)
            dk, k_part = head_back(r.k_un[m], both, cosine, sine, r.gain_k[...])
            grad = jnp.concatenate([dq, jnp.where(c == 0, dk, both)], 1).astype(BF)
            r.hg[0:1] += q_part
            r.hg[1:2] += jnp.where(c == 0, k_part, 0.0)
            r.dw[...] += t_dot(grad, first_in)
            part = dot_t(grad, r.w_all[...].reshape(WIDTH, 2 * HEAD))
            r.x_all[2 * m : 2 * m + 2] = part.astype(BF).reshape(2, TOK, WIDTH)
            p_near[m] = net.put(r.x_all.at[2 * m + 1 - c], r.s_all.at[m // 2, m % 2], over)

    p_sems, r_sems = net.take(8), net.take(8)

    def p_copy(m):
        return net.copy(
            r.s_all.at[m // 2, m % 2, :, first],
            r.cot_all.at[y, m // 4, :, first],
            (z, xl, xh, m % 4, c),
            p_sems + m,
            p_sems + (m // 4) * 4 + y,
        )

    def r_copy(m):
        return net.copy(
            r.s_all.at[m // 2, m % 2, :, last],
            r.cot_all.at[m % 4, 0, :, last],
            (z, xl, m // 4, y, c),
            r_sems + m,
            r_sems + m % 4,
        )

    def send_parts(n):
        for m in (2 * n, 2 * n + 1):
            p_near[m].wait_recv()
            r.s_all[m // 2, m % 2] = r.x_all[2 * m + c] + r.s_all[m // 2, m % 2]

            @pl.when(y != m % 4)
            def _():
                p_copy(m).start()

            @pl.when(y == m % 4)
            def _():
                r.cot_all[m % 4, m // 4, :, first] = r.s_all[m // 2, m % 2, :, first]

            @pl.when(xh != m // 4)
            def _():
                r_copy(m).start()

    def paired(source, pair):
        copy = net.put(source.at[:, 1 - c], pair.at[:, c], over)
        pair[:, c] = source[:, c]
        return copy

    def dealt(copy, pair, got, peers, index):
        copy.wait_recv()
        got[index(me)] = pair[index(me)]
        to = [moved(me, o) for o in peers]
        return net.put_all(
            [(pair.at[index(t)], got.at[index(me)], t) for t in to], got.at[pl.ds(0, len(peers))]
        )

    def wait_left(half):
        for o in Y_PEERS:
            k = p_sems + half * 4 + before(me, o)[3]
            net.copy(r.p_x_src, r.p_x, over, k, k).wait_recv()

    def sum_left(half):
        total = r.cot_all[0, half, :, first].astype(F32)
        for b in range(1, 4):
            total = total + r.cot_all[b, half, :, first].astype(F32)
        return total

    def sum_right(b):
        at = xh * 2 + b // 2
        return r.s_all[at, lax.rem(b, 2), :, last].astype(F32) + r.cot_all[b, 0, :, last].astype(F32)

    attend_back(3)
    attend_back(2)
    project_back(3)
    attend_back(1)
    send_parts(3)
    project_back(2)
    attend_back(0)
    send_parts(2)
    project_back(1)
    send_parts(1)
    project_back(0)
    r.dw_low[...] = r.dw[...].astype(BF)
    dw_z = scattered(Z_PEERS, lambda to: r.dw_low.at[:, columns(to[0], 2 * TOK)], r.dw_got)
    send_parts(0)
    hg_near = net.put(r.hg, r.hg_near, over)
    hg_near.wait_recv()
    r.hg_two[...] = r.hg[...] + r.hg_near[...]
    hg_ctx = scattered(CTX, lambda to: r.hg_two, r.hg_got)

    dwo_one.wait_recv()

    @pl.loop(0, 4)
    def _(a):
        for b in range(4):
            at = (a // 2, lax.rem(a, 2), b)
            total = r.dwo_got[(z, *at, slice(None), more)].astype(F32)
            for k in range(3):
                total = total + r.dwo_z[(k, *at)].astype(F32)
            r.dwo_z[(0, *at)] = total.astype(BF)

    dwo_one = scattered(Y_PEERS, lambda to: r.dwo_z.at[0, :, :, to[3]], r.dwo_y)
    dwo_two.wait_recv()

    @pl.loop(0, 4)
    def _(a):
        for b in range(4):
            at = (a, b // 2, b % 2)
            total = r.dwo_got[(*at, y, slice(None), less)].astype(F32)
            for k in range(3):
                total = total + r.dwp_y[(k, *at)].astype(F32)
            r.dwp_y[(0, *at)] = total.astype(BF)

    dwo_two = scattered(Z_PEERS, lambda to: r.dwp_y.at[0, to[0]], r.dwp_z)

    dwdy_sems = net.take(4)

    def dwdy_copy(k):
        to = moved(me, Y_PEERS[k])
        return net.copy(r.dwd_x.at[0, to[3]], r.dwd_y.at[k], to, dwdy_sems + k, dwdy_sems + k)

    @pl.when(xl == c)
    def _():
        for k in range(3):
            dwd_copy(k).wait_recv()
        for b in range(4):
            total = r.dwd[xh * 4 + b].astype(F32)
            for k in range(3):
                total = total + r.dwd_x[k, b].astype(F32)
            r.dwd_x[0, b] = total.astype(BF)
        for k in range(3):
            dwdy_copy(k).start()

    dgu_one.wait_recv()
    dgu_two.wait_recv()
    for a in range(4):
        one = r.dgu_x[0, a, y].astype(F32)
        two = r.dgv_y[0, a, at_x].astype(F32)
        for k in range(3):
            one = one + r.dgu_y[k, a].astype(F32)
            two = two + r.dgv_x[k, a].astype(F32)
        r.gu_src[a, :, :, left] = one.reshape(2, 8, SLICE)
        r.gu_src[a, :, :, right] = two.reshape(2, 8, SLICE)
    dgu_near = paired(r.gu_src, r.gu_pair)

    wait_left(1 - xh)
    r.p_x_src[...] = sum_left(1 - xh).astype(BF)
    p_x = net.put(r.p_x_src, r.p_x, moved(me, X_HALF))
    for b in range(4):
        net.copy(r.p_x_src, r.p_x, over, r_sems + b, r_sems + b).wait_recv()
    for o in Y_PEERS:
        b = moved(me, o)[3]
        r.cot_all[b, 0, :, last] = sum_right(b).astype(BF)
    r_y = scattered(
        Y_PEERS, lambda to: r.cot_all.at[to[3], 0, :, last], r.cot_all.at[pl.ds(0, 3), 1, :, last]
    )

    dw_z.wait_recv()
    total = r.dw_low[:, columns(z, 2 * TOK)].astype(F32)
    for k in range(3):
        total = total + r.dw_got[k].astype(F32)
    r.dw_mid[0] = total[:, :TOK].astype(BF)
    r.dw_mid[1] = total[:, TOK:].astype(BF)
    dw_xl = net.put(r.dw_mid.at[1 - xl], r.dw_xl, moved(me, X_LOW))

    dgu_z = dealt(dgu_near, r.gu_pair, r.gu_tmp, Z_PEERS, lambda at: at[0])
    dwo_one.wait_recv()
    for b in range(4):
        at = (b // 2, b % 2)
        total = r.dwo_z[(0, *at, y)].astype(F32)
        for k in range(3):
            total = total + r.dwo_y[(k, *at)].astype(F32)
        r.dwo_y[(0, *at)] = total.astype(BF)
    dwo_one = scattered(X_PEERS, lambda to: r.dwo_y.at[0, to[1], to[2]], r.dwo_x)
    dwo_two.wait_recv()
    for b in range(4):
        at = (b // 2, b % 2)
        total = r.dwp_y[(0, z, *at)].astype(F32)
        for k in range(3):
            total = total + r.dwp_z[(k, *at)].astype(F32)
        r.dwp_z[(0, *at)] = total.astype(BF)
    dwo_two = scattered(X_PEERS, lambda to: r.dwp_z.at[0, to[1], to[2]], r.dwp_x)

    dw_xl.wait_recv()
    total = r.dw_mid[xl].astype(F32) + r.dw_xl[...].astype(F32)
    r.wq_src[...] = total.T.reshape(8, 2, 8, 2 * HEAD)
    dw_near = paired(r.wq_src, r.wq_pair)
    dw_ctx = dealt(dw_near, r.wq_pair, r.wq_tmp, CTX, chip_of)

    hg_ctx.wait_recv()
    total = r.hg_two[...]
    for k in range(7):
        total = total + r.hg_got[k]
    r.hg_mid[...] = total
    hg_dp = scattered(DP_ALL, lambda to: r.hg_mid, r.hg_dp)

    def half_copy():
        return net.copy(r.dwd_sum.at[1 - c], r.dwd_half, over, dwdy_sems + 3, dwdy_sems + 3)

    @pl.when(xl == c)
    def _():
        for k in range(3):
            dwdy_copy(k).wait_recv()
        total = r.dwd_x[0, y].astype(F32)
        for k in range(3):
            total = total + r.dwd_y[k].astype(F32)
        r.dwd_sum[0] = total[:24]
        r.dwd_sum[1] = total[24:]
        half_copy().start()
        r.dwd_out[...] = r.dwd_sum[c]

    po_ring.wait_recv()
    total = r.resid[...] + r.po_got[z].astype(F32)
    for k in range(3):
        total = total + r.po_ring[k].astype(F32)
    r.resid[...] = total
    outs = [net.local(r.resid, r.output)]

    wait_left(xh)
    p_x.wait_recv()
    total = sum_left(xh) + r.p_x[...].astype(F32)
    r_y.wait_recv()
    other = sum_right(y)
    for k in range(3):
        other = other + r.cot_all[k, 1, :, last].astype(F32)
    total = jnp.concatenate([total, other], 1)
    inputs = r.tok[...].astype(F32)
    r.grad_resid[...] += norm_back(
        inputs, inverse_root(inputs), total * r.gain_one[...]
    )
    outs.append(net.local(r.grad_resid, r.input_grad))

    dwo_one.wait_recv()
    total = r.dwo_y[0, xl, xh].astype(F32)
    for k in range(3):
        total = total + r.dwo_x[k].astype(F32)
    r.dwo_out[:, more] = total
    dwo_two.wait_recv()
    total = r.dwp_z[0, xl, xh].astype(F32)
    for k in range(3):
        total = total + r.dwp_x[k].astype(F32)
    r.dwo_out[:, less] = total
    outs.append(net.local(r.dwo_out, r.grad_out))

    @pl.when(xl != c)
    def _():
        half_copy().wait_recv()
        r.dwd_out[...] = r.dwd_half[...]

    outs.append(net.local(r.dwd_out, r.grad_down))
    dgu_z.wait_recv()
    for j in range(8):
        r.dgu_out[:, j * SLICE : (j + 1) * SLICE] = r.gu_tmp[j // 2, j % 2, :, :SLICE]
        r.dgu_out[:, FF + j * SLICE : FF + (j + 1) * SLICE] = r.gu_tmp[j // 2, j % 2, :, SLICE:]
    outs.append(net.local(r.dgu_out, r.grad_up))
    lane = lax.broadcasted_iota(jnp.int32, (8, 128), 1)
    row = lax.broadcasted_iota(jnp.int32, (8, 128), 0)

    def picked(values, at):
        return jnp.sum(jnp.where(lane == at, values, 0.0), 1, keepdims=True)

    two = jnp.sum(r.dgu_out[...] * r.wgu[...].astype(F32), 1, keepdims=True)
    two = two / picked(r.gains[...], row + 8)
    dw_ctx.wait_recv()
    for j in range(16):
        extra = (KEY_AT, VALUE_AT)[j % 2] + j // 2 * HEAD
        r.dwq_out[:, j * HEAD : (j + 1) * HEAD] = r.wq_tmp[j // 2, j % 2, :, :HEAD]
        r.dwq_out[:, extra : extra + HEAD] = r.wq_tmp[j // 2, j % 2, :, HEAD:]
    outs.append(net.local(r.dwq_out, r.grad_qkv))
    one = jnp.sum(r.dwq_out[...] * r.wqkv[...].astype(F32), 1, keepdims=True)
    one = one / picked(r.gains[...], row)
    hg_dp.wait_recv()
    total = r.hg_mid[...]
    for k in range(7):
        total = total + r.hg_dp[k]
    heads = picked(total, here * 16 + mine)
    r.gains_out[...] = jnp.where(lane == 0, one, jnp.where(lane == 1, two, heads))
    outs.append(net.local(r.gains_out, r.gain_grads))

    for m in range(8):

        @pl.when(y != m % 4)
        def _():
            p_copy(m).wait_send()

        @pl.when(xh != m // 4)
        def _():
            r_copy(m).wait_send()

    @pl.when(xl == c)
    def _():
        for k, o in enumerate(Y_PEERS):
            at = r.wd_all.at[xh, y]
            net.copy(at, at, over, wd_sems + k, wd_sems + k).wait_send()
        for k, o in enumerate(X_PEERS):
            at = r.wd_all.at[xh]
            net.copy(at, at, over, wdx_sems + k, wdx_sems + k).wait_send()
        dwd_copy(half_at).wait_send()
        for k in range(3):
            dwdy_copy(k).wait_send()
        half_copy().wait_send()

    @pl.when(xl != c)
    def _():
        for k in range(3):
            if k != half_at:
                dwd_copy(k).wait_send()

    net.drain()
    for copy in outs:
        copy.wait()


def finish(*refs):
    ins, gains, outs = refs[:6], refs[6], refs[7:13]
    (attn, q, k, mlp), held, sems = refs[13:17], refs[17:23], refs[23]
    for i in range(6):
        pltpu.make_async_copy(ins[i], held[i], sems.at[i]).start()
    for i in range(8):
        attn[i] = gains[i, 0]
        mlp[i] = gains[i, 1]
    q[0] = gains[0, 2]
    k[0] = gains[1, 2]
    for i in range(6):
        pltpu.make_async_copy(ins[i], held[i], sems.at[i]).wait()
        pltpu.make_async_copy(held[i], outs[i], sems.at[i]).start()
    for i in range(6):
        pltpu.make_async_copy(held[i], outs[i], sems.at[i]).wait()


def on_device(
    tokens, lengths, attn_gain, q_gain, k_gain, qkv, w_out, mlp_gain, w_gate_up, w_down, cotangent
):
    gains = jnp.concatenate([attn_gain, mlp_gain, q_gain, k_gain]).astype(F32)
    gains = jnp.broadcast_to(jnp.pad(gains, (0, 128 - 18))[None], (8, 128))
    half = np.arange(HEAD // 2, dtype=np.float32) * np.float32(2.0 / HEAD)
    freq = np.float32(THETA) ** (-half)
    freq = jnp.asarray(np.concatenate([freq, freq])[None].astype(np.float32))
    hbm, smem = pl.BlockSpec(memory_space=pl.ANY), pl.BlockSpec(memory_space=pltpu.SMEM)
    outs = pl.pallas_call(
        body,
        name="layer",
        out_shape=tuple(jax.ShapeDtypeStruct(s, d) for s, d in OUTPUTS.values()),
        in_specs=[hbm] * 8 + [smem],
        out_specs=(hbm,) * len(OUTPUTS),
        scratch_shapes=[pltpu.VMEM(s, d) for s, d in BUFFERS.values()]
        + [pltpu.SemaphoreType.DMA((n,)) for n in SEMS],
        compiler_params=pltpu.CompilerParams(
            collective_id=1, has_side_effects=True, vmem_limit_bytes=VMEM_LIMIT
        ),
    )(tokens, qkv, w_out, w_gate_up, w_down, cotangent, gains, freq, lengths)
    o = dict(zip(OUTPUTS, outs))
    wide = [o[n] for n in ("output", "input_grad", "grad_qkv", "grad_out", "grad_up", "grad_down")]
    small = [jax.ShapeDtypeStruct((n,), F32) for n in (8, 1, 1, 8)]
    done = pl.pallas_call(
        finish,
        name="finish",
        out_shape=tuple(jax.ShapeDtypeStruct(a.shape, F32) for a in wide) + tuple(small),
        in_specs=[hbm] * 6 + [smem],
        out_specs=(hbm,) * 6 + (smem,) * 4,
        scratch_shapes=[pltpu.VMEM(a.shape, F32) for a in wide] + [pltpu.SemaphoreType.DMA((6,))],
    )(*wide, o["gain_grads"])
    output, input_grad, grad_qkv, grad_out, grad_up, grad_down, attn, q, k, mlp = done
    return output, input_grad, attn, q, k, grad_qkv, grad_out, mlp, grad_up, grad_down


def solution(mesh):
    torus = Mesh(mesh.devices.reshape(SIZES), AXES)
    rows, line = P(AXES, None), P(AXES)
    return jax.shard_map(
        on_device,
        mesh=torus,
        in_specs=(rows, P(DP, None), line, line, line, rows, rows, line, rows, rows, rows),
        out_specs=(rows, rows, line, line, line, rows, rows, line, rows, rows),
        check_vma=False,
    )
```
